32 devices in a mesh: ctx: 16 (over z, x, core), head: 2 (over y).
Axes of the slice: x: 2, y: 2, z: 4, core: 2. Of those that a mesh axis runs over, the one named last changes fastest.
Arguments:
- queries: bfloat16 [2048, 36864], P('ctx', 'head'), may hold values from -6 to 6
- latents: bfloat16 [4096, 576], P('ctx'), may hold values from -5 to 5
- up_value: bfloat16 [512, 8192], P(None, 'head'), may hold values from -0.25 to 0.25
- grad_out: bfloat16 [2048, 8192], P('ctx', 'head'), may hold values from -12 to 12
- out_saved: bfloat16 [2048, 8192], P('ctx', 'head'), may hold values from -6 to 6
- log_sums: float32 [2048, 64], P('ctx', 'head'), as said below
- doc_starts: int32 [65], replicated, may hold values from 0 to 4096, as said below
Outputs:
- grad_queries: bfloat16 [2048, 36864], P('ctx', 'head')
- grad_latents: float32 [4096, 576], P(('ctx', 'head'))
- grad_up_value: float32 [512, 8192], P('ctx', 'head')
The draws below stay inside these ranges and needn't reach their ends.
Inputs may be any that keep to these rules, and one draw needn't show every extreme that they name: doc_starts[0] is 0; the entries rise strictly until they reach 4096 and then stay at 4096; consecutive entries differ by at most 512, and some document has exactly 512 positions. log_sums[t, h] is the log of the sum of exp(score[t, h, s]) over the keys s allowed for query t, computed from these queries and latents.
All inputs are finite; a program needn't handle non-finite values.
Results may differ from the reference program's by a relative error of at most 0.0085.
Values may be sent and summed in bfloat16 or wider, within the bound.
No kernel may reach another device: no remote copies, remote signals or barrier semaphores. Data moves between devices by JAX's collectives and lax.ppermute only.
A program may use at most 128 MiB of HBM per device.

```python
import jax
import jax.numpy as jnp
from jax import lax

LAT = 512
ROPE = 64
FEAT = 576
VDIM = 128
HEADS = 64
Q_DEV = 128
KEY_DEV = 256
SPAN = 2
DOC_MAX = 512
KEYS = 4096
QUERIES = 2048
DOCS = 65


softmax_scale = 192.0 ** (-0.5)


def doc_index_drawn(positions, doc_starts):
    return jnp.sum((doc_starts[None, :] <= positions[:, None]).astype(jnp.int32), axis=1) - 1


def draw_world(key):
    key = jax.random.fold_in(key, 7)
    key_gap, key_pick, key_lat, key_query, key_lscale, key_qscale = jax.random.split(key, 6)
    gaps = jax.random.randint(key_gap, (DOCS - 1,), DOC_MAX // 8, DOC_MAX + 1)
    pick = jax.random.randint(key_pick, (), 0, 2)
    gaps = jnp.where(jnp.arange(DOCS - 1) == pick, DOC_MAX, gaps)
    starts = jnp.concatenate([jnp.zeros((1,), jnp.int32), jnp.cumsum(gaps).astype(jnp.int32)])
    starts = jnp.minimum(starts, KEYS).astype(jnp.int32)
    latents = jnp.clip(jax.random.normal(key_lat, (KEYS, FEAT), jnp.float32), -5.0, 5.0)
    queries = jnp.clip(jax.random.normal(key_query, (QUERIES, HEADS, FEAT), jnp.float32), -5.0, 5.0)
    latents = latents.astype(jnp.bfloat16)
    queries = queries.astype(jnp.bfloat16)
    padded = jnp.concatenate([jnp.zeros((SPAN * KEY_DEV, FEAT), jnp.bfloat16), latents], axis=0)
    window = (SPAN + 1) * KEY_DEV

    def one_block(block_id):
        query_block = lax.dynamic_slice_in_dim(queries, block_id * Q_DEV, Q_DEV, 0).astype(jnp.float32)
        key_block = lax.dynamic_slice_in_dim(padded, block_id * KEY_DEV, window, 0).astype(jnp.float32)
        query_pos = (block_id * KEY_DEV + KEY_DEV - Q_DEV + jnp.arange(Q_DEV)).astype(jnp.int32)
        key_pos = (block_id * KEY_DEV - SPAN * KEY_DEV + jnp.arange(window)).astype(jnp.int32)
        allowed = (doc_index_drawn(query_pos, starts)[:, None] == doc_index_drawn(key_pos, starts)[None, :]) & (key_pos[None, :] <= query_pos[:, None])
        scores = jnp.einsum('thf,sf->ths', query_block, key_block) * softmax_scale
        scores = jnp.where(allowed[:, None, :], scores, -jnp.inf)
        top = jnp.max(scores, axis=2, keepdims=True)
        return top[:, :, 0] + jnp.log(jnp.sum(jnp.exp(scores - top), axis=2))
    sums = lax.map(one_block, jnp.arange(KEYS // KEY_DEV).astype(jnp.int32)).reshape(QUERIES, HEADS)
    return (starts, latents, queries.reshape(QUERIES, HEADS * FEAT), sums)


def draw_doc_starts(key, part):
    return draw_world(key)[0]


def draw_latents(key, part):
    return draw_world(key)[1]


def draw_queries(key, part):
    return draw_world(key)[2]


def draw_log_sums(key, part):
    return draw_world(key)[3].astype(jnp.float32)


def shard_levels(key, dims, shards, smallest, high):
    loudness, own = 1.0, jax.random.fold_in(key, 6)
    for position, shards_of in shards:
        steps = jnp.exp(jax.random.uniform(jax.random.fold_in(own, position), (shards_of,), jnp.float32, smallest / len(shards), high / len(shards)))
        loudness = loudness * jnp.repeat(steps, dims[position] // shards_of).reshape([-1 if axis == position else 1 for axis in range(len(dims))])
    return loudness


def bell_draw(own_key, shape, spread, bound, cuts=(), kind=jnp.bfloat16):
    entries = spread * jax.random.normal(own_key, shape, jnp.float32)
    if cuts:
        entries = entries * shard_levels(own_key, shape, cuts, -0.22, 0.18)
    return jnp.clip(entries, -bound, bound).astype(kind)


def setup_inputs(seed: int = 0) -> dict:
    streams_of = jax.random.split(jax.random.key(seed), 8)
    queries = draw_queries(jax.random.fold_in(streams_of[7], 71), 0)
    latents = draw_latents(jax.random.fold_in(streams_of[7], 71), 0)
    up_value = bell_draw(streams_of[2], (LAT, HEADS * VDIM), LAT ** -0.5, 0.25, ((1, 2),))
    grad_out = bell_draw(streams_of[3], (QUERIES, HEADS * VDIM), 2.0, 12.0, ((0, 16), (1, 2)))
    out_saved = bell_draw(streams_of[4], (QUERIES, HEADS * VDIM), 1.0, 6.0, ((0, 16), (1, 2)))
    log_sums = draw_log_sums(jax.random.fold_in(streams_of[7], 71), 0)
    doc_starts = draw_doc_starts(jax.random.fold_in(streams_of[7], 71), 0)
    return {"queries": queries, "latents": latents, "up_value": up_value, "grad_out": grad_out, "out_saved": out_saved, "log_sums": log_sums, "doc_starts": doc_starts}


softmax_scale = 192.0 ** -0.5


def doc_index(positions, doc_starts):
    return jnp.sum((doc_starts[None, :] <= positions[:, None]).astype(jnp.int32), axis=1) - 1


def reference(queries, latents, up_value, grad_out, out_saved, log_sums, doc_starts):
    query_heads = queries.reshape(QUERIES, HEADS, FEAT)
    grad_heads = grad_out.reshape(QUERIES, HEADS, VDIM)
    saved_heads = out_saved.reshape(QUERIES, HEADS, VDIM)
    weight_heads = up_value.reshape(LAT, HEADS, VDIM).astype(jnp.float32)
    padded = jnp.concatenate([jnp.zeros((SPAN * KEY_DEV, FEAT), latents.dtype), latents], axis=0)
    window = (SPAN + 1) * KEY_DEV
    block_count = KEYS // KEY_DEV

    def step(carry, block_id):
        grad_lat_pad, grad_weight = carry
        query_block = lax.dynamic_slice_in_dim(query_heads, block_id * Q_DEV, Q_DEV, 0).astype(jnp.float32)
        grad_block = lax.dynamic_slice_in_dim(grad_heads, block_id * Q_DEV, Q_DEV, 0).astype(jnp.float32)
        saved_block = lax.dynamic_slice_in_dim(saved_heads, block_id * Q_DEV, Q_DEV, 0).astype(jnp.float32)
        sums_block = lax.dynamic_slice_in_dim(log_sums, block_id * Q_DEV, Q_DEV, 0)
        key_block = lax.dynamic_slice_in_dim(padded, block_id * KEY_DEV, window, 0).astype(jnp.float32)
        query_pos = (block_id * KEY_DEV + KEY_DEV - Q_DEV + jnp.arange(Q_DEV)).astype(jnp.int32)
        key_pos = (block_id * KEY_DEV - SPAN * KEY_DEV + jnp.arange(window)).astype(jnp.int32)
        allowed = (doc_index(query_pos, doc_starts)[:, None] == doc_index(key_pos, doc_starts)[None, :]) & (key_pos[None, :] <= query_pos[:, None])
        grad_lat_q = jnp.einsum("thv,jhv->thj", grad_block, weight_heads).astype(jnp.bfloat16).astype(jnp.float32)
        row_delta = jnp.sum(grad_block * saved_block, axis=2)
        scores = jnp.einsum("thf,sf->ths", query_block, key_block) * softmax_scale
        prob_full = jnp.where(allowed[:, None, :], jnp.exp(scores - sums_block[:, :, None]), 0.0)
        prob_half = prob_full.astype(jnp.bfloat16).astype(jnp.float32)
        values = key_block[:, :LAT]
        out_lat = jnp.einsum("ths,sj->thj", prob_half, values).astype(jnp.bfloat16).astype(jnp.float32)
        grad_prob = jnp.einsum("thj,sj->ths", grad_lat_q, values)
        grad_score = (prob_full * (grad_prob - row_delta[:, :, None]) * softmax_scale).astype(jnp.bfloat16).astype(jnp.float32)
        grad_query = jnp.einsum("ths,sf->thf", grad_score, key_block).astype(jnp.bfloat16)
        grad_key = jnp.einsum("ths,thf->sf", grad_score, query_block)
        grad_value = jnp.einsum("ths,thj->sj", prob_half, grad_lat_q)
        grad_key = grad_key + jnp.pad(grad_value, ((0, 0), (0, ROPE)))
        start = (block_id * KEY_DEV).astype(jnp.int32)
        current = lax.dynamic_slice_in_dim(grad_lat_pad, start, window, 0)
        grad_lat_pad = lax.dynamic_update_slice_in_dim(grad_lat_pad, current + grad_key, start, 0)
        grad_weight = grad_weight + jnp.einsum("thj,thv->jhv", out_lat, grad_block)
        return (grad_lat_pad, grad_weight), grad_query.reshape(Q_DEV, HEADS * FEAT)

    start_carry = (jnp.zeros((SPAN * KEY_DEV + KEYS, FEAT), jnp.float32), jnp.zeros((LAT, HEADS, VDIM), jnp.float32))
    (grad_lat_pad, grad_weight), grad_blocks = lax.scan(step, start_carry, jnp.arange(block_count).astype(jnp.int32))
    grad_queries = grad_blocks.reshape(QUERIES, HEADS * FEAT)
    grad_latents = grad_lat_pad[SPAN * KEY_DEV:]
    return grad_queries, grad_latents, grad_weight.reshape(LAT, HEADS * VDIM)
```

```python
import functools
import math

import jax
import jax.numpy as jnp
from jax import lax
from jax.experimental import pallas as pl
from jax.experimental.pallas import tpu as pltpu
from jax.sharding import PartitionSpec as P

softmax_scale = 192.0 ** (-0.5)
log2e = math.log2(math.e)
vmem_bytes = 56 * 1024 * 1024


def nt_dot(a, b):
    return lax.dot_general(a, b, (((1,), (1,)), ((), ())), preferred_element_type=jnp.float32)


def nn_dot(a, b):
    return lax.dot_general(a, b, (((1,), (0,)), ((), ())), preferred_element_type=jnp.float32)


def tn_dot(a, b):
    return lax.dot_general(a, b, (((0,), (0,)), ((), ())), preferred_element_type=jnp.float32)


def head_order(group):
    return list(range(0, group, 2)) + list(range(1, group, 2))


def wide_slices(q_ref, group, feat, width, parity):
    shift = (feat + (width - feat) - width) if parity == 0 else 2 * feat - width
    return jnp.concatenate(
        [q_ref[:, 2 * feat * k + shift : 2 * feat * k + shift + width] for k in range(group // 2)],
        axis=0,
    )


def column(block, index):
    lane = lax.broadcasted_iota(jnp.int32, block.shape, 1)
    return jnp.sum(jnp.where(lane == index, block, 0.0), axis=1, keepdims=True)


def glat_kernel(g_ref, w_ref, out_ref, *, group, rows, vdim):
    for slot, head in enumerate(head_order(group)):
        lanes = slice(head * vdim, (head + 1) * vdim)
        out_ref[slot * rows : (slot + 1) * rows, :] = nt_dot(g_ref[:, lanes], w_ref[:, lanes]).astype(
            out_ref.dtype
        )


def forward_kernel(
    core_ref, q_ref, c_ref, g_ref, lse_ref, bias_ref, *rest,
    group, rows, feat, lat, vdim, far, base, own_rows, aliased,
):
    far_ref, near_ref, keep_ref, send_ref = rest[2:] if aliased else rest
    width = c_ref.shape[2]
    step = pl.program_id(0) + base
    half = group // 2
    lse = lse_ref[...] * log2e
    bias = bias_ref[...]
    order = head_order(group)
    core = core_ref[0]
    for parity in range(2):
        scores = nt_dot(wide_slices(q_ref, group, feat, width, parity), c_ref[parity])
        for k in range(half):
            slot = parity * half + k
            shift = column(lse, step * group + order[slot])
            prob = jnp.exp2(
                scores[k * rows : (k + 1) * rows] * (softmax_scale * log2e) + (bias - shift)
            ).astype(jnp.bfloat16)
            span = slice(slot * rows, (slot + 1) * rows)
            far_ref[span, :] = prob[:, :far]
            near_ref[span, :] = prob[:, far:]
    for parity in range(2):
        span = slice(parity * half * rows, (parity + 1) * half * rows)
        olat = (
            nn_dot(far_ref[span, :], c_ref[0, :far, :lat])
            + nn_dot(near_ref[span, :], c_ref[0, far:, :lat])
        ).astype(jnp.bfloat16)
        for k in range(half):
            head = order[parity * half + k]
            lanes = slice(head * vdim, (head + 1) * vdim)
            part = tn_dot(olat[k * rows : (k + 1) * rows], g_ref[:, lanes])
            part = part.reshape(lat // (2 * own_rows), 2, own_rows, vdim)
            low, high = part[:, 0], part[:, 1]
            keep_ref[:, lanes] = (
                jnp.where(core == 0, low, high).reshape(lat // 2, vdim).astype(keep_ref.dtype)
            )
            send_ref[:, lanes] = (
                jnp.where(core == 0, high, low).reshape(lat // 2, vdim).astype(send_ref.dtype)
            )


def delta_of(g_ref, o_ref, lanes):
    return jnp.sum(
        g_ref[:, lanes].astype(jnp.float32) * o_ref[:, lanes].astype(jnp.float32), axis=1, keepdims=True
    )


def backward_far_kernel(
    q_ref, c_ref, g_ref, o_ref, glat_ref, p_ref, ds_ref, far2_ref, far1_ref, even_acc, odd_acc,
    *, group, rows, feat, lat, vdim, steps,
):
    width = c_ref.shape[2]
    far = p_ref.shape[1]
    half = group // 2
    order = head_order(group)

    @pl.when(pl.program_id(0) == 0)
    def _():
        even_acc[...] = jnp.zeros_like(even_acc)
        odd_acc[...] = jnp.zeros_like(odd_acc)

    for parity in range(2):
        span = slice(parity * half * rows, (parity + 1) * half * rows)
        gprob = nt_dot(glat_ref[span, :], c_ref[0, :far, :lat])
        for k in range(half):
            slot = parity * half + k
            head = order[slot]
            delta = delta_of(g_ref, o_ref, slice(head * vdim, (head + 1) * vdim))
            own = slice(slot * rows, (slot + 1) * rows)
            ds_ref[own, :] = (
                p_ref[own, :].astype(jnp.float32)
                * ((gprob[k * rows : (k + 1) * rows] - delta) * softmax_scale)
            ).astype(ds_ref.dtype)
        acc = even_acc if parity == 0 else odd_acc
        acc[...] += tn_dot(ds_ref[span, :], wide_slices(q_ref, group, feat, width, parity))
        even_acc[:, :lat] += tn_dot(p_ref[span, :], glat_ref[span, :])

    @pl.when(pl.program_id(0) == steps - 1)
    def _():
        total = even_acc[...] + pltpu.roll(odd_acc[...], feat, 1)
        total = total[:, :feat].astype(far2_ref.dtype)
        far2_ref[...] = total[: far2_ref.shape[0]]
        far1_ref[...] = total[far2_ref.shape[0] :]


def backward_near_kernel(
    q_ref, c_ref, g_ref, o_ref, glat_ref, p_ref, dsf_ref, gq_ref, near_ref, ds_ref, even_acc, odd_acc,
    *, group, rows, feat, lat, vdim, steps,
):
    width = c_ref.shape[2]
    far = dsf_ref.shape[1]
    half = group // 2
    order = head_order(group)

    @pl.when(pl.program_id(0) == 0)
    def _():
        even_acc[...] = jnp.zeros_like(even_acc)
        odd_acc[...] = jnp.zeros_like(odd_acc)

    parts = []
    for parity in range(2):
        span = slice(parity * half * rows, (parity + 1) * half * rows)
        gprob = nt_dot(glat_ref[span, :], c_ref[0, far:, :lat])
        for k in range(half):
            slot = parity * half + k
            head = order[slot]
            delta = delta_of(g_ref, o_ref, slice(head * vdim, (head + 1) * vdim))
            own = slice(slot * rows, (slot + 1) * rows)
            ds_ref[own, :] = (
                p_ref[own, :].astype(jnp.float32)
                * ((gprob[k * rows : (k + 1) * rows] - delta) * softmax_scale)
            ).astype(ds_ref.dtype)
        acc = even_acc if parity == 0 else odd_acc
        acc[...] += tn_dot(ds_ref[span, :], wide_slices(q_ref, group, feat, width, parity))
        even_acc[:, :lat] += tn_dot(p_ref[span, :], glat_ref[span, :])
        parts.append(
            nn_dot(dsf_ref[span, :], c_ref[parity, :far, :]) + nn_dot(ds_ref[span, :], c_ref[parity, far:, :])
        )
    both = 2 * width - 2 * feat
    for k in range(half):
        span = slice(k * rows, (k + 1) * rows)
        even, odd = parts[0][span], parts[1][span]
        start = 2 * feat * k
        gq_ref[:, start : start + width - both] = even[:, : width - both].astype(gq_ref.dtype)
        gq_ref[:, start + width - both : start + width] = (even[:, width - both :] + odd[:, :both]).astype(
            gq_ref.dtype
        )
        gq_ref[:, start + width : start + 2 * feat] = odd[:, both:].astype(gq_ref.dtype)

    @pl.when(pl.program_id(0) == steps - 1)
    def _():
        total = even_acc[...] + pltpu.roll(odd_acc[...], feat, 1)
        near_ref[...] = total[:, :feat]


def passed_along(value, axis, steps):
    count = lax.axis_size(axis)
    first, last = (max(0, -steps), min(count, count - steps))
    return lax.ppermute(value, axis, [(source, source + steps) for source in range(first, last)])


def swapped(value, axis, bit):
    count = lax.axis_size(axis)
    return lax.ppermute(value, axis, [(source, source ^ bit) for source in range(count)])


def params():
    return pltpu.CompilerParams(
        dimension_semantics=("arbitrary",), vmem_limit_bytes=vmem_bytes
    )


def cost(flops, moved):
    return pl.CostEstimate(flops=int(flops), bytes_accessed=int(moved), transcendentals=0)


def halve_rest(keep, recv, index, count, own_rows, axis, bit=2):
    cols = keep.shape[1]
    total = keep.astype(jnp.float32) + recv.astype(jnp.float32)
    while bit < count:
        blocks = count // bit // 2
        view = total.reshape(blocks, 2, own_rows, cols)
        mine = (index // bit) % 2
        send = lax.dynamic_index_in_dim(view, 1 - mine, 1, keepdims=False)
        hold = lax.dynamic_index_in_dim(view, mine, 1, keepdims=False)
        got = swapped(send.astype(jnp.bfloat16).reshape(blocks * own_rows, cols), axis, bit)
        total = hold.reshape(blocks * own_rows, cols) + got.astype(jnp.float32)
        bit *= 2
    return total


def on_device(queries, latents, up_value, grad_out, out_saved, log_sums, doc_starts):
    rows = queries.shape[0]
    key_rows, feat = latents.shape
    lat = up_value.shape[0]
    heads = log_sums.shape[1]
    vdim = grad_out.shape[1] // heads
    ctx = lax.axis_size("ctx")
    head_count = lax.axis_size("head")
    own_rows = lat // ctx
    chunks = 2
    group = min(8, heads // chunks)
    steps = heads // group
    chunk_steps = steps // chunks
    window = 2 * key_rows + rows
    far = window - key_rows
    width = -(-feat // 128) * 128

    device = lax.axis_index("ctx")
    prev1 = passed_along(latents, "ctx", 1)
    prev2 = passed_along(latents[key_rows - (far - key_rows) :], "ctx", 2)

    group_rows = group * rows
    lane_group = group * vdim
    glat = pl.pallas_call(
        functools.partial(glat_kernel, group=group, rows=rows, vdim=vdim),
        grid=(steps,),
        in_specs=[
            pl.BlockSpec((rows, lane_group), lambda i: (0, i)),
            pl.BlockSpec((lat, lane_group), lambda i: (0, i)),
        ],
        out_specs=pl.BlockSpec((group_rows, lat), lambda i: (i, 0)),
        out_shape=jax.ShapeDtypeStruct((heads * rows, lat), jnp.bfloat16),
        compiler_params=params(),
        cost_estimate=cost(4 * heads * rows * lat * vdim, 10e6),
        name="glat",
    )(grad_out, up_value)

    start = device * key_rows - far
    query_pos = device * key_rows + key_rows - rows + jnp.arange(rows, dtype=jnp.int32)
    first = jnp.max(jnp.where(doc_starts[None, :] <= query_pos[:, None], doc_starts[None, :], 0), axis=1)
    key_pos = start + jnp.arange(window, dtype=jnp.int32)
    allowed = (key_pos[None, :] >= first[:, None]) & (key_pos[None, :] <= query_pos[:, None])
    bias = jnp.where(allowed, 0.0, -1e30).astype(jnp.float32)

    keys = jnp.concatenate([prev2, prev1, latents], axis=0)
    keys = jnp.stack(
        [jnp.pad(keys, ((0, 0), (0, width - feat))), jnp.pad(keys, ((0, 0), (width - feat, 0)))]
    )
    core = (device % 2).astype(jnp.int32).reshape(1)

    whole = lambda shape: pl.BlockSpec(shape, lambda i: (0,) * len(shape))
    probs = None
    partials = []
    chunk_cols = heads // chunks * vdim
    for chunk in range(chunks):
        base = chunk * chunk_steps
        lanes = lambda i, base=base: (0, i + base)
        rowed = lambda i, base=base: (i + base, 0)
        in_specs = [
            pl.BlockSpec(memory_space=pltpu.SMEM),
            pl.BlockSpec((rows, group * feat), lanes),
            whole((2, window, width)),
            pl.BlockSpec((rows, lane_group), lanes),
            whole((rows, heads)),
            whole((rows, window)),
        ]
        operands = [core, queries, keys, grad_out, log_sums, bias]
        aliases = {}
        if probs is not None:
            in_specs += [pl.BlockSpec(memory_space=pl.ANY)] * 2
            operands += list(probs)
            aliases = {6: 0, 7: 1}
        *probs, keep, send = pl.pallas_call(
            functools.partial(
                forward_kernel, group=group, rows=rows, feat=feat, lat=lat, vdim=vdim, far=far,
                base=base, own_rows=own_rows, aliased=bool(aliases),
            ),
            grid=(chunk_steps,),
            in_specs=in_specs,
            out_specs=[
                pl.BlockSpec((group_rows, far), rowed),
                pl.BlockSpec((group_rows, key_rows), rowed),
                pl.BlockSpec((lat // 2, lane_group), lambda i: (0, i)),
                pl.BlockSpec((lat // 2, lane_group), lambda i: (0, i)),
            ],
            out_shape=[
                jax.ShapeDtypeStruct((heads * rows, far), jnp.bfloat16),
                jax.ShapeDtypeStruct((heads * rows, key_rows), jnp.bfloat16),
                jax.ShapeDtypeStruct((lat // 2, chunk_cols), jnp.bfloat16),
                jax.ShapeDtypeStruct((lat // 2, chunk_cols), jnp.bfloat16),
            ],
            input_output_aliases=aliases,
            compiler_params=params(),
            cost_estimate=cost(heads // chunks * rows * 2 * window * (width + lat) * 1.5, 8e6),
            name="forward",
        )(*operands)
        partials.append((keep, send))

    received = [swapped(send, "ctx", 1) for _, send in partials]

    lanes = lambda i: (0, i)
    rowed = lambda i: (i, 0)
    common_specs = [
        pl.BlockSpec((rows, group * feat), lanes),
        whole((2, window, width)),
        pl.BlockSpec((rows, lane_group), lanes),
        pl.BlockSpec((rows, lane_group), lanes),
        pl.BlockSpec((group_rows, lat), rowed),
    ]
    statics = dict(group=group, rows=rows, feat=feat, lat=lat, vdim=vdim, steps=steps)
    ds_far, far2, far1 = pl.pallas_call(
        functools.partial(backward_far_kernel, **statics),
        grid=(steps,),
        in_specs=common_specs + [pl.BlockSpec((group_rows, far), rowed)],
        out_specs=[
            pl.BlockSpec((group_rows, far), rowed),
            whole((far - key_rows, feat)),
            whole((key_rows, feat)),
        ],
        out_shape=[
            jax.ShapeDtypeStruct((heads * rows, far), jnp.bfloat16),
            jax.ShapeDtypeStruct((far - key_rows, feat), jnp.bfloat16),
            jax.ShapeDtypeStruct((key_rows, feat), jnp.bfloat16),
        ],
        scratch_shapes=[pltpu.VMEM((far, width), jnp.float32)] * 2,
        compiler_params=params(),
        cost_estimate=cost(heads * rows * 2 * far * (width + 2 * lat) * 1.5, 16e6),
        name="backward_far",
    )(queries, keys, grad_out, out_saved, glat, probs[0])
    got2 = passed_along(far2, "ctx", -2)
    got1 = passed_along(far1, "ctx", -1)

    grad_queries, near = pl.pallas_call(
        functools.partial(backward_near_kernel, **statics),
        grid=(steps,),
        in_specs=common_specs
        + [pl.BlockSpec((group_rows, key_rows), rowed), pl.BlockSpec((group_rows, far), rowed)],
        out_specs=[pl.BlockSpec((rows, group * feat), lanes), whole((key_rows, feat))],
        out_shape=[
            jax.ShapeDtypeStruct(queries.shape, jnp.bfloat16),
            jax.ShapeDtypeStruct((key_rows, feat), jnp.float32),
        ],
        scratch_shapes=[
            pltpu.VMEM((group_rows, key_rows), jnp.bfloat16),
            pltpu.VMEM((key_rows, width), jnp.float32),
            pltpu.VMEM((key_rows, width), jnp.float32),
        ],
        compiler_params=params(),
        cost_estimate=cost(heads * rows * 2 * (key_rows * (width + 2 * lat) + window * width) * 1.5, 20e6),
        name="backward_near",
    )(queries, keys, grad_out, out_saved, glat, probs[1], ds_far)

    shifted = got1.astype(jnp.float32) + jnp.pad(
        got2.astype(jnp.float32), ((2 * key_rows - far, 0), (0, 0))
    )
    total = near + shifted
    place = lax.axis_index("head")
    bit = head_count // 2
    while bit >= 1:
        part = total.shape[0] // 2
        view = total.reshape(2, part, feat)
        mine = (place // bit) % 2
        send = lax.dynamic_index_in_dim(view, 1 - mine, 0, keepdims=False).astype(jnp.bfloat16)
        total = lax.dynamic_index_in_dim(view, mine, 0, keepdims=False) + swapped(
            send, "head", bit
        ).astype(jnp.float32)
        bit //= 2
    grad_latents = total

    sums = [
        halve_rest(keep, recv, device, ctx, own_rows, "ctx")
        for (keep, _), recv in zip(partials, received)
    ]
    grad_up_value = jnp.concatenate(sums, axis=1)
    return (grad_queries, grad_latents, grad_up_value)


def solution(mesh):
    return jax.shard_map(
        on_device,
        mesh=mesh,
        in_specs=(
            P("ctx", "head"),
            P("ctx", None),
            P(None, "head"),
            P("ctx", "head"),
            P("ctx", "head"),
            P("ctx", "head"),
            P(),
        ),
        out_specs=(P("ctx", "head"), P(("ctx", "head"), None), P("ctx", "head")),
        check_vma=False,
    )
```

```python
import functools
import math

import jax
import jax.numpy as jnp
from jax import lax
from jax.experimental import pallas as pl
from jax.experimental.pallas import tpu as pltpu
from jax.sharding import PartitionSpec as P

softmax_scale = 192.0 ** (-0.5)
log2e = math.log2(math.e)
vmem_bytes = 60 * 1024 * 1024
chunks = 2
pieces = 4


def nt_dot(a, b):
    return lax.dot_general(a, b, (((1,), (1,)), ((), ())), preferred_element_type=jnp.float32)


def nn_dot(a, b):
    return lax.dot_general(a, b, (((1,), (0,)), ((), ())), preferred_element_type=jnp.float32)


def stacked_heads(ref, heads, width, start):
    return jnp.concatenate([ref[:, start(h) : start(h) + width] for h in heads], axis=0)


def beside_heads(ref, heads, width):
    return jnp.concatenate([ref[:, h * width : (h + 1) * width] for h in heads], axis=1)


def on_diagonal(ref, heads, width):
    blocks = [ref[:, h * width : (h + 1) * width] for h in heads]
    zero = jnp.zeros_like(blocks[0])
    return jnp.concatenate(
        [
            jnp.concatenate([block if i == j else zero for j in range(len(blocks))], axis=1)
            for i, block in enumerate(blocks)
        ],
        axis=0,
    )


def heads_of(unit, parity, half):
    return [2 * half * unit + 2 * k + parity for k in range(half)]


def wide_rows(q_ref, heads, feat, width):
    return stacked_heads(
        q_ref, heads, width, lambda h: h * feat if h % 2 == 0 else (h + 1) * feat - width
    )


def forward_kernel(
    place_ref, docs_ref, *rest, units, half, rows, feat, lat, vdim, base, own_rows, first, key_rows,
):
    if first:
        (lat0_ref, lat1_ref, lat2_ref, q_ref, g_ref, lse_ref, p_ref, keep_ref, send_ref, ct_ref, c_ref, bias_ref) = rest
    else:
        (ct_ref, c_ref, q_ref, g_ref, lse_ref, _, p_ref, keep_ref, send_ref, bias_ref) = rest
    window, width = c_ref.shape[1:]
    far = window - key_rows
    place = place_ref[0]

    @pl.when(pl.program_id(0) == 0)
    def _():
        query_pos = place * key_rows + (key_rows - rows) + lax.broadcasted_iota(jnp.int32, (8, rows), 1)
        start = jnp.zeros((8, rows), jnp.int32)
        for i in range(docs_ref.shape[0]):
            entry = docs_ref[i]
            start = jnp.where(entry <= query_pos, jnp.maximum(start, entry), start)
        key_pos = place * key_rows - far + lax.broadcasted_iota(jnp.int32, (window, rows), 0)
        allowed = (key_pos >= start[:1]) & (key_pos <= query_pos[:1])
        bias_ref[...] = jnp.where(allowed, 0.0, -1e30)
        if first:
            ct_ref[:, : far - key_rows] = lat2_ref[...]
            ct_ref[:, far - key_rows : far] = lat1_ref[...]
            ct_ref[:, far:] = lat0_ref[...]
            gap = jnp.zeros((width - feat, window), ct_ref.dtype)
            c_ref[0] = jnp.concatenate([ct_ref[...], gap], axis=0).T
            c_ref[1] = jnp.concatenate([gap, ct_ref[...]], axis=0).T

    bias = bias_ref[...]
    core = place % 2
    for unit in range(units):
        for parity in range(2):
            heads = heads_of(unit, parity, half)
            scores = nt_dot(c_ref[parity], wide_rows(q_ref, heads, feat, width))
            probs = []
            for k, head in enumerate(heads):
                index = (pl.program_id(0) + base) * (2 * half * units) + head
                shift = lse_ref[pl.ds(index, 1), :] * log2e
                probs.append(
                    jnp.exp2(
                        scores[:, k * rows : (k + 1) * rows] * (softmax_scale * log2e) + (bias - shift)
                    ).astype(jnp.bfloat16)
                )
            prob = jnp.concatenate(probs, axis=1)
            column = (2 * unit + parity) * half * rows
            p_ref[:, column : column + half * rows] = prob
            olat = nn_dot(ct_ref[:lat, :], prob).astype(jnp.bfloat16)
            part = nn_dot(olat, on_diagonal(g_ref, heads, vdim))
            part = part.reshape(lat // (2 * own_rows), 2, own_rows, half * vdim)
            low, high = part[:, 0], part[:, 1]
            keep = jnp.where(core == 0, low, high).reshape(lat // 2, half * vdim).astype(keep_ref.dtype)
            send = jnp.where(core == 0, high, low).reshape(lat // 2, half * vdim).astype(send_ref.dtype)
            for k, head in enumerate(heads):
                lanes = slice(head * vdim, (head + 1) * vdim)
                keep_ref[:, lanes] = keep[:, k * vdim : (k + 1) * vdim]
                send_ref[:, lanes] = send[:, k * vdim : (k + 1) * vdim]


def backward_kernel(
    ct_ref, c_ref, q_ref, g_ref, o_ref, w_ref, p_ref, *rest,
    units, half, rows, feat, lat, vdim, steps, first, last, aliased, ties, key_rows,
):
    rest = list(rest)
    acc_in = None if first else rest.pop(0)
    if aliased:
        rest.pop(0)
    rest = rest[ties:]
    gq_ref = rest.pop(0)
    if last:
        near_ref, far1_ref, far2_ref, even_acc, odd_acc = rest
    else:
        acc_out, even_acc, odd_acc = rest
    window, width = c_ref.shape[1:]

    @pl.when(pl.program_id(0) == 0)
    def _():
        even_acc[...] = jnp.zeros_like(even_acc) if first else acc_in[...]
        odd_acc[...] = jnp.zeros_like(odd_acc)

    for unit in range(units):
        dscores, probs, glats, queries, turned = [], [], [], [], []
        for parity in range(2):
            heads = heads_of(unit, parity, half)
            column = (2 * unit + parity) * half * rows
            prob = p_ref[:, column : column + half * rows]
            glat = nt_dot(on_diagonal(g_ref, heads, vdim), beside_heads(w_ref, heads, vdim)).astype(jnp.bfloat16)
            gprob = nt_dot(c_ref[0, :, :lat], glat)
            dscore = []
            for k, head in enumerate(heads):
                lanes = slice(head * vdim, (head + 1) * vdim)
                product = g_ref[:, lanes].astype(jnp.float32) * o_ref[:, lanes].astype(jnp.float32)
                delta = jnp.sum(product.T, axis=0, keepdims=True)
                part = slice(k * rows, (k + 1) * rows)
                dscore.append(
                    (prob[:, part].astype(jnp.float32) * ((gprob[:, part] - delta) * softmax_scale)).astype(
                        jnp.bfloat16
                    )
                )
            dscore = jnp.concatenate(dscore, axis=1)
            turned.append(nn_dot(ct_ref[...], dscore).astype(jnp.bfloat16))
            dscores.append(dscore)
            probs.append(prob)
            glats.append(glat)
            queries.append(wide_rows(q_ref, heads, feat, width))
        for k in range(half):
            part = slice(k * rows, (k + 1) * rows)
            pair = jnp.concatenate([turned[0][:, part], turned[1][:, part]], axis=0)
            start = (unit * half + k) * 2 * feat
            gq_ref[:, start : start + 2 * feat] = pair.T
        even_acc[:, :lat] += nn_dot(
            jnp.concatenate([dscores[0], probs[0], probs[1]], axis=1),
            jnp.concatenate([queries[0][:, :lat], glats[0], glats[1]], axis=0),
        )
        even_acc[:, lat:] += nn_dot(dscores[0], queries[0][:, lat:])
        odd_acc[...] += nn_dot(dscores[1], queries[1])

    @pl.when(pl.program_id(0) == steps - 1)
    def _():
        total = even_acc[...] + pltpu.roll(odd_acc[...], feat, 1)
        if last:
            far2 = far2_ref.shape[1]
            total = total.T[:feat]
            far2_ref[...] = total[:, :far2].astype(far2_ref.dtype)
            far1_ref[...] = total[:, far2 : far2 + key_rows].astype(far1_ref.dtype)
            near_ref[...] = total[:, far2 + key_rows :]
        else:
            acc_out[...] = total


def passed_along(value, axis, steps):
    count = lax.axis_size(axis)
    first, last = (max(0, -steps), min(count, count - steps))
    return lax.ppermute(value, axis, [(source, source + steps) for source in range(first, last)])


def swapped(value, axis, bit):
    count = lax.axis_size(axis)
    return lax.ppermute(value, axis, [(source, source ^ bit) for source in range(count)])


def params():
    return pltpu.CompilerParams(dimension_semantics=("arbitrary",), vmem_limit_bytes=vmem_bytes)


def cost(flops, moved):
    return pl.CostEstimate(flops=int(flops), bytes_accessed=int(moved), transcendentals=0)


class Halving:
    def __init__(self, terms, bits, index, axis):
        self.terms, self.open, self.index, self.axis = terms, sorted(bits, reverse=True), index, axis
        self.order = list(bits)

    def pick(self, term, dim, which):
        return lax.dynamic_index_in_dim(term, which, dim, keepdims=False)

    def total(self, terms):
        return sum(term.astype(jnp.float32) for term in terms)

    def send(self):
        bit = self.order[0]
        dim = self.open.index(bit)
        mine = (self.index >> bit) & 1
        part = self.total([self.pick(term, dim, 1 - mine) for term in self.terms])
        self.terms = [self.pick(term, dim, mine) for term in self.terms]
        return part.astype(jnp.bfloat16)

    def take(self, part):
        bit = self.order.pop(0)
        self.open.remove(bit)
        shape = part.shape
        flat = part.reshape((-1, shape[-1]))
        self.terms.append(swapped(flat, self.axis, 1 << bit).reshape(shape))
        return self.terms[-1]


def on_device(queries, latents, up_value, grad_out, out_saved, log_sums, doc_starts):
    rows = queries.shape[0]
    key_rows, feat = latents.shape
    lat = up_value.shape[0]
    heads = log_sums.shape[1]
    vdim = grad_out.shape[1] // heads
    ctx = lax.axis_size("ctx")
    own_rows = lat // ctx
    window = 2 * key_rows + rows
    far = window - key_rows
    width = -(-feat // 128) * 128
    half = max(1, min(2, heads // pieces // 2))
    unit = 2 * half

    place = lax.axis_index("ctx").astype(jnp.int32)
    turned = latents.T
    prev1 = passed_along(turned, "ctx", 1)
    prev2 = passed_along(turned[:, key_rows - (far - key_rows) :], "ctx", 2)
    sums_turned = log_sums.T

    def whole(*shape):
        return pl.BlockSpec(shape, lambda i: (0,) * len(shape))

    smem = pl.BlockSpec(memory_space=pltpu.SMEM)
    untouched = pl.BlockSpec(memory_space=pl.ANY)
    scalar = place.reshape(1)

    probs = None
    partials = []
    chunk_heads = heads // chunks
    units = max(1, min(1, chunk_heads // unit))
    group = units * unit
    steps = chunk_heads // group
    for chunk in range(chunks):
        base = chunk * steps
        lanes = lambda i, base=base: (0, i + base)
        first = chunk == 0
        in_specs = [smem, smem]
        operands = [scalar, doc_starts]
        if first:
            in_specs += [whole(feat, key_rows), whole(feat, key_rows), whole(feat, far - key_rows)]
            operands += [turned, prev1, prev2]
        else:
            in_specs += [whole(feat, window), whole(2, window, width)]
            operands += [keys_turned, keys]
        in_specs += [
            pl.BlockSpec((rows, group * feat), lanes),
            pl.BlockSpec((rows, group * vdim), lanes),
            whole(heads, rows),
        ]
        operands += [queries, grad_out, sums_turned]
        out_specs = [
            pl.BlockSpec((window, group * rows), lanes),
            pl.BlockSpec((lat // 2, group * vdim), lambda i: (0, i)),
            pl.BlockSpec((lat // 2, group * vdim), lambda i: (0, i)),
        ]
        out_shape = [
            jax.ShapeDtypeStruct((window, heads * rows), jnp.bfloat16),
            jax.ShapeDtypeStruct((lat // 2, chunk_heads * vdim), jnp.bfloat16),
            jax.ShapeDtypeStruct((lat // 2, chunk_heads * vdim), jnp.bfloat16),
        ]
        aliases = {}
        if first:
            out_specs += [whole(feat, window), whole(2, window, width)]
            out_shape += [
                jax.ShapeDtypeStruct((feat, window), jnp.bfloat16),
                jax.ShapeDtypeStruct((2, window, width), jnp.bfloat16),
            ]
        else:
            aliases = {len(operands): 0}
            in_specs.append(untouched)
            operands.append(probs)
        out = pl.pallas_call(
            functools.partial(
                forward_kernel, units=units, half=half, rows=rows, feat=feat, lat=lat, vdim=vdim,
                base=base, own_rows=own_rows, first=first, key_rows=key_rows,
            ),
            grid=(steps,),
            in_specs=in_specs,
            out_specs=out_specs,
            out_shape=out_shape,
            scratch_shapes=[pltpu.VMEM((window, rows), jnp.float32)],
            input_output_aliases=aliases,
            compiler_params=params(),
            cost_estimate=cost(chunk_heads * rows * 2 * window * (width + lat) * 2, 8e6),
            name="forward",
        )(*operands)
        probs, keep, send = out[:3]
        if first:
            keys_turned, keys = out[3:]
        partials.append((keep, send))

    upper = list(range(1, ctx.bit_length() - 1))
    orders = [upper[1:] + upper[:1], upper]
    halvings = []
    chunk_cols = chunk_heads * vdim
    for (keep, send), order in zip(partials, orders):
        shape = (2,) * len(upper) + (own_rows, chunk_cols)
        got = swapped(send, "ctx", 1)
        halvings.append(Halving([keep.reshape(shape), got.reshape(shape)], order, place, "ctx"))
    along, across = halvings

    piece_heads = heads // pieces
    units = 1
    group = units * unit
    steps = piece_heads // group
    acc = grad_queries = None
    for piece in range(pieces):
        ties = []
        if piece % 2 == 0 and along.order:
            part = along.send()
            ties.append(part)
            along.take(part)
        elif across.order:
            part = across.send()
            ties.append(part)
            across.take(part)
        first, last = piece == 0, piece == pieces - 1
        base = piece * steps
        lanes = lambda i, base=base: (0, i + base)
        in_specs = [
            whole(feat, window),
            whole(2, window, width),
            pl.BlockSpec((rows, group * feat), lanes),
            pl.BlockSpec((rows, group * vdim), lanes),
            pl.BlockSpec((rows, group * vdim), lanes),
            pl.BlockSpec((lat, group * vdim), lanes),
            pl.BlockSpec((window, group * rows), lanes),
        ]
        operands = [keys_turned, keys, queries, grad_out, out_saved, up_value, probs]
        aliases = {}
        if not first:
            in_specs.append(whole(window, width))
            operands.append(acc)
            aliases[len(operands)] = 0
            in_specs.append(untouched)
            operands.append(grad_queries)
            if not last:
                aliases[len(operands) - 2] = 1
        in_specs += [untouched] * len(ties)
        operands += ties
        out_specs = [pl.BlockSpec((rows, group * feat), lanes)]
        out_shape = [jax.ShapeDtypeStruct(queries.shape, jnp.bfloat16)]
        if last:
            out_specs += [whole(feat, key_rows), whole(feat, key_rows), whole(feat, far - key_rows)]
            out_shape += [
                jax.ShapeDtypeStruct((feat, key_rows), jnp.float32),
                jax.ShapeDtypeStruct((feat, key_rows), jnp.bfloat16),
                jax.ShapeDtypeStruct((feat, far - key_rows), jnp.bfloat16),
            ]
        else:
            out_specs.append(whole(window, width))
            out_shape.append(jax.ShapeDtypeStruct((window, width), jnp.float32))
        out = pl.pallas_call(
            functools.partial(
                backward_kernel, units=units, half=half, rows=rows, feat=feat, lat=lat, vdim=vdim,
                steps=steps, first=first, last=last, aliased=not first, ties=len(ties), key_rows=key_rows,
            ),
            grid=(steps,),
            in_specs=in_specs,
            out_specs=out_specs,
            out_shape=out_shape,
            scratch_shapes=[pltpu.VMEM((window, width), jnp.float32)] * 2,
            input_output_aliases=aliases,
            compiler_params=params(),
            cost_estimate=cost(piece_heads * rows * 2 * window * (2 * width + 2 * lat) * 2, 8e6),
            name="backward",
        )(*operands)
        grad_queries, *rest = out
        if last:
            near, far1, far2 = rest
        else:
            (acc,) = rest

    got1 = passed_along(far1, "ctx", -1)
    got2 = passed_along(far2, "ctx", -2)
    spare = 2 * key_rows - far
    total = near + got1.astype(jnp.float32)
    total = jnp.concatenate([total[:, :spare], total[:, spare:] + got2.astype(jnp.float32)], axis=1)
    position = lax.axis_index("head")
    bit = lax.axis_size("head") // 2
    while bit >= 1:
        part = total.shape[1] // 2
        mine = (position // bit) % 2
        send = lax.dynamic_slice_in_dim(total, (1 - mine) * part, part, 1).astype(jnp.bfloat16)
        hold = lax.dynamic_slice_in_dim(total, mine * part, part, 1)
        total = hold + swapped(send, "head", bit).astype(jnp.float32)
        bit //= 2
    grad_latents = total.T

    while along.order or across.order:
        for halving in (along, across):
            if halving.order:
                halving.take(halving.send())
    grad_up_value = jnp.concatenate([h.total(h.terms) for h in halvings], axis=1)
    return (grad_queries, grad_latents, grad_up_value)


def solution(mesh):
    return jax.shard_map(
        on_device,
        mesh=mesh,
        in_specs=(
            P("ctx", "head"),
            P("ctx", None),
            P(None, "head"),
            P("ctx", "head"),
            P("ctx", "head"),
            P("ctx", "head"),
            P(),
        ),
        out_specs=(P("ctx", "head"), P(("ctx", "head"), None), P("ctx", "head")),
        check_vma=False,
    )
```

```python
import functools
import math

import jax
import jax.numpy as jnp
from jax import lax
from jax.experimental import pallas as pl
from jax.experimental.pallas import tpu as pltpu
from jax.sharding import PartitionSpec as P

softmax_scale = 192.0 ** (-0.5)
log2e = math.log2(math.e)
vmem_bytes = 60 * 1024 * 1024
chunks = 2
pieces = 4


def nt_dot(a, b):
    return lax.dot_general(a, b, (((1,), (1,)), ((), ())), preferred_element_type=jnp.float32)


def nn_dot(a, b):
    return lax.dot_general(a, b, (((1,), (0,)), ((), ())), preferred_element_type=jnp.float32)


def beside_heads(ref, heads, width):
    return jnp.concatenate([ref[:, h * width : (h + 1) * width] for h in heads], axis=1)


def on_diagonal(ref, heads, width):
    blocks = [ref[:, h * width : (h + 1) * width] for h in heads]
    zero = jnp.zeros_like(blocks[0])
    return jnp.concatenate(
        [
            jnp.concatenate([block if i == j else zero for j in range(len(blocks))], axis=1)
            for i, block in enumerate(blocks)
        ],
        axis=0,
    )


def pairs_of(unit, per_unit):
    heads = list(range(unit * per_unit, (unit + 1) * per_unit))
    return [heads[i : i + 2] for i in range(0, per_unit, 2)]


def wide_rows(q_ref, heads, feat, width):
    parts = []
    for head in heads:
        if head * feat % 128 == 0:
            parts.append(q_ref[:, head * feat : head * feat + width])
        else:
            end = (head + 1) * feat
            wide = q_ref[:, end - width : end]
            parts.append(jnp.concatenate([wide[:, width - feat :], wide[:, : width - feat]], axis=1))
    return jnp.concatenate(parts, axis=0)


def forward_kernel(
    place_ref, docs_ref, *rest, units, per_unit, rows, feat, lat, vdim, base, own_rows, first, key_rows,
):
    if first:
        (lat0_ref, lat1_ref, lat2_ref, q_ref, g_ref, lse_ref, p_ref, keep_ref, send_ref, ct_ref, c_ref, bias_ref) = rest
    else:
        (ct_ref, c_ref, q_ref, g_ref, lse_ref, _, p_ref, keep_ref, send_ref, bias_ref) = rest
    window, width = c_ref.shape
    far = window - key_rows
    place = place_ref[0]

    @pl.when(pl.program_id(0) == 0)
    def _():
        query_pos = place * key_rows + (key_rows - rows) + lax.broadcasted_iota(jnp.int32, (8, rows), 1)
        start = jnp.zeros((8, rows), jnp.int32)
        for i in range(docs_ref.shape[0]):
            entry = docs_ref[i]
            start = jnp.where(entry <= query_pos, jnp.maximum(start, entry), start)
        key_pos = place * key_rows - far + lax.broadcasted_iota(jnp.int32, (window, rows), 0)
        allowed = (key_pos >= start[:1]) & (key_pos <= query_pos[:1])
        bias_ref[...] = jnp.where(allowed, 0.0, -1e30)
        if first:
            ct_ref[:, : far - key_rows] = lat2_ref[...]
            ct_ref[:, far - key_rows : far] = lat1_ref[...]
            ct_ref[:, far:] = lat0_ref[...]
            gap = jnp.zeros((width - feat, window), ct_ref.dtype)
            c_ref[...] = jnp.concatenate([ct_ref[...], gap], axis=0).T

    bias = bias_ref[...]
    core = place % 2
    for unit in range(units):
        pairs = pairs_of(unit, per_unit)
        heads = sum(pairs, [])
        scores = nt_dot(c_ref[...], wide_rows(q_ref, heads, feat, width))
        probs = []
        for k, head in enumerate(heads):
            index = (pl.program_id(0) + base) * (per_unit * units) + head
            shift = lse_ref[pl.ds(index, 1), :] * log2e
            probs.append(
                jnp.exp2(
                    scores[:, k * rows : (k + 1) * rows] * (softmax_scale * log2e) + (bias - shift)
                ).astype(jnp.bfloat16)
            )
        prob = jnp.concatenate(probs, axis=1)
        p_ref[:, unit * per_unit * rows : (unit + 1) * per_unit * rows] = prob
        olat = nn_dot(ct_ref[:lat, :], prob).astype(jnp.bfloat16)
        for i, pair in enumerate(pairs):
            part = nn_dot(olat[:, 2 * i * rows : 2 * (i + 1) * rows], on_diagonal(g_ref, pair, vdim))
            part = part.reshape(lat // (2 * own_rows), 2, own_rows, 2 * vdim)
            low, high = part[:, 0], part[:, 1]
            lanes = slice(pair[0] * vdim, (pair[0] + 2) * vdim)
            keep_ref[:, lanes] = (
                jnp.where(core == 0, low, high).reshape(lat // 2, 2 * vdim).astype(keep_ref.dtype)
            )
            send_ref[:, lanes] = (
                jnp.where(core == 0, high, low).reshape(lat // 2, 2 * vdim).astype(send_ref.dtype)
            )


def backward_kernel(
    ct_ref, c_ref, q_ref, g_ref, o_ref, w_ref, p_ref, *rest,
    units, per_unit, rows, feat, lat, vdim, steps, first, last, aliased, ties, key_rows,
):
    rest = list(rest)
    acc_in = None if first else rest.pop(0)
    if aliased:
        rest.pop(0)
    rest = rest[ties:]
    gq_ref = rest.pop(0)
    if last:
        near_ref, far1_ref, far2_ref, acc = rest
    else:
        acc_out, acc = rest
    window, width = c_ref.shape

    @pl.when(pl.program_id(0) == 0)
    def _():
        acc[...] = jnp.zeros_like(acc) if first else acc_in[...]

    for unit in range(units):
        pairs = pairs_of(unit, per_unit)
        heads = sum(pairs, [])
        prob = p_ref[:, unit * per_unit * rows : (unit + 1) * per_unit * rows]
        glat = jnp.concatenate(
            [
                nt_dot(on_diagonal(g_ref, pair, vdim), beside_heads(w_ref, pair, vdim)).astype(jnp.bfloat16)
                for pair in pairs
            ],
            axis=0,
        )
        gprob = nt_dot(c_ref[:, :lat], glat)
        dscore = []
        for k, head in enumerate(heads):
            lanes = slice(head * vdim, (head + 1) * vdim)
            product = g_ref[:, lanes].astype(jnp.float32) * o_ref[:, lanes].astype(jnp.float32)
            delta = jnp.sum(product.T, axis=0, keepdims=True)
            part = slice(k * rows, (k + 1) * rows)
            dscore.append(
                (prob[:, part].astype(jnp.float32) * ((gprob[:, part] - delta) * softmax_scale)).astype(
                    jnp.bfloat16
                )
            )
        dscore = jnp.concatenate(dscore, axis=1)
        turned = nn_dot(ct_ref[...], dscore).astype(jnp.bfloat16)
        for i, pair in enumerate(pairs):
            both = jnp.concatenate(
                [turned[:, (2 * i + j) * rows : (2 * i + j + 1) * rows] for j in range(2)], axis=0
            )
            gq_ref[:, pair[0] * feat : (pair[0] + 2) * feat] = both.T
        query = wide_rows(q_ref, heads, feat, width)
        acc[:, :lat] += nn_dot(
            jnp.concatenate([dscore, prob], axis=1), jnp.concatenate([query[:, :lat], glat], axis=0)
        )
        acc[:, lat:] += nn_dot(dscore, query[:, lat:])

    @pl.when(pl.program_id(0) == steps - 1)
    def _():
        if last:
            far2 = far2_ref.shape[1]
            total = acc[...].T[:feat]
            far2_ref[...] = total[:, :far2].astype(far2_ref.dtype)
            far1_ref[...] = total[:, far2 : far2 + key_rows].astype(far1_ref.dtype)
            near_ref[...] = total[:, far2 + key_rows :]
        else:
            acc_out[...] = acc[...]


def passed_along(value, axis, steps):
    count = lax.axis_size(axis)
    first, last = (max(0, -steps), min(count, count - steps))
    return lax.ppermute(value, axis, [(source, source + steps) for source in range(first, last)])


def swapped(value, axis, bit):
    count = lax.axis_size(axis)
    return lax.ppermute(value, axis, [(source, source ^ bit) for source in range(count)])


def params():
    return pltpu.CompilerParams(dimension_semantics=("arbitrary",), vmem_limit_bytes=vmem_bytes)


def cost(flops, moved):
    return pl.CostEstimate(flops=int(flops), bytes_accessed=int(moved), transcendentals=0)


class Halving:
    def __init__(self, terms, bits, index, axis):
        self.terms, self.open, self.index, self.axis = terms, sorted(bits, reverse=True), index, axis
        self.order = list(bits)

    def pick(self, term, dim, which):
        return lax.dynamic_index_in_dim(term, which, dim, keepdims=False)

    def total(self, terms):
        return sum(term.astype(jnp.float32) for term in terms)

    def send(self):
        bit = self.order[0]
        dim = self.open.index(bit)
        mine = (self.index >> bit) & 1
        part = self.total([self.pick(term, dim, 1 - mine) for term in self.terms])
        self.terms = [self.pick(term, dim, mine) for term in self.terms]
        return part.astype(jnp.bfloat16)

    def take(self, part):
        bit = self.order.pop(0)
        self.open.remove(bit)
        shape = part.shape
        flat = part.reshape((-1, shape[-1]))
        self.terms.append(swapped(flat, self.axis, 1 << bit).reshape(shape))
        return self.terms[-1]


def on_device(queries, latents, up_value, grad_out, out_saved, log_sums, doc_starts):
    rows = queries.shape[0]
    key_rows, feat = latents.shape
    lat = up_value.shape[0]
    heads = log_sums.shape[1]
    vdim = grad_out.shape[1] // heads
    ctx = lax.axis_size("ctx")
    own_rows = lat // ctx
    window = 2 * key_rows + rows
    far = window - key_rows
    width = -(-feat // 128) * 128
    unit = max(2, min(4, heads // pieces))

    place = lax.axis_index("ctx").astype(jnp.int32)
    turned = latents.T
    prev1 = passed_along(turned, "ctx", 1)
    prev2 = passed_along(turned[:, key_rows - (far - key_rows) :], "ctx", 2)
    sums_turned = log_sums.T

    def whole(*shape):
        return pl.BlockSpec(shape, lambda i: (0,) * len(shape))

    smem = pl.BlockSpec(memory_space=pltpu.SMEM)
    untouched = pl.BlockSpec(memory_space=pl.ANY)
    scalar = place.reshape(1)

    probs = None
    partials = []
    chunk_heads = heads // chunks
    units = max(1, min(1, chunk_heads // unit))
    group = units * unit
    steps = chunk_heads // group
    for chunk in range(chunks):
        base = chunk * steps
        lanes = lambda i, base=base: (0, i + base)
        first = chunk == 0
        in_specs = [smem, smem]
        operands = [scalar, doc_starts]
        if first:
            in_specs += [whole(feat, key_rows), whole(feat, key_rows), whole(feat, far - key_rows)]
            operands += [turned, prev1, prev2]
        else:
            in_specs += [whole(feat, window), whole(window, width)]
            operands += [keys_turned, keys]
        in_specs += [
            pl.BlockSpec((rows, group * feat), lanes),
            pl.BlockSpec((rows, group * vdim), lanes),
            whole(heads, rows),
        ]
        operands += [queries, grad_out, sums_turned]
        out_specs = [
            pl.BlockSpec((window, group * rows), lanes),
            pl.BlockSpec((lat // 2, group * vdim), lambda i: (0, i)),
            pl.BlockSpec((lat // 2, group * vdim), lambda i: (0, i)),
        ]
        out_shape = [
            jax.ShapeDtypeStruct((window, heads * rows), jnp.bfloat16),
            jax.ShapeDtypeStruct((lat // 2, chunk_heads * vdim), jnp.bfloat16),
            jax.ShapeDtypeStruct((lat // 2, chunk_heads * vdim), jnp.bfloat16),
        ]
        aliases = {}
        if first:
            out_specs += [whole(feat, window), whole(window, width)]
            out_shape += [
                jax.ShapeDtypeStruct((feat, window), jnp.bfloat16),
                jax.ShapeDtypeStruct((window, width), jnp.bfloat16),
            ]
        else:
            aliases = {len(operands): 0}
            in_specs.append(untouched)
            operands.append(probs)
        out = pl.pallas_call(
            functools.partial(
                forward_kernel, units=units, per_unit=unit, rows=rows, feat=feat, lat=lat, vdim=vdim,
                base=base, own_rows=own_rows, first=first, key_rows=key_rows,
            ),
            grid=(steps,),
            in_specs=in_specs,
            out_specs=out_specs,
            out_shape=out_shape,
            scratch_shapes=[pltpu.VMEM((window, rows), jnp.float32)],
            input_output_aliases=aliases,
            compiler_params=params(),
            cost_estimate=cost(chunk_heads * rows * 2 * window * (width + lat) * 2, 8e6),
            name="forward",
        )(*operands)
        probs, keep, send = out[:3]
        if first:
            keys_turned, keys = out[3:]
        partials.append((keep, send))

    upper = list(range(1, ctx.bit_length() - 1))
    orders = [upper[1:] + upper[:1], upper]
    halvings = []
    chunk_cols = chunk_heads * vdim
    for (keep, send), order in zip(partials, orders):
        shape = (2,) * len(upper) + (own_rows, chunk_cols)
        got = swapped(send, "ctx", 1)
        halvings.append(Halving([keep.reshape(shape), got.reshape(shape)], order, place, "ctx"))
    along, across = halvings

    piece_heads = heads // pieces
    units = 1
    group = units * unit
    steps = piece_heads // group
    acc = grad_queries = None
    for piece in range(pieces):
        ties = []
        if piece % 2 == 0 and along.order:
            part = along.send()
            ties.append(part)
            along.take(part)
        elif across.order:
            part = across.send()
            ties.append(part)
            across.take(part)
        first, last = piece == 0, piece == pieces - 1
        base = piece * steps
        lanes = lambda i, base=base: (0, i + base)
        in_specs = [
            whole(feat, window),
            whole(window, width),
            pl.BlockSpec((rows, group * feat), lanes),
            pl.BlockSpec((rows, group * vdim), lanes),
            pl.BlockSpec((rows, group * vdim), lanes),
            pl.BlockSpec((lat, group * vdim), lanes),
            pl.BlockSpec((window, group * rows), lanes),
        ]
        operands = [keys_turned, keys, queries, grad_out, out_saved, up_value, probs]
        aliases = {}
        if not first:
            in_specs.append(whole(window, width))
            operands.append(acc)
            aliases[len(operands)] = 0
            in_specs.append(untouched)
            operands.append(grad_queries)
            if not last:
                aliases[len(operands) - 2] = 1
        in_specs += [untouched] * len(ties)
        operands += ties
        out_specs = [pl.BlockSpec((rows, group * feat), lanes)]
        out_shape = [jax.ShapeDtypeStruct(queries.shape, jnp.bfloat16)]
        if last:
            out_specs += [whole(feat, key_rows), whole(feat, key_rows), whole(feat, far - key_rows)]
            out_shape += [
                jax.ShapeDtypeStruct((feat, key_rows), jnp.float32),
                jax.ShapeDtypeStruct((feat, key_rows), jnp.bfloat16),
                jax.ShapeDtypeStruct((feat, far - key_rows), jnp.bfloat16),
            ]
        else:
            out_specs.append(whole(window, width))
            out_shape.append(jax.ShapeDtypeStruct((window, width), jnp.float32))
        out = pl.pallas_call(
            functools.partial(
                backward_kernel, units=units, per_unit=unit, rows=rows, feat=feat, lat=lat, vdim=vdim,
                steps=steps, first=first, last=last, aliased=not first, ties=len(ties), key_rows=key_rows,
            ),
            grid=(steps,),
            in_specs=in_specs,
            out_specs=out_specs,
            out_shape=out_shape,
            scratch_shapes=[pltpu.VMEM((window, width), jnp.float32)],
            input_output_aliases=aliases,
            compiler_params=params(),
            cost_estimate=cost(piece_heads * rows * 2 * window * (2 * width + 2 * lat) * 2, 8e6),
            name="backward",
        )(*operands)
        grad_queries, *rest = out
        if last:
            near, far1, far2 = rest
        else:
            (acc,) = rest

    got1 = passed_along(far1, "ctx", -1)
    got2 = passed_along(far2, "ctx", -2)
    spare = 2 * key_rows - far
    total = near + got1.astype(jnp.float32)
    total = jnp.concatenate([total[:, :spare], total[:, spare:] + got2.astype(jnp.float32)], axis=1)
    position = lax.axis_index("head")
    bit = lax.axis_size("head") // 2
    while bit >= 1:
        part = total.shape[1] // 2
        mine = (position // bit) % 2
        send = lax.dynamic_slice_in_dim(total, (1 - mine) * part, part, 1).astype(jnp.bfloat16)
        hold = lax.dynamic_slice_in_dim(total, mine * part, part, 1)
        total = hold + swapped(send, "head", bit).astype(jnp.float32)
        bit //= 2
    grad_latents = total.T

    while along.order or across.order:
        for halving in (along, across):
            if halving.order:
                halving.take(halving.send())
    grad_up_value = jnp.concatenate([h.total(h.terms) for h in halvings], axis=1)
    return (grad_queries, grad_latents, grad_up_value)


def solution(mesh):
    return jax.shard_map(
        on_device,
        mesh=mesh,
        in_specs=(
            P("ctx", "head"),
            P("ctx", None),
            P(None, "head"),
            P("ctx", "head"),
            P("ctx", "head"),
            P("ctx", "head"),
            P(),
        ),
        out_specs=(P("ctx", "head"), P(("ctx", "head"), None), P("ctx", "head")),
        check_vma=False,
    )
```

```python
import functools
import math

import jax
import jax.numpy as jnp
from jax import lax
from jax.experimental import pallas as pl
from jax.experimental.pallas import tpu as pltpu
from jax.sharding import PartitionSpec as P

softmax_scale = 192.0 ** (-0.5)
log2e = math.log2(math.e)
vmem_bytes = 60 * 1024 * 1024
chunks = 2
pieces = 2


def nt_dot(a, b):
    return lax.dot_general(a, b, (((1,), (1,)), ((), ())), preferred_element_type=jnp.float32)


def nn_dot(a, b):
    return lax.dot_general(a, b, (((1,), (0,)), ((), ())), preferred_element_type=jnp.float32)


def beside_heads(ref, heads, width):
    return jnp.concatenate([ref[:, h * width : (h + 1) * width] for h in heads], axis=1)


def on_diagonal(ref, heads, width):
    blocks = [ref[:, h * width : (h + 1) * width] for h in heads]
    zero = jnp.zeros_like(blocks[0])
    return jnp.concatenate(
        [
            jnp.concatenate([block if i == j else zero for j in range(len(blocks))], axis=1)
            for i, block in enumerate(blocks)
        ],
        axis=0,
    )


def pairs_of(unit, per_unit):
    heads = list(range(unit * per_unit, (unit + 1) * per_unit))
    return [heads[i : i + 2] for i in range(0, per_unit, 2)]


def wide_rows(q_ref, heads, feat, width):
    parts = []
    for head in heads:
        if head * feat % 128 == 0:
            parts.append(q_ref[:, head * feat : head * feat + width])
        else:
            end = (head + 1) * feat
            wide = q_ref[:, end - width : end]
            parts.append(jnp.concatenate([wide[:, width - feat :], wide[:, : width - feat]], axis=1))
    return jnp.concatenate(parts, axis=0)


def forward_kernel(
    place_ref, docs_ref, *rest, units, per_unit, rows, feat, lat, vdim, base, own_rows, first, key_rows,
):
    if first:
        (lat0_ref, lat1_ref, lat2_ref, q_ref, g_ref, lse_ref, p_ref, keep_ref, send_ref, ct_ref, c_ref, bias_ref) = rest
    else:
        (ct_ref, c_ref, q_ref, g_ref, lse_ref, _, p_ref, keep_ref, send_ref, bias_ref) = rest
    window, width = c_ref.shape
    far = window - key_rows
    place = place_ref[0]

    @pl.when(pl.program_id(0) == 0)
    def _():
        query_pos = place * key_rows + (key_rows - rows) + lax.broadcasted_iota(jnp.int32, (8, rows), 1)
        start = jnp.zeros((8, rows), jnp.int32)
        for i in range(docs_ref.shape[0]):
            entry = docs_ref[i]
            start = jnp.where(entry <= query_pos, jnp.maximum(start, entry), start)
        key_pos = place * key_rows - far + lax.broadcasted_iota(jnp.int32, (window, rows), 0)
        allowed = (key_pos >= start[:1]) & (key_pos <= query_pos[:1])
        bias_ref[...] = jnp.where(allowed, 0.0, -1e30)
        if first:
            ct_ref[:, : far - key_rows] = lat2_ref[...]
            ct_ref[:, far - key_rows : far] = lat1_ref[...]
            ct_ref[:, far:] = lat0_ref[...]
            gap = jnp.zeros((width - feat, window), ct_ref.dtype)
            c_ref[...] = jnp.concatenate([ct_ref[...], gap], axis=0).T

    bias = bias_ref[...]
    core = place % 2
    span = per_unit * rows
    groups = [pairs_of(unit, per_unit) for unit in range(units)]
    scores = [nt_dot(c_ref[...], wide_rows(q_ref, sum(pairs, []), feat, width)) for pairs in groups]
    for unit, pairs in enumerate(groups):
        for k, head in enumerate(sum(pairs, [])):
            index = (pl.program_id(0) + base) * (per_unit * units) + head
            shift = lse_ref[pl.ds(index, 1), :] * log2e
            column = unit * span + k * rows
            p_ref[:, column : column + rows] = jnp.exp2(
                scores[unit][:, k * rows : (k + 1) * rows] * (softmax_scale * log2e) + (bias - shift)
            ).astype(jnp.bfloat16)
    olats = [
        nn_dot(ct_ref[:lat, :], p_ref[:, unit * span : (unit + 1) * span]).astype(jnp.bfloat16)
        for unit in range(units)
    ]
    for unit, pairs in enumerate(groups):
        for i, pair in enumerate(pairs):
            part = nn_dot(
                olats[unit][:, 2 * i * rows : 2 * (i + 1) * rows], on_diagonal(g_ref, pair, vdim)
            )
            part = part.reshape(lat // (2 * own_rows), 2, own_rows, 2 * vdim)
            low, high = part[:, 0], part[:, 1]
            lanes = slice(pair[0] * vdim, (pair[0] + 2) * vdim)
            keep_ref[:, lanes] = (
                jnp.where(core == 0, low, high).reshape(lat // 2, 2 * vdim).astype(keep_ref.dtype)
            )
            send_ref[:, lanes] = (
                jnp.where(core == 0, high, low).reshape(lat // 2, 2 * vdim).astype(send_ref.dtype)
            )


def backward_kernel(
    c_ref, q_ref, g_ref, o_ref, w_ref, p_ref, *rest,
    units, per_unit, rows, feat, lat, vdim, steps, first, last, ties, key_rows,
):
    rest = list(rest)
    acc_in = None if first else rest.pop(0)
    if not first:
        rest.pop(0)
    rest = rest[ties:]
    ds_ref = rest.pop(0)
    if last:
        near_ref, far1_ref, far2_ref, acc = rest
    else:
        acc_out, acc = rest
    span = per_unit * rows

    @pl.when(pl.program_id(0) == 0)
    def _():
        acc[...] = jnp.zeros_like(acc) if first else acc_in[...]

    groups = [pairs_of(unit, per_unit) for unit in range(units)]
    glats = [
        jnp.concatenate(
            [
                nt_dot(on_diagonal(g_ref, pair, vdim), beside_heads(w_ref, pair, vdim)).astype(jnp.bfloat16)
                for pair in pairs
            ],
            axis=0,
        )
        for pairs in groups
    ]
    gprobs = [nt_dot(c_ref[:, :lat], glat) for glat in glats]
    for unit, pairs in enumerate(groups):
        for k, head in enumerate(sum(pairs, [])):
            lanes = slice(head * vdim, (head + 1) * vdim)
            product = g_ref[:, lanes].astype(jnp.float32) * o_ref[:, lanes].astype(jnp.float32)
            delta = jnp.sum(product.T, axis=0, keepdims=True)
            own = slice(unit * span + k * rows, unit * span + (k + 1) * rows)
            ds_ref[:, own] = (
                p_ref[:, own].astype(jnp.float32)
                * ((gprobs[unit][:, k * rows : (k + 1) * rows] - delta) * softmax_scale)
            ).astype(jnp.bfloat16)
    queries = [wide_rows(q_ref, sum(pairs, []), feat, acc.shape[1]) for pairs in groups]
    acc[:, :lat] += nn_dot(
        jnp.concatenate([ds_ref[...], p_ref[...]], axis=1),
        jnp.concatenate([query[:, :lat] for query in queries] + glats, axis=0),
    )
    acc[:, lat:] += nn_dot(ds_ref[...], jnp.concatenate([query[:, lat:] for query in queries], axis=0))

    @pl.when(pl.program_id(0) == steps - 1)
    def _():
        if last:
            far2 = far2_ref.shape[1]
            total = acc[...].T[:feat]
            far2_ref[...] = total[:, :far2].astype(far2_ref.dtype)
            far1_ref[...] = total[:, far2 : far2 + key_rows].astype(far1_ref.dtype)
            near_ref[...] = total[:, far2 + key_rows :]
        else:
            acc_out[...] = acc[...]


def query_kernel(ct_ref, ds_ref, *rest, pairs, rows, feat):
    gq_ref = rest[-1]
    turned = nn_dot(ct_ref[...], ds_ref[...]).astype(jnp.bfloat16)
    for i in range(pairs):
        both = jnp.concatenate(
            [turned[:, (2 * i + j) * rows : (2 * i + j + 1) * rows] for j in range(2)], axis=0
        )
        gq_ref[:, 2 * i * feat : 2 * (i + 1) * feat] = both.T


def passed_along(value, axis, steps):
    count = lax.axis_size(axis)
    first, last = (max(0, -steps), min(count, count - steps))
    return lax.ppermute(value, axis, [(source, source + steps) for source in range(first, last)])


def swapped(value, axis, bit):
    count = lax.axis_size(axis)
    return lax.ppermute(value, axis, [(source, source ^ bit) for source in range(count)])


def params():
    return pltpu.CompilerParams(dimension_semantics=("arbitrary",), vmem_limit_bytes=vmem_bytes)


def cost(flops, moved):
    return pl.CostEstimate(flops=int(flops), bytes_accessed=int(moved), transcendentals=0)


class Halving:
    def __init__(self, terms, bits, index, axis):
        self.terms, self.open, self.index, self.axis = terms, sorted(bits, reverse=True), index, axis
        self.order = list(bits)

    def pick(self, term, dim, which):
        return lax.dynamic_index_in_dim(term, which, dim, keepdims=False)

    def total(self, terms):
        return sum(term.astype(jnp.float32) for term in terms)

    def send(self):
        bit = self.order[0]
        dim = self.open.index(bit)
        mine = (self.index >> bit) & 1
        part = self.total([self.pick(term, dim, 1 - mine) for term in self.terms])
        self.terms = [self.pick(term, dim, mine) for term in self.terms]
        return part.astype(jnp.bfloat16)

    def take(self, part):
        bit = self.order.pop(0)
        self.open.remove(bit)
        shape = part.shape
        flat = part.reshape((-1, shape[-1]))
        self.terms.append(swapped(flat, self.axis, 1 << bit).reshape(shape))
        return self.terms[-1]


def on_device(queries, latents, up_value, grad_out, out_saved, log_sums, doc_starts):
    rows = queries.shape[0]
    key_rows, feat = latents.shape
    lat = up_value.shape[0]
    heads = log_sums.shape[1]
    vdim = grad_out.shape[1] // heads
    ctx = lax.axis_size("ctx")
    own_rows = lat // ctx
    window = 2 * key_rows + rows
    far = window - key_rows
    width = -(-feat // 128) * 128
    unit = max(2, min(4, heads // pieces))

    place = lax.axis_index("ctx").astype(jnp.int32)
    turned = latents.T
    prev1 = passed_along(turned, "ctx", 1)
    prev2 = passed_along(turned[:, key_rows - (far - key_rows) :], "ctx", 2)
    sums_turned = log_sums.T

    def whole(*shape):
        return pl.BlockSpec(shape, lambda i: (0,) * len(shape))

    smem = pl.BlockSpec(memory_space=pltpu.SMEM)
    untouched = pl.BlockSpec(memory_space=pl.ANY)
    scalar = place.reshape(1)

    probs = None
    partials = []
    chunk_heads = heads // chunks
    units = max(1, min(2, chunk_heads // unit))
    group = units * unit
    steps = chunk_heads // group
    for chunk in range(chunks):
        base = chunk * steps
        lanes = lambda i, base=base: (0, i + base)
        first = chunk == 0
        in_specs = [smem, smem]
        operands = [scalar, doc_starts]
        if first:
            in_specs += [whole(feat, key_rows), whole(feat, key_rows), whole(feat, far - key_rows)]
            operands += [turned, prev1, prev2]
        else:
            in_specs += [whole(feat, window), whole(window, width)]
            operands += [keys_turned, keys]
        in_specs += [
            pl.BlockSpec((rows, group * feat), lanes),
            pl.BlockSpec((rows, group * vdim), lanes),
            whole(heads, rows),
        ]
        operands += [queries, grad_out, sums_turned]
        out_specs = [
            pl.BlockSpec((window, group * rows), lanes),
            pl.BlockSpec((lat // 2, group * vdim), lambda i: (0, i)),
            pl.BlockSpec((lat // 2, group * vdim), lambda i: (0, i)),
        ]
        out_shape = [
            jax.ShapeDtypeStruct((window, heads * rows), jnp.bfloat16),
            jax.ShapeDtypeStruct((lat // 2, chunk_heads * vdim), jnp.bfloat16),
            jax.ShapeDtypeStruct((lat // 2, chunk_heads * vdim), jnp.bfloat16),
        ]
        aliases = {}
        if first:
            out_specs += [whole(feat, window), whole(window, width)]
            out_shape += [
                jax.ShapeDtypeStruct((feat, window), jnp.bfloat16),
                jax.ShapeDtypeStruct((window, width), jnp.bfloat16),
            ]
        else:
            aliases = {len(operands): 0}
            in_specs.append(untouched)
            operands.append(probs)
        out = pl.pallas_call(
            functools.partial(
                forward_kernel, units=units, per_unit=unit, rows=rows, feat=feat, lat=lat, vdim=vdim,
                base=base, own_rows=own_rows, first=first, key_rows=key_rows,
            ),
            grid=(steps,),
            in_specs=in_specs,
            out_specs=out_specs,
            out_shape=out_shape,
            scratch_shapes=[pltpu.VMEM((window, rows), jnp.float32)],
            input_output_aliases=aliases,
            compiler_params=params(),
            cost_estimate=cost(chunk_heads * rows * 2 * window * (width + lat) * 2, 8e6),
            name="forward",
        )(*operands)
        probs, keep, send = out[:3]
        if first:
            keys_turned, keys = out[3:]
        partials.append((keep, send))

    upper = list(range(1, ctx.bit_length() - 1))
    orders = [upper[1:] + upper[:1], upper]
    halvings = []
    chunk_cols = chunk_heads * vdim
    for (keep, send), order in zip(partials, orders):
        shape = (2,) * len(upper) + (own_rows, chunk_cols)
        got = swapped(send, "ctx", 1)
        halvings.append(Halving([keep.reshape(shape), got.reshape(shape)], order, place, "ctx"))

    piece_heads = heads // pieces
    units = max(1, min(2, piece_heads // unit))
    group = units * unit
    steps = piece_heads // group
    acc = dscores = None
    for piece in range(pieces):
        ties = []
        for halving in halvings:
            part = halving.send()
            ties.append(part)
            halving.take(part)
        first, last = piece == 0, piece == pieces - 1
        base = piece * steps
        lanes = lambda i, base=base: (0, i + base)
        in_specs = [
            whole(window, width),
            pl.BlockSpec((rows, group * feat), lanes),
            pl.BlockSpec((rows, group * vdim), lanes),
            pl.BlockSpec((rows, group * vdim), lanes),
            pl.BlockSpec((lat, group * vdim), lanes),
            pl.BlockSpec((window, group * rows), lanes),
        ]
        operands = [keys, queries, grad_out, out_saved, up_value, probs]
        aliases = {}
        if not first:
            in_specs.append(whole(window, width))
            operands.append(acc)
            aliases[len(operands)] = 0
            in_specs.append(untouched)
            operands.append(dscores)
        in_specs += [untouched] * len(ties)
        operands += ties
        out_specs = [pl.BlockSpec((window, group * rows), lanes)]
        out_shape = [jax.ShapeDtypeStruct((window, heads * rows), jnp.bfloat16)]
        if last:
            out_specs += [whole(feat, key_rows), whole(feat, key_rows), whole(feat, far - key_rows)]
            out_shape += [
                jax.ShapeDtypeStruct((feat, key_rows), jnp.float32),
                jax.ShapeDtypeStruct((feat, key_rows), jnp.bfloat16),
                jax.ShapeDtypeStruct((feat, far - key_rows), jnp.bfloat16),
            ]
        else:
            out_specs.append(whole(window, width))
            out_shape.append(jax.ShapeDtypeStruct((window, width), jnp.float32))
        out = pl.pallas_call(
            functools.partial(
                backward_kernel, units=units, per_unit=unit, rows=rows, feat=feat, lat=lat, vdim=vdim,
                steps=steps, first=first, last=last, ties=len(ties), key_rows=key_rows,
            ),
            grid=(steps,),
            in_specs=in_specs,
            out_specs=out_specs,
            out_shape=out_shape,
            scratch_shapes=[pltpu.VMEM((window, width), jnp.float32)],
            input_output_aliases=aliases,
            compiler_params=params(),
            cost_estimate=cost(piece_heads * rows * 2 * window * (width + 2 * lat) * 2, 8e6),
            name="backward",
        )(*operands)
        dscores, *rest = out
        if last:
            near, far1, far2 = rest
        else:
            (acc,) = rest

    def query_gradient(piece, so_far, ties):
        base = piece * steps
        lanes = lambda i: (0, i + base)
        extra = ([] if so_far is None else [so_far]) + ties
        return pl.pallas_call(
            functools.partial(query_kernel, pairs=group // 2, rows=rows, feat=feat),
            grid=(steps,),
            in_specs=[whole(feat, window), pl.BlockSpec((window, group * rows), lanes)] + [untouched] * len(extra),
            out_specs=pl.BlockSpec((rows, group * feat), lanes),
            out_shape=jax.ShapeDtypeStruct(queries.shape, jnp.bfloat16),
            input_output_aliases={} if so_far is None else {2: 0},
            compiler_params=params(),
            cost_estimate=cost(piece_heads * rows * 2 * window * width * 3, 8e6),
            name="query_gradient",
        )(keys_turned, dscores, *extra)

    got1 = passed_along(far1, "ctx", -1)
    got2 = passed_along(far2, "ctx", -2)
    spare = 2 * key_rows - far
    ties = []
    for halving in halvings:
        if halving.order:
            part = halving.send()
            ties.append(part)
            halving.take(part)
    grad_queries = query_gradient(0, None, ties)
    total = near + got1.astype(jnp.float32)
    total = jnp.concatenate([total[:, :spare], total[:, spare:] + got2.astype(jnp.float32)], axis=1)
    position = lax.axis_index("head")
    bit = lax.axis_size("head") // 2
    ties = []
    while bit >= 1:
        part = total.shape[1] // 2
        mine = (position // bit) % 2
        send = lax.dynamic_slice_in_dim(total, (1 - mine) * part, part, 1).astype(jnp.bfloat16)
        hold = lax.dynamic_slice_in_dim(total, mine * part, part, 1)
        ties = ties or [send]
        total = hold + swapped(send, "head", bit).astype(jnp.float32)
        bit //= 2
    grad_latents = total.T

    grad_queries = query_gradient(1, grad_queries, ties)
    while any(halving.order for halving in halvings):
        for halving in halvings:
            if halving.order:
                halving.take(halving.send())
    grad_up_value = jnp.concatenate([h.total(h.terms) for h in halvings], axis=1)
    return (grad_queries, grad_latents, grad_up_value)


def solution(mesh):
    return jax.shard_map(
        on_device,
        mesh=mesh,
        in_specs=(
            P("ctx", "head"),
            P("ctx", None),
            P(None, "head"),
            P("ctx", "head"),
            P("ctx", "head"),
            P("ctx", "head"),
            P(),
        ),
        out_specs=(P("ctx", "head"), P(("ctx", "head"), None), P("ctx", "head")),
        check_vma=False,
    )
```

```python
import functools

import jax
import jax.numpy as jnp
from jax import lax
from jax.experimental import pallas as pl
from jax.experimental.pallas import tpu as pltpu
from jax.sharding import PartitionSpec as P

softmax_scale = 192.0 ** (-0.5)
vmem_bytes = 60 * 1024 * 1024
small_bytes = 16 * 1024 * 1024
chunks = 2
pieces = 2


def nt_dot(a, b):
    return lax.dot_general(a, b, (((1,), (1,)), ((), ())), preferred_element_type=jnp.float32)


def nn_dot(a, b):
    return lax.dot_general(a, b, (((1,), (0,)), ((), ())), preferred_element_type=jnp.float32)


def beside_heads(ref, heads, width):
    return jnp.concatenate([ref[:, h * width : (h + 1) * width] for h in heads], axis=1)


def on_diagonal(ref, heads, width):
    blocks = [ref[:, h * width : (h + 1) * width] for h in heads]
    zero = jnp.zeros_like(blocks[0])
    return jnp.concatenate(
        [
            jnp.concatenate([block if i == j else zero for j in range(len(blocks))], axis=1)
            for i, block in enumerate(blocks)
        ],
        axis=0,
    )


def pairs_of(unit, per_unit):
    heads = list(range(unit * per_unit, (unit + 1) * per_unit))
    return [heads[i : i + 2] for i in range(0, per_unit, 2)]


def wide_rows(q_ref, heads, feat, width):
    parts = []
    for head in heads:
        if head * feat % 128 == 0:
            parts.append(q_ref[:, head * feat : head * feat + width])
        else:
            end = (head + 1) * feat
            wide = q_ref[:, end - width : end]
            parts.append(jnp.concatenate([wide[:, width - feat :], wide[:, : width - feat]], axis=1))
    return jnp.concatenate(parts, axis=0)


def forward_kernel(
    place_ref, docs_ref, *rest, units, per_unit, rows, feat, lat, vdim, base, own_rows, first, key_rows,
):
    if first:
        (lat0_ref, lat1_ref, lat2_ref, q_ref, g_ref, lse_ref, p_ref, keep_ref, send_ref, ct_ref, c_ref, bias_ref) = rest
    else:
        (ct_ref, c_ref, q_ref, g_ref, lse_ref, _, p_ref, part_ref, bias_ref) = rest
    window, width = c_ref.shape
    far = window - key_rows
    place = place_ref[0]

    @pl.when(pl.program_id(0) == 0)
    def _():
        query_pos = place * key_rows + (key_rows - rows) + lax.broadcasted_iota(jnp.int32, (8, rows), 1)
        start = jnp.zeros((8, rows), jnp.int32)
        for i in range(docs_ref.shape[0]):
            entry = docs_ref[i]
            start = jnp.where(entry <= query_pos, jnp.maximum(start, entry), start)
        key_pos = place * key_rows - far + lax.broadcasted_iota(jnp.int32, (window, rows), 0)
        allowed = (key_pos >= start[:1]) & (key_pos <= query_pos[:1])
        bias_ref[...] = jnp.where(allowed, 0.0, -1e30)
        if first:
            ct_ref[:, : far - key_rows] = lat2_ref[...]
            ct_ref[:, far - key_rows : far] = lat1_ref[...]
            ct_ref[:, far:] = lat0_ref[...]
            gap = jnp.zeros((width - feat, window), ct_ref.dtype)
            c_ref[...] = jnp.concatenate([ct_ref[...], gap], axis=0).T

    bias = bias_ref[...]
    core = place % 2
    span = per_unit * rows
    groups = [pairs_of(unit, per_unit) for unit in range(units)]
    scores = [nt_dot(c_ref[...], wide_rows(q_ref, sum(pairs, []), feat, width)) for pairs in groups]
    for unit, pairs in enumerate(groups):
        for k, head in enumerate(sum(pairs, [])):
            index = (pl.program_id(0) + base) * (per_unit * units) + head
            shift = lse_ref[pl.ds(index, 1), :]
            column = unit * span + k * rows
            p_ref[:, column : column + rows] = jnp.exp(
                scores[unit][:, k * rows : (k + 1) * rows] * softmax_scale + (bias - shift)
            ).astype(jnp.bfloat16)
    olats = [
        nn_dot(ct_ref[:lat, :], p_ref[:, unit * span : (unit + 1) * span]).astype(jnp.bfloat16)
        for unit in range(units)
    ]
    for unit, pairs in enumerate(groups):
        for i, pair in enumerate(pairs):
            part = nn_dot(
                olats[unit][:, 2 * i * rows : 2 * (i + 1) * rows], on_diagonal(g_ref, pair, vdim)
            )
            lanes = slice(pair[0] * vdim, (pair[0] + 2) * vdim)
            if not first:
                part_ref[:, lanes] = part.astype(part_ref.dtype)
                continue
            part = part.reshape(lat // (2 * own_rows), 2, own_rows, 2 * vdim)
            low, high = part[:, 0], part[:, 1]
            keep_ref[:, lanes] = (
                jnp.where(core == 0, low, high).reshape(lat // 2, 2 * vdim).astype(keep_ref.dtype)
            )
            send_ref[:, lanes] = (
                jnp.where(core == 0, high, low).reshape(lat // 2, 2 * vdim).astype(send_ref.dtype)
            )


def backward_kernel(
    c_ref, q_ref, g_ref, o_ref, w_ref, p_ref, *rest,
    units, per_unit, rows, feat, lat, vdim, steps, first, last, ties, key_rows,
):
    rest = list(rest)
    acc_in = None if first else rest.pop(0)
    if not first:
        rest.pop(0)
    rest = rest[ties:]
    ds_ref = rest.pop(0)
    if last:
        near_ref, far1_ref, far2_ref, acc = rest
    else:
        acc_out, acc = rest
    span = per_unit * rows

    @pl.when(pl.program_id(0) == 0)
    def _():
        acc[...] = jnp.zeros_like(acc) if first else acc_in[...]

    groups = [pairs_of(unit, per_unit) for unit in range(units)]
    glats = [
        jnp.concatenate(
            [
                nt_dot(on_diagonal(g_ref, pair, vdim), beside_heads(w_ref, pair, vdim)).astype(jnp.bfloat16)
                for pair in pairs
            ],
            axis=0,
        )
        for pairs in groups
    ]
    gprobs = [nt_dot(c_ref[:, :lat], glat) for glat in glats]
    for unit, pairs in enumerate(groups):
        for k, head in enumerate(sum(pairs, [])):
            lanes = slice(head * vdim, (head + 1) * vdim)
            product = g_ref[:, lanes].astype(jnp.float32) * o_ref[:, lanes].astype(jnp.float32)
            delta = jnp.sum(product.T, axis=0, keepdims=True)
            own = slice(unit * span + k * rows, unit * span + (k + 1) * rows)
            ds_ref[:, own] = (
                p_ref[:, own].astype(jnp.float32)
                * ((gprobs[unit][:, k * rows : (k + 1) * rows] - delta) * softmax_scale)
            ).astype(jnp.bfloat16)
    queries = [wide_rows(q_ref, sum(pairs, []), feat, acc.shape[1]) for pairs in groups]
    acc[:, :lat] += nn_dot(
        jnp.concatenate([ds_ref[...], p_ref[...]], axis=1),
        jnp.concatenate([query[:, :lat] for query in queries] + glats, axis=0),
    )
    acc[:, lat:] += nn_dot(ds_ref[...], jnp.concatenate([query[:, lat:] for query in queries], axis=0))

    @pl.when(pl.program_id(0) == steps - 1)
    def _():
        if last:
            far2 = far2_ref.shape[1]
            total = acc[...].T[:feat]
            far2_ref[...] = total[:, :far2].astype(far2_ref.dtype)
            far1_ref[...] = total[:, far2 : far2 + key_rows].astype(far1_ref.dtype)
            near_ref[...] = total[:, far2 + key_rows :]
        else:
            acc_out[...] = acc[...]


def query_kernel(ct_ref, ds_ref, *rest, pairs, rows, feat):
    gq_ref, token_ref = rest[-2:]
    token_ref[...] = jnp.zeros_like(token_ref)
    turned = nn_dot(ct_ref[...], ds_ref[...]).astype(jnp.bfloat16)
    for i in range(pairs):
        both = jnp.concatenate(
            [turned[:, (2 * i + j) * rows : (2 * i + j + 1) * rows] for j in range(2)], axis=0
        )
        gq_ref[:, 2 * i * feat : 2 * (i + 1) * feat] = both.T


def passed_along(value, axis, steps):
    count = lax.axis_size(axis)
    first, last = (max(0, -steps), min(count, count - steps))
    return lax.ppermute(value, axis, [(source, source + steps) for source in range(first, last)])


def swapped(value, axis, bit):
    count = lax.axis_size(axis)
    return lax.ppermute(value, axis, [(source, source ^ bit) for source in range(count)])


def params():
    return pltpu.CompilerParams(dimension_semantics=("arbitrary",), vmem_limit_bytes=vmem_bytes)


def cost(flops, moved):
    return pl.CostEstimate(flops=int(flops / 8), bytes_accessed=int(moved), transcendentals=0)


def bit_of(place, bit):
    return (place >> bit) & 1


def fetched_sum(place, terms, bits, opened, sent, buffers, sems):
    copies = []
    for i, (term, held) in enumerate(zip(terms, bits)):
        where = []
        for bit in held:
            if bit == sent:
                where.append(1 - bit_of(place, bit))
            elif bit in opened:
                where.append(slice(None))
            else:
                where.append(bit_of(place, bit))
        source = term.at[tuple(where)] if where else term
        copies.append(pltpu.make_async_copy(source, buffers.at[i], sems.at[i]))
    for copy in copies:
        copy.start()
    for copy in copies:
        copy.wait()
    return sum(buffers[i].astype(jnp.float32) for i in range(len(copies)))


def halving_kernel(place_ref, *refs, bits, opened, sent):
    count = len(bits)
    out_ref, buffers, sems = refs[count:]
    out_ref[...] = fetched_sum(
        place_ref[0], refs[:count], bits, opened, sent, buffers, sems
    ).astype(out_ref.dtype)


def final_kernel(place_ref, done_ref, hold_ref, got_ref, *refs, bits):
    count = len(bits)
    out_ref, lat_ref, buffers, sems = refs[count:]
    cols = done_ref.shape[1]
    out_ref[:, :cols] = fetched_sum(place_ref[0], refs[:count], bits, (), None, buffers, sems)
    out_ref[:, cols:] = done_ref[...].astype(jnp.float32)
    lat_ref[...] = hold_ref[...] + got_ref[...].astype(jnp.float32)


def latent_kernel(side_ref, near_ref, got1_ref, got2_ref, _, send_ref, hold_ref):
    low = near_ref[...] + got1_ref[...].astype(jnp.float32)
    part = send_ref.shape[1]
    spare = near_ref.shape[1] - got2_ref.shape[1]
    whole = jnp.concatenate([low[:, :spare], low[:, spare:] + got2_ref[...].astype(jnp.float32)], axis=1)
    first, second = whole[:, :part], whole[:, part:]
    lower = side_ref[0] == 0
    send_ref[...] = jnp.where(lower, second, first).astype(send_ref.dtype)
    hold_ref[...] = jnp.where(lower, first, second)


class Halving:
    def __init__(self, terms, bits, place, axis):
        self.opened = sorted(bits, reverse=True)
        self.terms, self.bits = list(terms), [tuple(self.opened) for _ in terms]
        self.order, self.place, self.axis = list(bits), place, axis

    def step(self):
        bit = self.order.pop(0)
        shape = (2,) * (len(self.opened) - 1) + self.terms[0].shape[-2:]
        count = len(self.terms)
        sent = pl.pallas_call(
            functools.partial(
                halving_kernel, bits=tuple(self.bits), opened=tuple(self.opened), sent=bit
            ),
            in_specs=[pl.BlockSpec(memory_space=pltpu.SMEM)] + [pl.BlockSpec(memory_space=pl.ANY)] * count,
            out_shape=jax.ShapeDtypeStruct(shape, jnp.bfloat16),
            scratch_shapes=[pltpu.VMEM((count, *shape), jnp.bfloat16), pltpu.SemaphoreType.DMA((count,))],
            compiler_params=pltpu.CompilerParams(vmem_limit_bytes=small_bytes),
            cost_estimate=cost(1e6, 2e6),
            name="halving",
        )(self.place, *self.terms)
        self.opened.remove(bit)
        flat = sent.reshape((-1, shape[-1]))
        self.terms.append(swapped(flat, self.axis, 1 << bit).reshape(shape))
        self.bits.append(tuple(self.opened))
        return sent


def on_device(queries, latents, up_value, grad_out, out_saved, log_sums, doc_starts):
    rows = queries.shape[0]
    key_rows, feat = latents.shape
    lat = up_value.shape[0]
    heads = log_sums.shape[1]
    vdim = grad_out.shape[1] // heads
    ctx = lax.axis_size("ctx")
    own_rows = lat // ctx
    window = 2 * key_rows + rows
    far = window - key_rows
    width = -(-feat // 128) * 128
    unit = max(2, min(4, heads // pieces))

    place = lax.axis_index("ctx").astype(jnp.int32)
    turned = latents.T
    prev1 = passed_along(turned, "ctx", 1)
    prev2 = passed_along(turned[:, key_rows - (far - key_rows) :], "ctx", 2)
    sums_turned = log_sums.T

    def whole(*shape):
        return pl.BlockSpec(shape, lambda i: (0,) * len(shape))

    smem = pl.BlockSpec(memory_space=pltpu.SMEM)
    untouched = pl.BlockSpec(memory_space=pl.ANY)
    scalar = place.reshape(1)

    probs = None
    chunk_heads = heads // chunks
    units = max(1, min(2, chunk_heads // unit))
    group = units * unit
    steps = chunk_heads // group
    for chunk in range(chunks):
        base = chunk * steps
        lanes = lambda i, base=base: (0, i + base)
        first = chunk == 0
        in_specs = [smem, smem]
        operands = [scalar, doc_starts]
        if first:
            in_specs += [whole(feat, key_rows), whole(feat, key_rows), whole(feat, far - key_rows)]
            operands += [turned, prev1, prev2]
        else:
            in_specs += [whole(feat, window), whole(window, width)]
            operands += [keys_turned, keys]
        in_specs += [
            pl.BlockSpec((rows, group * feat), lanes),
            pl.BlockSpec((rows, group * vdim), lanes),
            whole(heads, rows),
        ]
        operands += [queries, grad_out, sums_turned]
        halves = 2 if first else 1
        out_specs = [pl.BlockSpec((window, group * rows), lanes)]
        out_specs += [pl.BlockSpec((lat // halves, group * vdim), lambda i: (0, i))] * halves
        out_shape = [jax.ShapeDtypeStruct((window, heads * rows), jnp.bfloat16)]
        out_shape += [jax.ShapeDtypeStruct((lat // halves, chunk_heads * vdim), jnp.bfloat16)] * halves
        aliases = {}
        if first:
            out_specs += [whole(feat, window), whole(window, width)]
            out_shape += [
                jax.ShapeDtypeStruct((feat, window), jnp.bfloat16),
                jax.ShapeDtypeStruct((window, width), jnp.bfloat16),
            ]
        else:
            aliases = {len(operands): 0}
            in_specs.append(untouched)
            operands.append(probs)
        out = pl.pallas_call(
            functools.partial(
                forward_kernel, units=units, per_unit=unit, rows=rows, feat=feat, lat=lat, vdim=vdim,
                base=base, own_rows=own_rows, first=first, key_rows=key_rows,
            ),
            grid=(steps,),
            in_specs=in_specs,
            out_specs=out_specs,
            out_shape=out_shape,
            scratch_shapes=[pltpu.VMEM((window, rows), jnp.float32)],
            input_output_aliases=aliases,
            compiler_params=params(),
            cost_estimate=cost(chunk_heads * rows * 2 * window * (width + lat) * 2, 1e6),
            name="forward",
        )(*operands)
        if first:
            probs, keep, send, keys_turned, keys = out
        else:
            probs, part = out
            scattered = lax.psum_scatter(part, "ctx", scatter_dimension=0, tiled=True)

    upper = list(range(1, ctx.bit_length() - 1))
    shape = (2,) * len(upper) + (own_rows, chunk_heads * vdim)
    got = swapped(send, "ctx", 1)
    halving = Halving([keep.reshape(shape), got.reshape(shape)], upper, scalar, "ctx")

    piece_heads = heads // pieces
    units = max(1, min(2, piece_heads // unit))
    group = units * unit
    steps = piece_heads // group
    acc = dscores = None
    for piece in range(pieces):
        ties = []
        if halving.order:
            ties.append(halving.step())
        first, last = piece == 0, piece == pieces - 1
        base = piece * steps
        lanes = lambda i, base=base: (0, i + base)
        in_specs = [
            whole(window, width),
            pl.BlockSpec((rows, group * feat), lanes),
            pl.BlockSpec((rows, group * vdim), lanes),
            pl.BlockSpec((rows, group * vdim), lanes),
            pl.BlockSpec((lat, group * vdim), lanes),
            pl.BlockSpec((window, group * rows), lanes),
        ]
        operands = [keys, queries, grad_out, out_saved, up_value, probs]
        aliases = {}
        if not first:
            in_specs.append(whole(window, width))
            operands.append(acc)
            aliases[len(operands)] = 0
            in_specs.append(untouched)
            operands.append(dscores)
        in_specs += [untouched] * len(ties)
        operands += ties
        out_specs = [pl.BlockSpec((window, group * rows), lanes)]
        out_shape = [jax.ShapeDtypeStruct((window, heads * rows), jnp.bfloat16)]
        if last:
            out_specs += [whole(feat, key_rows), whole(feat, key_rows), whole(feat, far - key_rows)]
            out_shape += [
                jax.ShapeDtypeStruct((feat, key_rows), jnp.float32),
                jax.ShapeDtypeStruct((feat, key_rows), jnp.bfloat16),
                jax.ShapeDtypeStruct((feat, far - key_rows), jnp.bfloat16),
            ]
        else:
            out_specs.append(whole(window, width))
            out_shape.append(jax.ShapeDtypeStruct((window, width), jnp.float32))
        out = pl.pallas_call(
            functools.partial(
                backward_kernel, units=units, per_unit=unit, rows=rows, feat=feat, lat=lat, vdim=vdim,
                steps=steps, first=first, last=last, ties=len(ties), key_rows=key_rows,
            ),
            grid=(steps,),
            in_specs=in_specs,
            out_specs=out_specs,
            out_shape=out_shape,
            scratch_shapes=[pltpu.VMEM((window, width), jnp.float32)],
            input_output_aliases=aliases,
            compiler_params=params(),
            cost_estimate=cost(piece_heads * rows * 2 * window * (width + 2 * lat) * 2, 1e6),
            name="backward",
        )(*operands)
        dscores, *rest = out
        if last:
            near, far1, far2 = rest
        else:
            (acc,) = rest

    def query_gradient(piece, so_far, ties):
        base = piece * steps
        lanes = lambda i: (0, i + base)
        extra = ([] if so_far is None else [so_far]) + ties
        return pl.pallas_call(
            functools.partial(query_kernel, pairs=group // 2, rows=rows, feat=feat),
            grid=(steps,),
            in_specs=[whole(feat, window), pl.BlockSpec((window, group * rows), lanes)] + [untouched] * len(extra),
            out_specs=[pl.BlockSpec((rows, group * feat), lanes), whole(8, 128)],
            out_shape=[
                jax.ShapeDtypeStruct(queries.shape, jnp.bfloat16),
                jax.ShapeDtypeStruct((8, 128), jnp.float32),
            ],
            input_output_aliases={} if so_far is None else {2: 0},
            compiler_params=params(),
            cost_estimate=cost(piece_heads * rows * 2 * window * width * 3, 1e6),
            name="query_gradient",
        )(keys_turned, dscores, *extra)

    got1 = passed_along(far1, "ctx", -1)
    got2 = passed_along(far2, "ctx", -2)
    ties = [halving.step()] if halving.order else []
    grad_queries, token = query_gradient(0, None, ties)
    position = lax.axis_index("head").astype(jnp.int32)
    bit = lax.axis_size("head") // 2
    part = key_rows // 2
    send, hold = pl.pallas_call(
        latent_kernel,
        in_specs=[smem] + [pl.BlockSpec(memory_space=pltpu.VMEM)] * 3 + [untouched],
        out_shape=[
            jax.ShapeDtypeStruct((feat, part), jnp.bfloat16),
            jax.ShapeDtypeStruct((feat, part), jnp.float32),
        ],
        compiler_params=pltpu.CompilerParams(vmem_limit_bytes=small_bytes),
        cost_estimate=cost(1e6, 2e6),
        name="latent",
    )((position // bit % 2).reshape(1), near, got1, got2, token)
    got = swapped(send, "head", bit)
    ties = [send]
    if halving.order:
        ties.append(halving.step())
    grad_queries, _ = query_gradient(1, grad_queries, ties)
    while halving.order:
        halving.step()
    while bit > 1:
        total = hold + got.astype(jnp.float32)
        bit //= 2
        part //= 2
        mine = (position // bit) % 2
        send = lax.dynamic_slice_in_dim(total, (1 - mine) * part, part, 1).astype(jnp.bfloat16)
        hold = lax.dynamic_slice_in_dim(total, mine * part, part, 1)
        got = swapped(send, "head", bit)
    count = len(halving.terms)
    cols = chunk_heads * vdim
    vmem = pl.BlockSpec(memory_space=pltpu.VMEM)
    grad_up_value, turned_latents = pl.pallas_call(
        functools.partial(final_kernel, bits=tuple(halving.bits)),
        in_specs=[smem, vmem, vmem, vmem] + [untouched] * count,
        out_shape=[
            jax.ShapeDtypeStruct((own_rows, heads * vdim), jnp.float32),
            jax.ShapeDtypeStruct((feat, part), jnp.float32),
        ],
        scratch_shapes=[pltpu.VMEM((count, own_rows, cols), jnp.bfloat16), pltpu.SemaphoreType.DMA((count,))],
        compiler_params=pltpu.CompilerParams(vmem_limit_bytes=small_bytes),
        cost_estimate=cost(1e6, 2e6),
        name="final",
    )(scalar, scattered, hold, got, *halving.terms)
    return (grad_queries, turned_latents.T, grad_up_value)


def solution(mesh):
    return jax.shard_map(
        on_device,
        mesh=mesh,
        in_specs=(
            P("ctx", "head"),
            P("ctx", None),
            P(None, "head"),
            P("ctx", "head"),
            P("ctx", "head"),
            P("ctx", "head"),
            P(),
        ),
        out_specs=(P("ctx", "head"), P(("ctx", "head"), None), P("ctx", "head")),
        check_vma=False,
    )
```

```python
import functools

import jax
import jax.numpy as jnp
from jax import lax
from jax.experimental import pallas as pl
from jax.experimental.pallas import tpu as pltpu
from jax.sharding import PartitionSpec as P

softmax_scale = 192.0 ** (-0.5)
vmem_bytes = 32 * 1024 * 1024
small_bytes = 16 * 1024 * 1024
chunks = 2
pieces = 2


def nt_dot(a, b):
    return lax.dot_general(a, b, (((1,), (1,)), ((), ())), preferred_element_type=jnp.float32)


def nn_dot(a, b):
    return lax.dot_general(a, b, (((1,), (0,)), ((), ())), preferred_element_type=jnp.float32)


def beside_heads(ref, heads, width):
    return jnp.concatenate([ref[:, h * width : (h + 1) * width] for h in heads], axis=1)


def on_diagonal(ref, heads, width):
    blocks = [ref[:, h * width : (h + 1) * width] for h in heads]
    zero = jnp.zeros_like(blocks[0])
    return jnp.concatenate(
        [
            jnp.concatenate([block if i == j else zero for j in range(len(blocks))], axis=1)
            for i, block in enumerate(blocks)
        ],
        axis=0,
    )


def pairs_of(unit, per_unit):
    heads = list(range(unit * per_unit, (unit + 1) * per_unit))
    return [heads[i : i + 2] for i in range(0, per_unit, 2)]


def wide_rows(q_ref, heads, feat, width):
    parts = []
    for head in heads:
        if head * feat % 128 == 0:
            parts.append(q_ref[:, head * feat : head * feat + width])
        else:
            end = (head + 1) * feat
            wide = q_ref[:, end - width : end]
            parts.append(jnp.concatenate([wide[:, width - feat :], wide[:, : width - feat]], axis=1))
    return jnp.concatenate(parts, axis=0)


def forward_kernel(
    place_ref, docs_ref, *rest, units, per_unit, rows, feat, lat, vdim, base, own_rows, first, key_rows,
):
    if first:
        (lat0_ref, lat1_ref, lat2_ref, q_ref, g_ref, lse_ref, p_ref, keep_ref, send_ref, ct_ref, c_ref, bias_ref) = rest
    else:
        (ct_ref, c_ref, q_ref, g_ref, lse_ref, _, p_ref, keep_ref, send_ref, bias_ref) = rest
    window, width = c_ref.shape
    far = window - key_rows
    place = place_ref[0]

    @pl.when(pl.program_id(0) == 0)
    def _():
        query_pos = place * key_rows + (key_rows - rows) + lax.broadcasted_iota(jnp.int32, (8, rows), 1)
        start = jnp.zeros((8, rows), jnp.int32)
        for i in range(docs_ref.shape[0]):
            entry = docs_ref[i]
            start = jnp.where(entry <= query_pos, jnp.maximum(start, entry), start)
        key_pos = place * key_rows - far + lax.broadcasted_iota(jnp.int32, (window, rows), 0)
        allowed = (key_pos >= start[:1]) & (key_pos <= query_pos[:1])
        bias_ref[...] = jnp.where(allowed, 0.0, -1e30)
        if first:
            ct_ref[:, : far - key_rows] = lat2_ref[...]
            ct_ref[:, far - key_rows : far] = lat1_ref[...]
            ct_ref[:, far:] = lat0_ref[...]
            gap = jnp.zeros((width - feat, window), ct_ref.dtype)
            c_ref[...] = jnp.concatenate([ct_ref[...], gap], axis=0).T

    bias = bias_ref[...]
    core = place % 2
    span = per_unit * rows
    groups = [pairs_of(unit, per_unit) for unit in range(units)]
    scores = [nt_dot(c_ref[...], wide_rows(q_ref, sum(pairs, []), feat, width)) for pairs in groups]
    for unit, pairs in enumerate(groups):
        for k, head in enumerate(sum(pairs, [])):
            index = (pl.program_id(0) + base) * (per_unit * units) + head
            shift = lse_ref[pl.ds(index, 1), :]
            column = unit * span + k * rows
            p_ref[:, column : column + rows] = jnp.exp(
                scores[unit][:, k * rows : (k + 1) * rows] * softmax_scale + (bias - shift)
            ).astype(jnp.bfloat16)
    olats = [
        nn_dot(ct_ref[:lat, :], p_ref[:, unit * span : (unit + 1) * span]).astype(jnp.bfloat16)
        for unit in range(units)
    ]
    for unit, pairs in enumerate(groups):
        for i, pair in enumerate(pairs):
            part = nn_dot(
                olats[unit][:, 2 * i * rows : 2 * (i + 1) * rows], on_diagonal(g_ref, pair, vdim)
            )
            lanes = slice(pair[0] * vdim, (pair[0] + 2) * vdim)
            part = part.reshape(lat // (2 * own_rows), 2, own_rows, 2 * vdim)
            low, high = part[:, 0], part[:, 1]
            keep_ref[:, lanes] = (
                jnp.where(core == 0, low, high).reshape(lat // 2, 2 * vdim).astype(keep_ref.dtype)
            )
            send_ref[:, lanes] = (
                jnp.where(core == 0, high, low).reshape(lat // 2, 2 * vdim).astype(send_ref.dtype)
            )


def backward_kernel(
    c_ref, q_ref, g_ref, o_ref, w_ref, p_ref, *rest,
    units, per_unit, rows, feat, lat, vdim, steps, first, last, ties, key_rows,
):
    rest = list(rest)
    acc_in = None if first else rest.pop(0)
    if not first:
        rest.pop(0)
    rest = rest[ties:]
    ds_ref = rest.pop(0)
    if last:
        near_ref, far1_ref, far2_ref, acc = rest
    else:
        acc_out, acc = rest
    span = per_unit * rows

    @pl.when(pl.program_id(0) == 0)
    def _():
        acc[...] = jnp.zeros_like(acc) if first else acc_in[...]

    groups = [pairs_of(unit, per_unit) for unit in range(units)]
    glats = [
        jnp.concatenate(
            [
                nt_dot(on_diagonal(g_ref, pair, vdim), beside_heads(w_ref, pair, vdim)).astype(jnp.bfloat16)
                for pair in pairs
            ],
            axis=0,
        )
        for pairs in groups
    ]
    gprobs = [nt_dot(c_ref[:, :lat], glat) for glat in glats]
    for unit, pairs in enumerate(groups):
        for k, head in enumerate(sum(pairs, [])):
            lanes = slice(head * vdim, (head + 1) * vdim)
            product = g_ref[:, lanes].astype(jnp.float32) * o_ref[:, lanes].astype(jnp.float32)
            delta = jnp.sum(product.T, axis=0, keepdims=True)
            own = slice(unit * span + k * rows, unit * span + (k + 1) * rows)
            ds_ref[:, own] = (
                p_ref[:, own].astype(jnp.float32)
                * ((gprobs[unit][:, k * rows : (k + 1) * rows] - delta) * softmax_scale)
            ).astype(jnp.bfloat16)
    queries = [wide_rows(q_ref, sum(pairs, []), feat, acc.shape[1]) for pairs in groups]
    acc[:, :lat] += nn_dot(
        jnp.concatenate([ds_ref[...], p_ref[...]], axis=1),
        jnp.concatenate([query[:, :lat] for query in queries] + glats, axis=0),
    )
    acc[:, lat:] += nn_dot(ds_ref[...], jnp.concatenate([query[:, lat:] for query in queries], axis=0))

    @pl.when(pl.program_id(0) == steps - 1)
    def _():
        if last:
            far2 = far2_ref.shape[1]
            total = acc[...].T[:feat]
            far2_ref[...] = total[:, :far2].astype(far2_ref.dtype)
            far1_ref[...] = total[:, far2 : far2 + key_rows].astype(far1_ref.dtype)
            near_ref[...] = total[:, far2 + key_rows :]
        else:
            acc_out[...] = acc[...]


def query_kernel(ct_ref, ds_ref, *rest, pairs, rows, feat):
    gq_ref, token_ref = rest[-2:]
    token_ref[...] = jnp.zeros_like(token_ref)
    turned = nn_dot(ct_ref[...], ds_ref[...]).astype(jnp.bfloat16)
    for i in range(pairs):
        both = jnp.concatenate(
            [turned[:, (2 * i + j) * rows : (2 * i + j + 1) * rows] for j in range(2)], axis=0
        )
        gq_ref[:, 2 * i * feat : 2 * (i + 1) * feat] = both.T


def passed_along(value, axis, steps):
    count = lax.axis_size(axis)
    first, last = (max(0, -steps), min(count, count - steps))
    return lax.ppermute(value, axis, [(source, source + steps) for source in range(first, last)])


def swapped(value, axis, bit):
    count = lax.axis_size(axis)
    return lax.ppermute(value, axis, [(source, source ^ bit) for source in range(count)])


def params():
    return pltpu.CompilerParams(dimension_semantics=("arbitrary",), vmem_limit_bytes=vmem_bytes)


def cost(flops, moved):
    return pl.CostEstimate(flops=int(flops / 8), bytes_accessed=int(moved), transcendentals=0)


def bit_of(place, bit):
    return (place >> bit) & 1


def summed(refs):
    return sum(ref[...].astype(jnp.float32) for ref in refs)


def halving_kernel(place_ref, *refs):
    out_ref = refs[-1]
    out_ref[...] = summed(refs[:-1]).astype(out_ref.dtype)


def final_kernel(place_ref, hold_ref, got_ref, *refs, counts):
    out_ref, lat_ref = refs[-2:]
    lat_ref[...] = hold_ref[...] + got_ref[...].astype(jnp.float32)
    cols = refs[0].shape[-1]
    start = 0
    for i, count in enumerate(counts):
        out_ref[:, i * cols : (i + 1) * cols] = summed(refs[start : start + count])
        start += count


def latent_kernel(side_ref, near_ref, got1_ref, got2_ref, _, send_ref, hold_ref):
    low = near_ref[...] + got1_ref[...].astype(jnp.float32)
    part = send_ref.shape[1]
    spare = near_ref.shape[1] - got2_ref.shape[1]
    whole = jnp.concatenate([low[:, :spare], low[:, spare:] + got2_ref[...].astype(jnp.float32)], axis=1)
    first, second = whole[:, :part], whole[:, part:]
    lower = side_ref[0] == 0
    send_ref[...] = jnp.where(lower, second, first).astype(send_ref.dtype)
    hold_ref[...] = jnp.where(lower, first, second)


class Halving:
    def __init__(self, terms, bits, place, axis):
        self.opened = sorted(bits, reverse=True)
        self.terms, self.bits = list(terms), [tuple(self.opened) for _ in terms]
        self.order, self.place, self.axis = list(bits), place, axis

    def spec(self, term, held, sent):
        shape, index = [], []
        for bit in held:
            if bit in self.opened and bit != sent and sent is not None:
                shape.append(2)
                index.append(lambda place: 0)
            else:
                shape.append(None)
                index.append(
                    (lambda place, bit=bit: 1 - bit_of(place, bit))
                    if bit == sent
                    else (lambda place, bit=bit: bit_of(place, bit))
                )
        shape += term.shape[-2:]
        return pl.BlockSpec(tuple(shape), lambda i, place: (*(f(place[0]) for f in index), 0, 0))

    def specs(self, sent):
        return [self.spec(term, held, sent) for term, held in zip(self.terms, self.bits)]

    def step(self):
        bit = self.order.pop(0)
        shape = (2,) * (len(self.opened) - 1) + self.terms[0].shape[-2:]
        sent = pl.pallas_call(
            halving_kernel,
            grid_spec=pltpu.PrefetchScalarGridSpec(
                num_scalar_prefetch=1,
                grid=(1,),
                in_specs=self.specs(bit),
                out_specs=pl.BlockSpec(shape, lambda i, place: (0,) * len(shape)),
            ),
            out_shape=jax.ShapeDtypeStruct(shape, jnp.bfloat16),
            compiler_params=pltpu.CompilerParams(vmem_limit_bytes=small_bytes),
            cost_estimate=cost(1e6, 2e6),
            name="halving",
        )(self.place, *self.terms)
        self.opened.remove(bit)
        flat = sent.reshape((-1, shape[-1]))
        self.terms.append(swapped(flat, self.axis, 1 << bit).reshape(shape))
        self.bits.append(tuple(self.opened))
        return sent


def on_device(queries, latents, up_value, grad_out, out_saved, log_sums, doc_starts):
    rows = queries.shape[0]
    key_rows, feat = latents.shape
    lat = up_value.shape[0]
    heads = log_sums.shape[1]
    vdim = grad_out.shape[1] // heads
    ctx = lax.axis_size("ctx")
    own_rows = lat // ctx
    window = 2 * key_rows + rows
    far = window - key_rows
    width = -(-feat // 128) * 128
    unit = max(2, min(4, heads // pieces))

    place = lax.axis_index("ctx").astype(jnp.int32)
    turned = latents.T
    prev1 = passed_along(turned, "ctx", 1)
    prev2 = passed_along(turned[:, key_rows - (far - key_rows) :], "ctx", 2)
    sums_turned = log_sums.T

    def whole(*shape):
        return pl.BlockSpec(shape, lambda i: (0,) * len(shape))

    smem = pl.BlockSpec(memory_space=pltpu.SMEM)
    untouched = pl.BlockSpec(memory_space=pl.ANY)
    scalar = place.reshape(1)

    probs = None
    partials = []
    chunk_heads = heads // chunks
    units = max(1, min(2, chunk_heads // unit))
    group = units * unit
    steps = chunk_heads // group
    for chunk in range(chunks):
        base = chunk * steps
        lanes = lambda i, base=base: (0, i + base)
        first = chunk == 0
        in_specs = [smem, smem]
        operands = [scalar, doc_starts]
        if first:
            in_specs += [whole(feat, key_rows), whole(feat, key_rows), whole(feat, far - key_rows)]
            operands += [turned, prev1, prev2]
        else:
            in_specs += [whole(feat, window), whole(window, width)]
            operands += [keys_turned, keys]
        in_specs += [
            pl.BlockSpec((rows, group * feat), lanes),
            pl.BlockSpec((rows, group * vdim), lanes),
            whole(heads, rows),
        ]
        operands += [queries, grad_out, sums_turned]
        halves = 2
        out_specs = [pl.BlockSpec((window, group * rows), lanes)]
        out_specs += [pl.BlockSpec((lat // halves, group * vdim), lambda i: (0, i))] * halves
        out_shape = [jax.ShapeDtypeStruct((window, heads * rows), jnp.bfloat16)]
        out_shape += [jax.ShapeDtypeStruct((lat // halves, chunk_heads * vdim), jnp.bfloat16)] * halves
        aliases = {}
        if first:
            out_specs += [whole(feat, window), whole(window, width)]
            out_shape += [
                jax.ShapeDtypeStruct((feat, window), jnp.bfloat16),
                jax.ShapeDtypeStruct((window, width), jnp.bfloat16),
            ]
        else:
            aliases = {len(operands): 0}
            in_specs.append(untouched)
            operands.append(probs)
        out = pl.pallas_call(
            functools.partial(
                forward_kernel, units=units, per_unit=unit, rows=rows, feat=feat, lat=lat, vdim=vdim,
                base=base, own_rows=own_rows, first=first, key_rows=key_rows,
            ),
            grid=(steps,),
            in_specs=in_specs,
            out_specs=out_specs,
            out_shape=out_shape,
            scratch_shapes=[pltpu.VMEM((window, rows), jnp.float32)],
            input_output_aliases=aliases,
            compiler_params=params(),
            cost_estimate=cost(chunk_heads * rows * 2 * window * (width + lat) * 2, 1e6),
            name="forward",
        )(*operands)
        if first:
            keys_turned, keys = out[3:]
        probs, keep, send = out[:3]
        partials.append((keep, send))

    upper = list(range(1, ctx.bit_length() - 1))
    shape = (2,) * len(upper) + (own_rows, chunk_heads * vdim)
    halvings = []
    for (keep, send), order in zip(partials, (upper[1:] + upper[:1], upper)):
        got = swapped(send, "ctx", 1)
        halvings.append(Halving([keep.reshape(shape), got.reshape(shape)], order, scalar, "ctx"))

    piece_heads = heads // pieces
    units = max(1, min(2, piece_heads // unit))
    group = units * unit
    steps = piece_heads // group
    acc = dscores = None
    for piece in range(pieces):
        ties = [halving.step() for halving in halvings if halving.order]
        first, last = piece == 0, piece == pieces - 1
        base = piece * steps
        lanes = lambda i, base=base: (0, i + base)
        in_specs = [
            whole(window, width),
            pl.BlockSpec((rows, group * feat), lanes),
            pl.BlockSpec((rows, group * vdim), lanes),
            pl.BlockSpec((rows, group * vdim), lanes),
            pl.BlockSpec((lat, group * vdim), lanes),
            pl.BlockSpec((window, group * rows), lanes),
        ]
        operands = [keys, queries, grad_out, out_saved, up_value, probs]
        aliases = {}
        if not first:
            in_specs.append(whole(window, width))
            operands.append(acc)
            aliases[len(operands)] = 0
            in_specs.append(untouched)
            operands.append(dscores)
        in_specs += [untouched] * len(ties)
        operands += ties
        out_specs = [pl.BlockSpec((window, group * rows), lanes)]
        out_shape = [jax.ShapeDtypeStruct((window, heads * rows), jnp.bfloat16)]
        if last:
            out_specs += [whole(feat, key_rows), whole(feat, key_rows), whole(feat, far - key_rows)]
            out_shape += [
                jax.ShapeDtypeStruct((feat, key_rows), jnp.float32),
                jax.ShapeDtypeStruct((feat, key_rows), jnp.bfloat16),
                jax.ShapeDtypeStruct((feat, far - key_rows), jnp.bfloat16),
            ]
        else:
            out_specs.append(whole(window, width))
            out_shape.append(jax.ShapeDtypeStruct((window, width), jnp.float32))
        out = pl.pallas_call(
            functools.partial(
                backward_kernel, units=units, per_unit=unit, rows=rows, feat=feat, lat=lat, vdim=vdim,
                steps=steps, first=first, last=last, ties=len(ties), key_rows=key_rows,
            ),
            grid=(steps,),
            in_specs=in_specs,
            out_specs=out_specs,
            out_shape=out_shape,
            scratch_shapes=[pltpu.VMEM((window, width), jnp.float32)],
            input_output_aliases=aliases,
            compiler_params=params(),
            cost_estimate=cost(piece_heads * rows * 2 * window * (width + 2 * lat) * 2, 1e6),
            name="backward",
        )(*operands)
        dscores, *rest = out
        if last:
            near, far1, far2 = rest
        else:
            (acc,) = rest

    def query_gradient(piece, so_far, ties):
        base = piece * steps
        lanes = lambda i: (0, i + base)
        extra = ([] if so_far is None else [so_far]) + ties
        return pl.pallas_call(
            functools.partial(query_kernel, pairs=group // 2, rows=rows, feat=feat),
            grid=(steps,),
            in_specs=[whole(feat, window), pl.BlockSpec((window, group * rows), lanes)] + [untouched] * len(extra),
            out_specs=[pl.BlockSpec((rows, group * feat), lanes), whole(8, 128)],
            out_shape=[
                jax.ShapeDtypeStruct(queries.shape, jnp.bfloat16),
                jax.ShapeDtypeStruct((8, 128), jnp.float32),
            ],
            input_output_aliases={} if so_far is None else {2: 0},
            compiler_params=params(),
            cost_estimate=cost(piece_heads * rows * 2 * window * width * 3, 1e6),
            name="query_gradient",
        )(keys_turned, dscores, *extra)

    got1 = passed_along(far1, "ctx", -1)
    got2 = passed_along(far2, "ctx", -2)
    ties = [halving.step() for halving in halvings if halving.order]
    grad_queries, token = query_gradient(0, None, ties)
    position = lax.axis_index("head").astype(jnp.int32)
    bit = lax.axis_size("head") // 2
    part = key_rows // 2
    send, hold = pl.pallas_call(
        latent_kernel,
        in_specs=[smem] + [pl.BlockSpec(memory_space=pltpu.VMEM)] * 3 + [untouched],
        out_shape=[
            jax.ShapeDtypeStruct((feat, part), jnp.bfloat16),
            jax.ShapeDtypeStruct((feat, part), jnp.float32),
        ],
        compiler_params=pltpu.CompilerParams(vmem_limit_bytes=small_bytes),
        cost_estimate=cost(1e6, 2e6),
        name="latent",
    )((position // bit % 2).reshape(1), near, got1, got2, token)
    got = swapped(send, "head", bit)
    ties = [send] + [halving.step() for halving in halvings if halving.order]
    grad_queries, _ = query_gradient(1, grad_queries, ties)
    for halving in halvings:
        while halving.order:
            halving.step()
    while bit > 1:
        total = hold + got.astype(jnp.float32)
        bit //= 2
        part //= 2
        mine = (position // bit) % 2
        send = lax.dynamic_slice_in_dim(total, (1 - mine) * part, part, 1).astype(jnp.bfloat16)
        hold = lax.dynamic_slice_in_dim(total, mine * part, part, 1)
        got = swapped(send, "head", bit)
    one = lambda *shape: pl.BlockSpec(shape, lambda i, place: (0,) * len(shape))
    grad_up_value, turned_latents = pl.pallas_call(
        functools.partial(final_kernel, counts=[len(halving.terms) for halving in halvings]),
        grid_spec=pltpu.PrefetchScalarGridSpec(
            num_scalar_prefetch=1,
            grid=(1,),
            in_specs=[one(feat, part), one(feat, part)] + sum((halving.specs(None) for halving in halvings), []),
            out_specs=[one(own_rows, heads * vdim), one(feat, part)],
        ),
        out_shape=[
            jax.ShapeDtypeStruct((own_rows, heads * vdim), jnp.float32),
            jax.ShapeDtypeStruct((feat, part), jnp.float32),
        ],
        compiler_params=pltpu.CompilerParams(vmem_limit_bytes=small_bytes),
        cost_estimate=cost(1e6, 2e6),
        name="final",
    )(scalar, hold, got, *sum((halving.terms for halving in halvings), []))
    return (grad_queries, turned_latents.T, grad_up_value)


def solution(mesh):
    return jax.shard_map(
        on_device,
        mesh=mesh,
        in_specs=(
            P("ctx", "head"),
            P("ctx", None),
            P(None, "head"),
            P("ctx", "head"),
            P("ctx", "head"),
            P("ctx", "head"),
            P(),
        ),
        out_specs=(P("ctx", "head"), P(("ctx", "head"), None), P("ctx", "head")),
        check_vma=False,
    )
```

```python
import functools

import jax
import jax.numpy as jnp
from jax import lax
from jax.experimental import pallas as pl
from jax.experimental.pallas import tpu as pltpu
from jax.sharding import PartitionSpec as P

softmax_scale = 192.0 ** (-0.5)
vmem_bytes = 32 * 1024 * 1024
prepare_bytes = 54 * 1024 * 1024
small_bytes = 16 * 1024 * 1024
chunks = 2
pieces = 2


def nt_dot(a, b):
    return lax.dot_general(a, b, (((1,), (1,)), ((), ())), preferred_element_type=jnp.float32)


def nn_dot(a, b):
    return lax.dot_general(a, b, (((1,), (0,)), ((), ())), preferred_element_type=jnp.float32)


def beside_heads(ref, heads, width):
    return jnp.concatenate([ref[:, h * width : (h + 1) * width] for h in heads], axis=1)


def on_diagonal(ref, heads, width):
    blocks = [ref[:, h * width : (h + 1) * width] for h in heads]
    zero = jnp.zeros_like(blocks[0])
    return jnp.concatenate(
        [
            jnp.concatenate([block if i == j else zero for j in range(len(blocks))], axis=1)
            for i, block in enumerate(blocks)
        ],
        axis=0,
    )


def pairs_of(unit, per_unit):
    heads = list(range(unit * per_unit, (unit + 1) * per_unit))
    return [heads[i : i + 2] for i in range(0, per_unit, 2)]


def wide_rows(q_ref, heads, feat, width):
    parts = []
    for head in heads:
        if head * feat % 128 == 0:
            parts.append(q_ref[:, head * feat : head * feat + width])
        else:
            end = (head + 1) * feat
            wide = q_ref[:, end - width : end]
            parts.append(jnp.concatenate([wide[:, width - feat :], wide[:, : width - feat]], axis=1))
    return jnp.concatenate(parts, axis=0)


def prepare_kernel(
    place_ref, docs_ref, lat_ref, lse_ref, q_ref, g_ref, o_ref, w_ref,
    own_ref, table_ref, qs_ref, glat_ref, *, units, per_unit, rows, feat, vdim, key_rows,
):
    heads = lse_ref.shape[0]
    window = table_ref.shape[0] - 2 * heads
    width = qs_ref.shape[1]
    span = per_unit * rows

    @pl.when(pl.program_id(0) == 0)
    def _():
        own_ref[...] = lat_ref[...]
        table_ref[window : window + heads, :] = lse_ref[...]
        place = place_ref[0]
        query_pos = place * key_rows + (key_rows - rows) + lax.broadcasted_iota(jnp.int32, (8, rows), 1)
        start = jnp.zeros((8, rows), jnp.int32)
        for i in range(docs_ref.shape[0]):
            entry = docs_ref[i]
            start = jnp.where(entry <= query_pos, jnp.maximum(start, entry), start)
        key_pos = (place + 1) * key_rows - window + lax.broadcasted_iota(jnp.int32, (window, rows), 0)
        allowed = (key_pos >= start[:1]) & (key_pos <= query_pos[:1])
        table_ref[:window, :] = jnp.where(allowed, 0.0, -1e30)

    deltas = []
    for unit in range(units):
        pairs = pairs_of(unit, per_unit)
        qs_ref[unit * span : (unit + 1) * span, :] = wide_rows(q_ref, sum(pairs, []), feat, width)
        for i, pair in enumerate(pairs):
            row = unit * span + 2 * i * rows
            glat_ref[row : row + 2 * rows, :] = nt_dot(
                on_diagonal(g_ref, pair, vdim), beside_heads(w_ref, pair, vdim)
            ).astype(glat_ref.dtype)
            for head in pair:
                lanes = slice(head * vdim, (head + 1) * vdim)
                product = g_ref[:, lanes].astype(jnp.float32) * o_ref[:, lanes].astype(jnp.float32)
                deltas.append(jnp.sum(product.T, axis=0, keepdims=True))
    count = len(deltas)
    row = window + heads + pl.program_id(0) * count
    table_ref[pl.ds(pl.multiple_of(row, count), count), :] = jnp.concatenate(deltas, axis=0)


def forward_kernel(
    place_ref, *rest, units, per_unit, rows, feat, lat, vdim, base, own_rows, first, key_rows,
):
    if first:
        (lat0_ref, lat1_ref, lat2_ref, qs_ref, g_ref, table_ref, p_ref, keep_ref, send_ref, ct_ref, c_ref) = rest
    else:
        (ct_ref, c_ref, qs_ref, g_ref, table_ref, _, p_ref, keep_ref, send_ref) = rest
    window, width = c_ref.shape
    far = window - key_rows
    core = place_ref[0] % 2

    if first:

        @pl.when(pl.program_id(0) == 0)
        def _():
            ct_ref[:, : far - key_rows] = lat2_ref[...]
            ct_ref[:, far - key_rows : far] = lat1_ref[...]
            ct_ref[:, far:] = lat0_ref[...]
            gap = jnp.zeros((width - feat, window), ct_ref.dtype)
            c_ref[...] = jnp.concatenate([ct_ref[...], gap], axis=0).T

    bias = table_ref[:window, :]
    span = per_unit * rows
    scores = [nt_dot(c_ref[...], qs_ref[unit * span : (unit + 1) * span, :]) for unit in range(units)]
    for unit in range(units):
        for k in range(per_unit):
            index = ((pl.program_id(0) + base) * units + unit) * per_unit + k
            shift = table_ref[pl.ds(window + index, 1), :]
            column = unit * span + k * rows
            p_ref[:, column : column + rows] = jnp.exp(
                scores[unit][:, k * rows : (k + 1) * rows] * softmax_scale + (bias - shift)
            ).astype(jnp.bfloat16)
    olats = [
        nn_dot(ct_ref[:lat, :], p_ref[:, unit * span : (unit + 1) * span]).astype(jnp.bfloat16)
        for unit in range(units)
    ]
    for unit in range(units):
        for i, pair in enumerate(pairs_of(unit, per_unit)):
            part = nn_dot(
                olats[unit][:, 2 * i * rows : 2 * (i + 1) * rows], on_diagonal(g_ref, pair, vdim)
            )
            lanes = slice(pair[0] * vdim, (pair[0] + 2) * vdim)
            part = part.reshape(lat // (2 * own_rows), 2, own_rows, 2 * vdim)
            low, high = part[:, 0], part[:, 1]
            keep_ref[:, lanes] = (
                jnp.where(core == 0, low, high).reshape(lat // 2, 2 * vdim).astype(keep_ref.dtype)
            )
            send_ref[:, lanes] = (
                jnp.where(core == 0, high, low).reshape(lat // 2, 2 * vdim).astype(send_ref.dtype)
            )


def backward_kernel(
    c_ref, qs_ref, glat_ref, table_ref, p_ref, *rest,
    units, per_unit, rows, feat, lat, steps, base, first, last, ties, key_rows,
):
    rest = list(rest)
    acc_in = None if first else rest.pop(0)
    rest = rest[ties:]
    ds_ref = rest.pop(0)
    if last:
        near_ref, far1_ref, far2_ref, acc = rest
    else:
        acc_out, acc = rest
    span = per_unit * rows

    @pl.when(pl.program_id(0) == 0)
    def _():
        acc[...] = jnp.zeros_like(acc) if first else acc_in[...]

    first_delta = (table_ref.shape[0] + c_ref.shape[0]) // 2
    gprobs = [
        nt_dot(c_ref[:, :lat], glat_ref[unit * span : (unit + 1) * span, :]) for unit in range(units)
    ]
    for unit in range(units):
        for k in range(per_unit):
            index = ((pl.program_id(0) + base) * units + unit) * per_unit + k
            delta = table_ref[pl.ds(first_delta + index, 1), :]
            own = slice(unit * span + k * rows, unit * span + (k + 1) * rows)
            ds_ref[:, own] = (
                p_ref[:, own].astype(jnp.float32)
                * ((gprobs[unit][:, k * rows : (k + 1) * rows] - delta) * softmax_scale)
            ).astype(jnp.bfloat16)
    acc[:, :lat] += nn_dot(
        jnp.concatenate([ds_ref[...], p_ref[...]], axis=1),
        jnp.concatenate([qs_ref[:, :lat], glat_ref[...]], axis=0),
    )
    acc[:, lat:] += nn_dot(ds_ref[...], qs_ref[:, lat:])

    @pl.when(pl.program_id(0) == steps - 1)
    def _():
        if last:
            far2 = far2_ref.shape[1]
            total = acc[...].T[:feat]
            far2_ref[...] = total[:, :far2].astype(far2_ref.dtype)
            far1_ref[...] = total[:, far2 : far2 + key_rows].astype(far1_ref.dtype)
            near_ref[...] = total[:, far2 + key_rows :]
        else:
            acc_out[...] = acc[...]


def query_kernel(ct_ref, ds_ref, *rest, pairs, rows, feat):
    gq_ref, token_ref = rest[-2:]
    token_ref[...] = jnp.zeros_like(token_ref)
    turned = nn_dot(ct_ref[...], ds_ref[...]).astype(jnp.bfloat16)
    for i in range(pairs):
        both = jnp.concatenate(
            [turned[:, (2 * i + j) * rows : (2 * i + j + 1) * rows] for j in range(2)], axis=0
        )
        gq_ref[:, 2 * i * feat : 2 * (i + 1) * feat] = both.T


def passed_along(value, axis, steps):
    count = lax.axis_size(axis)
    first, last = (max(0, -steps), min(count, count - steps))
    return lax.ppermute(value, axis, [(source, source + steps) for source in range(first, last)])


def swapped(value, axis, bit):
    count = lax.axis_size(axis)
    return lax.ppermute(value, axis, [(source, source ^ bit) for source in range(count)])


def params(limit=vmem_bytes):
    return pltpu.CompilerParams(dimension_semantics=("arbitrary",), vmem_limit_bytes=limit)


def cost(flops, moved):
    return pl.CostEstimate(flops=int(flops / 8), bytes_accessed=int(moved), transcendentals=0)


def bit_of(place, bit):
    return (place >> bit) & 1


def halving_kernel(place_ref, hold_ref, got_ref, send_ref, keep_ref, *, dim, bit):
    mine = bit_of(place_ref[0], bit)
    lead = (slice(None),) * dim
    for which, out_ref in ((1 - mine, send_ref), (mine, keep_ref)):
        where = lead + (which,)
        out_ref[...] = (hold_ref[where].astype(jnp.float32) + got_ref[where].astype(jnp.float32)).astype(
            out_ref.dtype
        )


def final_kernel(hold_ref, got_ref, *refs):
    out_ref, lat_ref = refs[-2:]
    lat_ref[...] = hold_ref[...] + got_ref[...].astype(jnp.float32)
    cols = refs[0].shape[-1]
    for i in range(len(refs) // 2 - 1):
        out_ref[:, i * cols : (i + 1) * cols] = refs[2 * i][...] + refs[2 * i + 1][...].astype(jnp.float32)


def latent_kernel(side_ref, near_ref, got1_ref, got2_ref, _, send_ref, hold_ref):
    low = near_ref[...] + got1_ref[...].astype(jnp.float32)
    part = send_ref.shape[1]
    spare = near_ref.shape[1] - got2_ref.shape[1]
    whole = jnp.concatenate([low[:, :spare], low[:, spare:] + got2_ref[...].astype(jnp.float32)], axis=1)
    first, second = whole[:, :part], whole[:, part:]
    lower = side_ref[0] == 0
    send_ref[...] = jnp.where(lower, second, first).astype(send_ref.dtype)
    hold_ref[...] = jnp.where(lower, first, second)


class Halving:
    def __init__(self, hold, got, bits, place, axis):
        self.hold, self.got, self.place, self.axis = hold, got, place, axis
        self.opened, self.order = sorted(bits, reverse=True), list(bits)

    def step(self):
        bit = self.order.pop(0)
        shape = (2,) * (len(self.opened) - 1) + self.hold.shape[-2:]
        vmem = pl.BlockSpec(memory_space=pltpu.VMEM)
        sent, self.hold = pl.pallas_call(
            functools.partial(halving_kernel, dim=self.opened.index(bit), bit=bit),
            in_specs=[pl.BlockSpec(memory_space=pltpu.SMEM), vmem, vmem],
            out_shape=[jax.ShapeDtypeStruct(shape, jnp.bfloat16), jax.ShapeDtypeStruct(shape, jnp.float32)],
            compiler_params=pltpu.CompilerParams(vmem_limit_bytes=small_bytes),
            cost_estimate=cost(1e6, 2e6),
            name="halving",
        )(self.place, self.hold, self.got)
        self.opened.remove(bit)
        self.got = swapped(sent.reshape((-1, shape[-1])), self.axis, 1 << bit).reshape(shape)
        return sent


def on_device(queries, latents, up_value, grad_out, out_saved, log_sums, doc_starts):
    rows = queries.shape[0]
    key_rows, feat = latents.shape
    lat = up_value.shape[0]
    heads = log_sums.shape[1]
    vdim = grad_out.shape[1] // heads
    ctx = lax.axis_size("ctx")
    own_rows = lat // ctx
    window = 2 * key_rows + rows
    far = window - key_rows
    width = -(-feat // 128) * 128
    unit = max(2, min(4, heads // pieces))

    place = lax.axis_index("ctx").astype(jnp.int32)
    turned = latents.T
    prev1 = passed_along(turned, "ctx", 1)
    prev2 = passed_along(turned[:, key_rows - (far - key_rows) :], "ctx", 2)
    sums_turned = log_sums.T

    def whole(*shape):
        return pl.BlockSpec(shape, lambda i: (0,) * len(shape))

    smem = pl.BlockSpec(memory_space=pltpu.SMEM)
    untouched = pl.BlockSpec(memory_space=pl.ANY)
    scalar = place.reshape(1)

    chunk_heads = heads // chunks
    units = max(1, min(2, heads // unit))
    group = units * unit
    lanes = lambda i: (0, i)
    rowed = lambda i: (i, 0)
    own, table, stacked, glat = pl.pallas_call(
        functools.partial(
            prepare_kernel, units=units, per_unit=unit, rows=rows, feat=feat, vdim=vdim, key_rows=key_rows
        ),
        grid=(heads // group,),
        in_specs=[
            smem,
            smem,
            whole(feat, key_rows),
            whole(heads, rows),
            pl.BlockSpec((rows, group * feat), lanes),
            pl.BlockSpec((rows, group * vdim), lanes),
            pl.BlockSpec((rows, group * vdim), lanes),
            pl.BlockSpec((lat, group * vdim), lanes),
        ],
        out_specs=[
            whole(feat, key_rows),
            whole(window + 2 * heads, rows),
            pl.BlockSpec((group * rows, width), rowed),
            pl.BlockSpec((group * rows, lat), rowed),
        ],
        out_shape=[
            jax.ShapeDtypeStruct((feat, key_rows), jnp.bfloat16),
            jax.ShapeDtypeStruct((window + 2 * heads, rows), jnp.float32),
            jax.ShapeDtypeStruct((heads * rows, width), jnp.bfloat16),
            jax.ShapeDtypeStruct((heads * rows, lat), jnp.bfloat16),
        ],
        compiler_params=params(prepare_bytes),
        cost_estimate=cost(heads * rows * 4 * lat * vdim, 20e6),
        name="prepare",
    )(scalar, doc_starts, turned, sums_turned, queries, grad_out, out_saved, up_value)

    probs = None
    partials = []
    units = max(1, min(2, chunk_heads // unit))
    group = units * unit
    steps = chunk_heads // group
    for chunk in range(chunks):
        base = chunk * steps
        lanes = lambda i, base=base: (0, i + base)
        rowed = lambda i, base=base: (i + base, 0)
        first = chunk == 0
        in_specs = [smem]
        operands = [scalar]
        if first:
            in_specs += [whole(feat, key_rows), whole(feat, key_rows), whole(feat, far - key_rows)]
            operands += [own, prev1, prev2]
        else:
            in_specs += [whole(feat, window), whole(window, width)]
            operands += [keys_turned, keys]
        in_specs += [
            pl.BlockSpec((group * rows, width), rowed),
            pl.BlockSpec((rows, group * vdim), lanes),
            whole(window + 2 * heads, rows),
        ]
        operands += [stacked, grad_out, table]
        halves = [pl.BlockSpec((lat // 2, group * vdim), lambda i: (0, i))] * 2
        out_specs = [pl.BlockSpec((window, group * rows), lanes)] + halves
        out_shape = [jax.ShapeDtypeStruct((window, heads * rows), jnp.bfloat16)]
        out_shape += [jax.ShapeDtypeStruct((lat // 2, chunk_heads * vdim), jnp.bfloat16)] * 2
        aliases = {}
        if first:
            out_specs += [whole(feat, window), whole(window, width)]
            out_shape += [
                jax.ShapeDtypeStruct((feat, window), jnp.bfloat16),
                jax.ShapeDtypeStruct((window, width), jnp.bfloat16),
            ]
        else:
            aliases = {len(operands): 0}
            in_specs.append(untouched)
            operands.append(probs)
        out = pl.pallas_call(
            functools.partial(
                forward_kernel, units=units, per_unit=unit, rows=rows, feat=feat, lat=lat, vdim=vdim,
                base=base, own_rows=own_rows, first=first, key_rows=key_rows,
            ),
            grid=(steps,),
            in_specs=in_specs,
            out_specs=out_specs,
            out_shape=out_shape,
            input_output_aliases=aliases,
            compiler_params=params(),
            cost_estimate=cost(chunk_heads * rows * 2 * window * (width + lat) * 2, 1e6),
            name="forward",
        )(*operands)
        if first:
            keys_turned, keys = out[3:]
        probs, keep, send = out[:3]
        partials.append((keep, send))

    upper = list(range(1, ctx.bit_length() - 1))
    shape = (2,) * len(upper) + (own_rows, chunk_heads * vdim)
    halvings = []
    for (keep, send), order in zip(partials, (upper[1:] + upper[:1], upper)):
        got = swapped(send, "ctx", 1)
        halvings.append(Halving(keep.reshape(shape), got.reshape(shape), order, scalar, "ctx"))

    piece_heads = heads // pieces
    units = max(1, min(2, piece_heads // unit))
    group = units * unit
    steps = piece_heads // group
    acc = None
    for piece in range(pieces):
        ties = [halving.step() for halving in halvings if halving.order]
        first, last = piece == 0, piece == pieces - 1
        base = piece * steps
        lanes = lambda i, base=base: (0, i + base)
        rowed = lambda i, base=base: (i + base, 0)
        in_specs = [
            whole(window, width),
            pl.BlockSpec((group * rows, width), rowed),
            pl.BlockSpec((group * rows, lat), rowed),
            whole(window + 2 * heads, rows),
            pl.BlockSpec((window, group * rows), lanes),
        ]
        operands = [keys, stacked, glat, table, probs]
        if not first:
            in_specs.append(whole(window, width))
            operands.append(acc)
        in_specs += [untouched] * len(ties)
        operands += ties
        out_specs = [pl.BlockSpec((window, group * rows), lanes)]
        out_shape = [jax.ShapeDtypeStruct((window, heads * rows), jnp.bfloat16)]
        if last:
            out_specs += [whole(feat, key_rows), whole(feat, key_rows), whole(feat, far - key_rows)]
            out_shape += [
                jax.ShapeDtypeStruct((feat, key_rows), jnp.float32),
                jax.ShapeDtypeStruct((feat, key_rows), jnp.bfloat16),
                jax.ShapeDtypeStruct((feat, far - key_rows), jnp.bfloat16),
            ]
        else:
            out_specs.append(whole(window, width))
            out_shape.append(jax.ShapeDtypeStruct((window, width), jnp.float32))
        probs, *rest = pl.pallas_call(
            functools.partial(
                backward_kernel, units=units, per_unit=unit, rows=rows, feat=feat, lat=lat, base=base,
                steps=steps, first=first, last=last, ties=len(ties), key_rows=key_rows,
            ),
            grid=(steps,),
            in_specs=in_specs,
            out_specs=out_specs,
            out_shape=out_shape,
            scratch_shapes=[pltpu.VMEM((window, width), jnp.float32)],
            input_output_aliases={4: 0},
            compiler_params=params(),
            cost_estimate=cost(piece_heads * rows * 2 * window * (width + 2 * lat) * 2, 1e6),
            name="backward",
        )(*operands)
        if last:
            near, far1, far2 = rest
        else:
            (acc,) = rest
    dscores = probs

    def query_gradient(piece, so_far, ties):
        base = piece * steps
        lanes = lambda i: (0, i + base)
        extra = ([] if so_far is None else [so_far]) + ties
        return pl.pallas_call(
            functools.partial(query_kernel, pairs=group // 2, rows=rows, feat=feat),
            grid=(steps,),
            in_specs=[whole(feat, window), pl.BlockSpec((window, group * rows), lanes)] + [untouched] * len(extra),
            out_specs=[pl.BlockSpec((rows, group * feat), lanes), whole(8, 128)],
            out_shape=[
                jax.ShapeDtypeStruct(queries.shape, jnp.bfloat16),
                jax.ShapeDtypeStruct((8, 128), jnp.float32),
            ],
            input_output_aliases={} if so_far is None else {2: 0},
            compiler_params=params(),
            cost_estimate=cost(piece_heads * rows * 2 * window * width * 3, 1e6),
            name="query_gradient",
        )(keys_turned, dscores, *extra)

    got1 = passed_along(far1, "ctx", -1)
    got2 = passed_along(far2, "ctx", -2)
    ties = [halving.step() for halving in halvings if halving.order]
    grad_queries, token = query_gradient(0, None, ties)
    position = lax.axis_index("head").astype(jnp.int32)
    bit = lax.axis_size("head") // 2
    part = key_rows // 2
    send, hold = pl.pallas_call(
        latent_kernel,
        in_specs=[smem] + [pl.BlockSpec(memory_space=pltpu.VMEM)] * 3 + [untouched],
        out_shape=[
            jax.ShapeDtypeStruct((feat, part), jnp.bfloat16),
            jax.ShapeDtypeStruct((feat, part), jnp.float32),
        ],
        compiler_params=pltpu.CompilerParams(vmem_limit_bytes=small_bytes),
        cost_estimate=cost(1e6, 2e6),
        name="latent",
    )((position // bit % 2).reshape(1), near, got1, got2, token)
    got = swapped(send, "head", bit)
    ties = [send] + [halving.got for halving in halvings]
    grad_queries, _ = query_gradient(1, grad_queries, ties)
    for halving in halvings:
        while halving.order:
            halving.step()
    while bit > 1:
        total = hold + got.astype(jnp.float32)
        bit //= 2
        part //= 2
        mine = (position // bit) % 2
        send = lax.dynamic_slice_in_dim(total, (1 - mine) * part, part, 1).astype(jnp.bfloat16)
        hold = lax.dynamic_slice_in_dim(total, mine * part, part, 1)
        got = swapped(send, "head", bit)
    vmem = pl.BlockSpec(memory_space=pltpu.VMEM)
    terms = sum(([halving.hold, halving.got] for halving in halvings), [])
    grad_up_value, turned_latents = pl.pallas_call(
        final_kernel,
        in_specs=[vmem] * (2 + len(terms)),
        out_shape=[
            jax.ShapeDtypeStruct((own_rows, heads * vdim), jnp.float32),
            jax.ShapeDtypeStruct((feat, part), jnp.float32),
        ],
        compiler_params=pltpu.CompilerParams(vmem_limit_bytes=small_bytes),
        cost_estimate=cost(1e6, 2e6),
        name="final",
    )(hold, got, *terms)
    return (grad_queries, turned_latents.T, grad_up_value)


def solution(mesh):
    return jax.shard_map(
        on_device,
        mesh=mesh,
        in_specs=(
            P("ctx", "head"),
            P("ctx", None),
            P(None, "head"),
            P("ctx", "head"),
            P("ctx", "head"),
            P("ctx", "head"),
            P(),
        ),
        out_specs=(P("ctx", "head"), P(("ctx", "head"), None), P("ctx", "head")),
        check_vma=False,
    )
```

```python
import functools

import jax
import jax.numpy as jnp
from jax import lax
from jax.experimental import pallas as pl
from jax.experimental.pallas import tpu as pltpu
from jax.sharding import PartitionSpec as P

softmax_scale = 192.0 ** (-0.5)
vmem_bytes = 32 * 1024 * 1024
prepare_bytes = 54 * 1024 * 1024
small_bytes = 16 * 1024 * 1024
chunks = 2
pieces = 2


def nt_dot(a, b):
    return lax.dot_general(a, b, (((1,), (1,)), ((), ())), preferred_element_type=jnp.float32)


def nn_dot(a, b):
    return lax.dot_general(a, b, (((1,), (0,)), ((), ())), preferred_element_type=jnp.float32)


def beside_heads(ref, heads, width):
    return jnp.concatenate([ref[:, h * width : (h + 1) * width] for h in heads], axis=1)


def on_diagonal(ref, heads, width):
    blocks = [ref[:, h * width : (h + 1) * width] for h in heads]
    zero = jnp.zeros_like(blocks[0])
    return jnp.concatenate(
        [
            jnp.concatenate([block if i == j else zero for j in range(len(blocks))], axis=1)
            for i, block in enumerate(blocks)
        ],
        axis=0,
    )


def pairs_of(unit, per_unit):
    heads = list(range(unit * per_unit, (unit + 1) * per_unit))
    return [heads[i : i + 2] for i in range(0, per_unit, 2)]


def wide_rows(q_ref, heads, feat, width):
    parts = []
    for head in heads:
        if head * feat % 128 == 0:
            parts.append(q_ref[:, head * feat : head * feat + width])
        else:
            end = (head + 1) * feat
            wide = q_ref[:, end - width : end]
            parts.append(jnp.concatenate([wide[:, width - feat :], wide[:, : width - feat]], axis=1))
    return jnp.concatenate(parts, axis=0)


def prepare_kernel(
    place_ref, docs_ref, lat_ref, lse_ref, g_ref, o_ref, w_ref, own_ref, table_ref, glat_ref,
    *, units, per_unit, rows, vdim, key_rows,
):
    heads = lse_ref.shape[0]
    window = table_ref.shape[0] - 2 * heads
    span = per_unit * rows

    @pl.when(pl.program_id(0) == 0)
    def _():
        own_ref[...] = lat_ref[...]
        table_ref[window : window + heads, :] = lse_ref[...]
        place = place_ref[0]
        query_pos = place * key_rows + (key_rows - rows) + lax.broadcasted_iota(jnp.int32, (8, rows), 1)
        start = jnp.zeros((8, rows), jnp.int32)
        for i in range(docs_ref.shape[0]):
            entry = docs_ref[i]
            start = jnp.where(entry <= query_pos, jnp.maximum(start, entry), start)
        key_pos = (place + 1) * key_rows - window + lax.broadcasted_iota(jnp.int32, (window, rows), 0)
        allowed = (key_pos >= start[:1]) & (key_pos <= query_pos[:1])
        table_ref[:window, :] = jnp.where(allowed, 0.0, -1e30)

    deltas = []
    for unit in range(units):
        pairs = pairs_of(unit, per_unit)
        for i, pair in enumerate(pairs):
            row = unit * span + 2 * i * rows
            glat_ref[row : row + 2 * rows, :] = nt_dot(
                on_diagonal(g_ref, pair, vdim), beside_heads(w_ref, pair, vdim)
            ).astype(glat_ref.dtype)
            for head in pair:
                lanes = slice(head * vdim, (head + 1) * vdim)
                product = g_ref[:, lanes].astype(jnp.float32) * o_ref[:, lanes].astype(jnp.float32)
                deltas.append(jnp.sum(product.T, axis=0, keepdims=True))
    count = len(deltas)
    row = window + heads + pl.program_id(0) * count
    table_ref[pl.ds(pl.multiple_of(row, count), count), :] = jnp.concatenate(deltas, axis=0)


def forward_kernel(
    place_ref, *rest, units, per_unit, rows, feat, lat, vdim, base, own_rows, first, key_rows,
):
    if first:
        (lat0_ref, lat1_ref, lat2_ref, q_ref, g_ref, table_ref, p_ref, keep_ref, send_ref, ct_ref, c_ref) = rest
    else:
        (ct_ref, c_ref, q_ref, g_ref, table_ref, _, p_ref, keep_ref, send_ref) = rest
    window, width = c_ref.shape
    far = window - key_rows
    core = place_ref[0] % 2

    if first:

        @pl.when(pl.program_id(0) == 0)
        def _():
            ct_ref[:, : far - key_rows] = lat2_ref[...]
            ct_ref[:, far - key_rows : far] = lat1_ref[...]
            ct_ref[:, far:] = lat0_ref[...]
            gap = jnp.zeros((width - feat, window), ct_ref.dtype)
            c_ref[...] = jnp.concatenate([ct_ref[...], gap], axis=0).T

    bias = table_ref[:window, :]
    span = per_unit * rows
    scores = [
        nt_dot(c_ref[...], wide_rows(q_ref, sum(pairs_of(unit, per_unit), []), feat, width)) for unit in range(units)
    ]
    for unit in range(units):
        for k in range(per_unit):
            index = ((pl.program_id(0) + base) * units + unit) * per_unit + k
            shift = table_ref[pl.ds(window + index, 1), :]
            column = unit * span + k * rows
            p_ref[:, column : column + rows] = jnp.exp(
                scores[unit][:, k * rows : (k + 1) * rows] * softmax_scale + (bias - shift)
            ).astype(jnp.bfloat16)
    olats = [
        nn_dot(ct_ref[:lat, :], p_ref[:, unit * span : (unit + 1) * span]).astype(jnp.bfloat16)
        for unit in range(units)
    ]
    for unit in range(units):
        for i, pair in enumerate(pairs_of(unit, per_unit)):
            part = nn_dot(
                olats[unit][:, 2 * i * rows : 2 * (i + 1) * rows], on_diagonal(g_ref, pair, vdim)
            )
            lanes = slice(pair[0] * vdim, (pair[0] + 2) * vdim)
            part = part.reshape(lat // (2 * own_rows), 2, own_rows, 2 * vdim)
            low, high = part[:, 0], part[:, 1]
            keep_ref[:, lanes] = (
                jnp.where(core == 0, low, high).reshape(lat // 2, 2 * vdim).astype(keep_ref.dtype)
            )
            send_ref[:, lanes] = (
                jnp.where(core == 0, high, low).reshape(lat // 2, 2 * vdim).astype(send_ref.dtype)
            )


def store_turned(gq_ref, turned, first_head, count, rows, feat):
    for k in range(0, count, 2):
        both = jnp.concatenate(
            [turned[:, (k + j) * rows : (k + j + 1) * rows] for j in range(2)], axis=0
        )
        gq_ref[:, (first_head + k) * feat : (first_head + k + 2) * feat] = both.T


def backward_kernel(
    ct_ref, c_ref, q_ref, glat_ref, table_ref, p_ref, *rest,
    units, per_unit, rows, feat, lat, steps, base, first, last, ties, key_rows,
):
    rest = list(rest)
    acc_in = None if first else rest.pop(0)
    rest = rest[ties:]
    if last:
        ds_ref, near_ref, far1_ref, far2_ref, acc = rest
    else:
        gq_ref, acc_out, acc, ds_ref = rest
    span = per_unit * rows
    width = c_ref.shape[1]

    @pl.when(pl.program_id(0) == 0)
    def _():
        acc[...] = jnp.zeros_like(acc) if first else acc_in[...]

    first_delta = (table_ref.shape[0] + c_ref.shape[0]) // 2
    gprobs = [
        nt_dot(c_ref[:, :lat], glat_ref[unit * span : (unit + 1) * span, :]) for unit in range(units)
    ]
    for unit in range(units):
        for k in range(per_unit):
            index = ((pl.program_id(0) + base) * units + unit) * per_unit + k
            delta = table_ref[pl.ds(first_delta + index, 1), :]
            own = slice(unit * span + k * rows, unit * span + (k + 1) * rows)
            ds_ref[:, own] = (
                p_ref[:, own].astype(jnp.float32)
                * ((gprobs[unit][:, k * rows : (k + 1) * rows] - delta) * softmax_scale)
            ).astype(jnp.bfloat16)
    query = wide_rows(q_ref, list(range(units * per_unit)), feat, width)
    acc[:, :lat] += nn_dot(
        jnp.concatenate([ds_ref[...], p_ref[...]], axis=1),
        jnp.concatenate([query[:, :lat], glat_ref[...]], axis=0),
    )
    acc[:, lat:] += nn_dot(ds_ref[...], query[:, lat:])
    if not last:
        for unit in range(units):
            turned = nn_dot(ct_ref[...], ds_ref[:, unit * span : (unit + 1) * span]).astype(jnp.bfloat16)
            store_turned(gq_ref, turned, unit * per_unit, per_unit, rows, feat)

    @pl.when(pl.program_id(0) == steps - 1)
    def _():
        if last:
            far2 = far2_ref.shape[1]
            total = acc[...].T[:feat]
            far2_ref[...] = total[:, :far2].astype(far2_ref.dtype)
            far1_ref[...] = total[:, far2 : far2 + key_rows].astype(far1_ref.dtype)
            near_ref[...] = total[:, far2 + key_rows :]
        else:
            acc_out[...] = acc[...]


def query_kernel(ct_ref, ds_ref, *rest, count, rows, feat):
    gq_ref, token_ref = rest[-2:]
    token_ref[...] = jnp.zeros_like(token_ref)
    store_turned(gq_ref, nn_dot(ct_ref[...], ds_ref[...]).astype(jnp.bfloat16), 0, count, rows, feat)


def passed_along(value, axis, steps):
    count = lax.axis_size(axis)
    first, last = (max(0, -steps), min(count, count - steps))
    return lax.ppermute(value, axis, [(source, source + steps) for source in range(first, last)])


def swapped(value, axis, bit):
    count = lax.axis_size(axis)
    return lax.ppermute(value, axis, [(source, source ^ bit) for source in range(count)])


def params(limit=vmem_bytes):
    return pltpu.CompilerParams(dimension_semantics=("arbitrary",), vmem_limit_bytes=limit)


def cost(flops, moved):
    return pl.CostEstimate(flops=int(flops), bytes_accessed=int(moved), transcendentals=0)


def bit_of(place, bit):
    return (place >> bit) & 1


def halving_kernel(place_ref, hold_ref, got_ref, send_ref, keep_ref, *, dim, bit):
    mine = bit_of(place_ref[0], bit)
    lead = (slice(None),) * dim
    for which, out_ref in ((1 - mine, send_ref), (mine, keep_ref)):
        where = lead + (which,)
        out_ref[...] = (hold_ref[where].astype(jnp.float32) + got_ref[where].astype(jnp.float32)).astype(
            out_ref.dtype
        )


def final_kernel(hold_ref, got_ref, *refs):
    out_ref, lat_ref = refs[-2:]
    lat_ref[...] = hold_ref[...] + got_ref[...].astype(jnp.float32)
    cols = refs[0].shape[-1]
    for i in range(len(refs) // 2 - 1):
        out_ref[:, i * cols : (i + 1) * cols] = refs[2 * i][...] + refs[2 * i + 1][...].astype(jnp.float32)


def latent_kernel(side_ref, near_ref, got1_ref, got2_ref, _, send_ref, hold_ref):
    low = near_ref[...] + got1_ref[...].astype(jnp.float32)
    part = send_ref.shape[1]
    spare = near_ref.shape[1] - got2_ref.shape[1]
    whole = jnp.concatenate([low[:, :spare], low[:, spare:] + got2_ref[...].astype(jnp.float32)], axis=1)
    first, second = whole[:, :part], whole[:, part:]
    lower = side_ref[0] == 0
    send_ref[...] = jnp.where(lower, second, first).astype(send_ref.dtype)
    hold_ref[...] = jnp.where(lower, first, second)


class Halving:
    def __init__(self, hold, got, bits, place, axis):
        self.hold, self.got, self.place, self.axis = hold, got, place, axis
        self.opened, self.order = sorted(bits, reverse=True), list(bits)

    def step(self):
        bit = self.order.pop(0)
        shape = (2,) * (len(self.opened) - 1) + self.hold.shape[-2:]
        vmem = pl.BlockSpec(memory_space=pltpu.VMEM)
        sent, self.hold = pl.pallas_call(
            functools.partial(halving_kernel, dim=self.opened.index(bit), bit=bit),
            in_specs=[pl.BlockSpec(memory_space=pltpu.SMEM), vmem, vmem],
            out_shape=[jax.ShapeDtypeStruct(shape, jnp.bfloat16), jax.ShapeDtypeStruct(shape, jnp.float32)],
            compiler_params=pltpu.CompilerParams(vmem_limit_bytes=small_bytes),
            cost_estimate=cost(1e6, 2e6),
            name="halving",
        )(self.place, self.hold, self.got)
        self.opened.remove(bit)
        self.got = swapped(sent.reshape((-1, shape[-1])), self.axis, 1 << bit).reshape(shape)
        return sent


def on_device(queries, latents, up_value, grad_out, out_saved, log_sums, doc_starts):
    rows = queries.shape[0]
    key_rows, feat = latents.shape
    lat = up_value.shape[0]
    heads = log_sums.shape[1]
    vdim = grad_out.shape[1] // heads
    ctx = lax.axis_size("ctx")
    own_rows = lat // ctx
    window = 2 * key_rows + rows
    far = window - key_rows
    width = -(-feat // 128) * 128
    unit = max(2, min(4, heads // pieces))

    place = lax.axis_index("ctx").astype(jnp.int32)
    turned = latents.T
    prev1 = passed_along(turned, "ctx", 1)
    prev2 = passed_along(turned[:, key_rows - (far - key_rows) :], "ctx", 2)
    sums_turned = log_sums.T

    def whole(*shape):
        return pl.BlockSpec(shape, lambda i: (0,) * len(shape))

    smem = pl.BlockSpec(memory_space=pltpu.SMEM)
    untouched = pl.BlockSpec(memory_space=pl.ANY)
    scalar = place.reshape(1)

    chunk_heads = heads // chunks
    units = max(1, min(2, heads // unit))
    group = units * unit
    lanes = lambda i: (0, i)
    rowed = lambda i: (i, 0)
    own, table, glat = pl.pallas_call(
        functools.partial(
            prepare_kernel, units=units, per_unit=unit, rows=rows, vdim=vdim, key_rows=key_rows
        ),
        grid=(heads // group,),
        in_specs=[
            smem,
            smem,
            whole(feat, key_rows),
            whole(heads, rows),
            pl.BlockSpec((rows, group * vdim), lanes),
            pl.BlockSpec((rows, group * vdim), lanes),
            pl.BlockSpec((lat, group * vdim), lanes),
        ],
        out_specs=[
            whole(feat, key_rows),
            whole(window + 2 * heads, rows),
            pl.BlockSpec((group * rows, lat), rowed),
        ],
        out_shape=[
            jax.ShapeDtypeStruct((feat, key_rows), jnp.bfloat16),
            jax.ShapeDtypeStruct((window + 2 * heads, rows), jnp.float32),
            jax.ShapeDtypeStruct((heads * rows, lat), jnp.bfloat16),
        ],
        compiler_params=params(prepare_bytes),
        cost_estimate=cost(heads * rows * 4 * lat * vdim, 20e6),
        name="prepare",
    )(scalar, doc_starts, turned, sums_turned, grad_out, out_saved, up_value)

    probs = None
    partials = []
    units = max(1, min(2, chunk_heads // unit))
    group = units * unit
    steps = chunk_heads // group
    for chunk in range(chunks):
        base = chunk * steps
        lanes = lambda i, base=base: (0, i + base)
        rowed = lambda i, base=base: (i + base, 0)
        first = chunk == 0
        in_specs = [smem]
        operands = [scalar]
        if first:
            in_specs += [whole(feat, key_rows), whole(feat, key_rows), whole(feat, far - key_rows)]
            operands += [own, prev1, prev2]
        else:
            in_specs += [whole(feat, window), whole(window, width)]
            operands += [keys_turned, keys]
        in_specs += [
            pl.BlockSpec((rows, group * feat), lanes),
            pl.BlockSpec((rows, group * vdim), lanes),
            whole(window + 2 * heads, rows),
        ]
        operands += [queries, grad_out, table]
        halves = [pl.BlockSpec((lat // 2, group * vdim), lambda i: (0, i))] * 2
        out_specs = [pl.BlockSpec((window, group * rows), lanes)] + halves
        out_shape = [jax.ShapeDtypeStruct((window, heads * rows), jnp.bfloat16)]
        out_shape += [jax.ShapeDtypeStruct((lat // 2, chunk_heads * vdim), jnp.bfloat16)] * 2
        aliases = {}
        if first:
            out_specs += [whole(feat, window), whole(window, width)]
            out_shape += [
                jax.ShapeDtypeStruct((feat, window), jnp.bfloat16),
                jax.ShapeDtypeStruct((window, width), jnp.bfloat16),
            ]
        else:
            aliases = {len(operands): 0}
            in_specs.append(untouched)
            operands.append(probs)
        out = pl.pallas_call(
            functools.partial(
                forward_kernel, units=units, per_unit=unit, rows=rows, feat=feat, lat=lat, vdim=vdim,
                base=base, own_rows=own_rows, first=first, key_rows=key_rows,
            ),
            grid=(steps,),
            in_specs=in_specs,
            out_specs=out_specs,
            out_shape=out_shape,
            input_output_aliases=aliases,
            compiler_params=params(),
            cost_estimate=cost(chunk_heads * rows * 2 * window * (width + lat) * 2, 1e6),
            name="forward",
        )(*operands)
        if first:
            keys_turned, keys = out[3:]
        probs, keep, send = out[:3]
        partials.append((keep, send))

    upper = list(range(1, ctx.bit_length() - 1))
    shape = (2,) * len(upper) + (own_rows, chunk_heads * vdim)
    halvings = []
    for (keep, send), order in zip(partials, (upper[1:] + upper[:1], upper)):
        got = swapped(send, "ctx", 1)
        halvings.append(Halving(keep.reshape(shape), got.reshape(shape), order, scalar, "ctx"))

    piece_heads = heads // pieces
    units = max(1, min(2, piece_heads // unit))
    group = units * unit
    steps = piece_heads // group
    acc = None
    for piece in range(pieces):
        ties = [halving.step() for halving in halvings if halving.order]
        first, last = piece == 0, piece == pieces - 1
        base = piece * steps
        lanes = lambda i, base=base: (0, i + base)
        rowed = lambda i, base=base: (i + base, 0)
        in_specs = [
            whole(feat, window),
            whole(window, width),
            pl.BlockSpec((rows, group * feat), lanes),
            pl.BlockSpec((group * rows, lat), rowed),
            whole(window + 2 * heads, rows),
            pl.BlockSpec((window, group * rows), lanes),
        ]
        operands = [keys_turned, keys, queries, glat, table, probs]
        if not first:
            in_specs.append(whole(window, width))
            operands.append(acc)
        in_specs += [untouched] * len(ties)
        operands += ties
        scratch = [pltpu.VMEM((window, width), jnp.float32)]
        if last:
            out_specs = [pl.BlockSpec((window, group * rows), lambda i: (0, i))]
            out_shape = [jax.ShapeDtypeStruct((window, piece_heads * rows), jnp.bfloat16)]
            out_specs += [whole(feat, key_rows), whole(feat, key_rows), whole(feat, far - key_rows)]
            out_shape += [
                jax.ShapeDtypeStruct((feat, key_rows), jnp.float32),
                jax.ShapeDtypeStruct((feat, key_rows), jnp.bfloat16),
                jax.ShapeDtypeStruct((feat, far - key_rows), jnp.bfloat16),
            ]
        else:
            out_specs = [pl.BlockSpec((rows, group * feat), lanes), whole(window, width)]
            out_shape = [
                jax.ShapeDtypeStruct(queries.shape, jnp.bfloat16),
                jax.ShapeDtypeStruct((window, width), jnp.float32),
            ]
            scratch.append(pltpu.VMEM((window, group * rows), jnp.bfloat16))
        out = pl.pallas_call(
            functools.partial(
                backward_kernel, units=units, per_unit=unit, rows=rows, feat=feat, lat=lat, base=base,
                steps=steps, first=first, last=last, ties=len(ties), key_rows=key_rows,
            ),
            grid=(steps,),
            in_specs=in_specs,
            out_specs=out_specs,
            out_shape=out_shape,
            scratch_shapes=scratch,
            compiler_params=params(),
            cost_estimate=cost(piece_heads * rows * 2 * window * (width + 2 * lat) * 2, 1e6),
            name="backward",
        )(*operands)
        if last:
            dscores, near, far1, far2 = out
        else:
            grad_queries, acc = out

    late_heads = piece_heads // 2
    late_group = min(4, late_heads)
    late_steps = late_heads // late_group

    def query_gradient(call, so_far, ties):
        out_base = (heads - piece_heads + call * late_heads) // late_group
        return pl.pallas_call(
            functools.partial(query_kernel, count=late_group, rows=rows, feat=feat),
            grid=(late_steps,),
            in_specs=[
                whole(feat, window),
                pl.BlockSpec((window, late_group * rows), lambda i: (0, call * late_steps + i)),
            ]
            + [untouched] * (1 + len(ties)),
            out_specs=[
                pl.BlockSpec((rows, late_group * feat), lambda i: (0, out_base + i)),
                whole(8, 128),
            ],
            out_shape=[
                jax.ShapeDtypeStruct(queries.shape, jnp.bfloat16),
                jax.ShapeDtypeStruct((8, 128), jnp.float32),
            ],
            input_output_aliases={2: 0},
            compiler_params=params(),
            cost_estimate=cost(late_heads * rows * 2 * window * width * 3, 1e6),
            name="query_gradient",
        )(keys_turned, dscores, so_far, *ties)

    got1 = passed_along(far1, "ctx", -1)
    got2 = passed_along(far2, "ctx", -2)
    ties = [halving.step() for halving in halvings if halving.order]
    grad_queries, token = query_gradient(0, grad_queries, ties)
    position = lax.axis_index("head").astype(jnp.int32)
    bit = lax.axis_size("head") // 2
    part = key_rows // 2
    send, hold = pl.pallas_call(
        latent_kernel,
        in_specs=[smem] + [pl.BlockSpec(memory_space=pltpu.VMEM)] * 3 + [untouched],
        out_shape=[
            jax.ShapeDtypeStruct((feat, part), jnp.bfloat16),
            jax.ShapeDtypeStruct((feat, part), jnp.float32),
        ],
        compiler_params=pltpu.CompilerParams(vmem_limit_bytes=small_bytes),
        cost_estimate=cost(1e6, 2e6),
        name="latent",
    )((position // bit % 2).reshape(1), near, got1, got2, token)
    got = swapped(send, "head", bit)
    ties = [send] + [halving.got for halving in halvings]
    grad_queries, _ = query_gradient(1, grad_queries, ties)
    for halving in halvings:
        while halving.order:
            halving.step()
    while bit > 1:
        total = hold + got.astype(jnp.float32)
        bit //= 2
        part //= 2
        mine = (position // bit) % 2
        send = lax.dynamic_slice_in_dim(total, (1 - mine) * part, part, 1).astype(jnp.bfloat16)
        hold = lax.dynamic_slice_in_dim(total, mine * part, part, 1)
        got = swapped(send, "head", bit)
    vmem = pl.BlockSpec(memory_space=pltpu.VMEM)
    terms = sum(([halving.hold, halving.got] for halving in halvings), [])
    grad_up_value, turned_latents = pl.pallas_call(
        final_kernel,
        in_specs=[vmem] * (2 + len(terms)),
        out_shape=[
            jax.ShapeDtypeStruct((own_rows, heads * vdim), jnp.float32),
            jax.ShapeDtypeStruct((feat, part), jnp.float32),
        ],
        compiler_params=pltpu.CompilerParams(vmem_limit_bytes=small_bytes),
        cost_estimate=cost(1e6, 2e6),
        name="final",
    )(hold, got, *terms)
    return (grad_queries, turned_latents.T, grad_up_value)


def solution(mesh):
    return jax.shard_map(
        on_device,
        mesh=mesh,
        in_specs=(
            P("ctx", "head"),
            P("ctx", None),
            P(None, "head"),
            P("ctx", "head"),
            P("ctx", "head"),
            P("ctx", "head"),
            P(),
        ),
        out_specs=(P("ctx", "head"), P(("ctx", "head"), None), P("ctx", "head")),
        check_vma=False,
    )
```

```python
import functools

import jax
import jax.numpy as jnp
from jax import lax
from jax.experimental import pallas as pl
from jax.experimental.pallas import tpu as pltpu
from jax.sharding import PartitionSpec as P

softmax_scale = 192.0 ** (-0.5)
vmem_bytes = 20 * 1024 * 1024
prepare_bytes = 54 * 1024 * 1024
small_bytes = 8 * 1024 * 1024
chunks = 2
pieces = 2


def nt_dot(a, b):
    return lax.dot_general(a, b, (((1,), (1,)), ((), ())), preferred_element_type=jnp.float32)


def nn_dot(a, b):
    return lax.dot_general(a, b, (((1,), (0,)), ((), ())), preferred_element_type=jnp.float32)


def beside_heads(ref, heads, width):
    return jnp.concatenate([ref[:, h * width : (h + 1) * width] for h in heads], axis=1)


def on_diagonal(ref, heads, width):
    blocks = [ref[:, h * width : (h + 1) * width] for h in heads]
    zero = jnp.zeros_like(blocks[0])
    return jnp.concatenate(
        [
            jnp.concatenate([block if i == j else zero for j in range(len(blocks))], axis=1)
            for i, block in enumerate(blocks)
        ],
        axis=0,
    )


def pairs_of(unit, per_unit):
    heads = list(range(unit * per_unit, (unit + 1) * per_unit))
    return [heads[i : i + 2] for i in range(0, per_unit, 2)]


def wide_rows(q_ref, heads, feat, width):
    parts = []
    for head in heads:
        if head * feat % 128 == 0:
            parts.append(q_ref[:, head * feat : head * feat + width])
        else:
            end = (head + 1) * feat
            wide = q_ref[:, end - width : end]
            parts.append(jnp.concatenate([wide[:, width - feat :], wide[:, : width - feat]], axis=1))
    return jnp.concatenate(parts, axis=0)


def prepare_kernel(
    place_ref, docs_ref, lse_ref, g_ref, o_ref, w_ref, table_ref, glat_ref,
    *, units, per_unit, rows, vdim, key_rows,
):
    heads = lse_ref.shape[0]
    window = table_ref.shape[0] - 2 * heads
    span = per_unit * rows

    @pl.when(pl.program_id(0) == 0)
    def _():
        table_ref[window : window + heads, :] = lse_ref[...]
        place = place_ref[0]
        query_pos = place * key_rows + (key_rows - rows) + lax.broadcasted_iota(jnp.int32, (8, rows), 1)
        start = jnp.zeros((8, rows), jnp.int32)
        for i in range(docs_ref.shape[0]):
            entry = docs_ref[i]
            start = jnp.where(entry <= query_pos, jnp.maximum(start, entry), start)
        key_pos = (place + 1) * key_rows - window + lax.broadcasted_iota(jnp.int32, (window, rows), 0)
        allowed = (key_pos >= start[:1]) & (key_pos <= query_pos[:1])
        table_ref[:window, :] = jnp.where(allowed, 0.0, -1e30)

    deltas = []
    for unit in range(units):
        pairs = pairs_of(unit, per_unit)
        for i, pair in enumerate(pairs):
            row = unit * span + 2 * i * rows
            glat_ref[row : row + 2 * rows, :] = nt_dot(
                on_diagonal(g_ref, pair, vdim), beside_heads(w_ref, pair, vdim)
            ).astype(glat_ref.dtype)
            for head in pair:
                lanes = slice(head * vdim, (head + 1) * vdim)
                product = g_ref[:, lanes].astype(jnp.float32) * o_ref[:, lanes].astype(jnp.float32)
                deltas.append(jnp.sum(product.T, axis=0, keepdims=True))
    count = len(deltas)
    row = window + heads + pl.program_id(0) * count
    table_ref[pl.ds(pl.multiple_of(row, count), count), :] = jnp.concatenate(deltas, axis=0)


def forward_kernel(
    place_ref, *rest, units, per_unit, rows, feat, lat, vdim, base, own_rows, first, key_rows,
):
    if first:
        (lat0_ref, lat1_ref, lat2_ref, q_ref, g_ref, table_ref, p_ref, keep_ref, send_ref, ct_ref, c_ref) = rest
    else:
        (ct_ref, c_ref, q_ref, g_ref, table_ref, _, p_ref, keep_ref, send_ref) = rest
    window, width = c_ref.shape
    far = window - key_rows
    core = place_ref[0] % 2

    if first:

        @pl.when(pl.program_id(0) == 0)
        def _():
            ct_ref[:, : far - key_rows] = lat2_ref[...]
            ct_ref[:, far - key_rows : far] = lat1_ref[...]
            ct_ref[:, far:] = lat0_ref[...]
            gap = jnp.zeros((width - feat, window), ct_ref.dtype)
            c_ref[...] = jnp.concatenate([ct_ref[...], gap], axis=0).T

    bias = table_ref[:window, :]
    span = per_unit * rows
    scores = [
        nt_dot(c_ref[...], wide_rows(q_ref, sum(pairs_of(unit, per_unit), []), feat, width)) for unit in range(units)
    ]
    for unit in range(units):
        for k in range(per_unit):
            index = ((pl.program_id(0) + base) * units + unit) * per_unit + k
            shift = table_ref[pl.ds(window + index, 1), :]
            column = unit * span + k * rows
            p_ref[:, column : column + rows] = jnp.exp(
                scores[unit][:, k * rows : (k + 1) * rows] * softmax_scale + (bias - shift)
            ).astype(jnp.bfloat16)
    olats = [
        nn_dot(ct_ref[:lat, :], p_ref[:, unit * span : (unit + 1) * span]).astype(jnp.bfloat16)
        for unit in range(units)
    ]
    for unit in range(units):
        for i, pair in enumerate(pairs_of(unit, per_unit)):
            part = nn_dot(
                olats[unit][:, 2 * i * rows : 2 * (i + 1) * rows], on_diagonal(g_ref, pair, vdim)
            )
            lanes = slice(pair[0] * vdim, (pair[0] + 2) * vdim)
            part = part.reshape(lat // (2 * own_rows), 2, own_rows, 2 * vdim)
            low, high = part[:, 0], part[:, 1]
            keep_ref[:, lanes] = (
                jnp.where(core == 0, low, high).reshape(lat // 2, 2 * vdim).astype(keep_ref.dtype)
            )
            send_ref[:, lanes] = (
                jnp.where(core == 0, high, low).reshape(lat // 2, 2 * vdim).astype(send_ref.dtype)
            )


def store_turned(gq_ref, turned, first_head, count, rows, feat):
    for k in range(0, count, 2):
        both = jnp.concatenate(
            [turned[:, (k + j) * rows : (k + j + 1) * rows] for j in range(2)], axis=0
        )
        gq_ref[:, (first_head + k) * feat : (first_head + k + 2) * feat] = both.T


def backward_kernel(
    ct_ref, c_ref, q_ref, glat_ref, table_ref, p_ref, *rest,
    units, per_unit, rows, feat, lat, steps, base, first, last, ties, key_rows,
):
    rest = list(rest)
    acc_in = None if first else rest.pop(0)
    rest = rest[ties:]
    if last:
        ds_ref, near_ref, far1_ref, far2_ref, acc = rest
    else:
        gq_ref, acc_out, acc, ds_ref = rest
    span = per_unit * rows
    width = c_ref.shape[1]

    @pl.when(pl.program_id(0) == 0)
    def _():
        acc[...] = jnp.zeros_like(acc) if first else acc_in[...]

    first_delta = (table_ref.shape[0] + c_ref.shape[0]) // 2
    gprobs = [
        nt_dot(c_ref[:, :lat], glat_ref[unit * span : (unit + 1) * span, :]) for unit in range(units)
    ]
    for unit in range(units):
        for k in range(per_unit):
            index = ((pl.program_id(0) + base) * units + unit) * per_unit + k
            delta = table_ref[pl.ds(first_delta + index, 1), :]
            own = slice(unit * span + k * rows, unit * span + (k + 1) * rows)
            ds_ref[:, own] = (
                p_ref[:, own].astype(jnp.float32)
                * ((gprobs[unit][:, k * rows : (k + 1) * rows] - delta) * softmax_scale)
            ).astype(jnp.bfloat16)
    query = wide_rows(q_ref, list(range(units * per_unit)), feat, width)
    acc[:, :lat] += nn_dot(
        jnp.concatenate([ds_ref[...], p_ref[...]], axis=1),
        jnp.concatenate([query[:, :lat], glat_ref[...]], axis=0),
    )
    acc[:, lat:] += nn_dot(ds_ref[...], query[:, lat:])
    if not last:
        for unit in range(units):
            turned = nn_dot(ct_ref[...], ds_ref[:, unit * span : (unit + 1) * span]).astype(jnp.bfloat16)
            store_turned(gq_ref, turned, unit * per_unit, per_unit, rows, feat)

    @pl.when(pl.program_id(0) == steps - 1)
    def _():
        if last:
            far2 = far2_ref.shape[1]
            total = acc[...].T[:feat]
            far2_ref[...] = total[:, :far2].astype(far2_ref.dtype)
            far1_ref[...] = total[:, far2 : far2 + key_rows].astype(far1_ref.dtype)
            near_ref[...] = total[:, far2 + key_rows :]
        else:
            acc_out[...] = acc[...]


def query_kernel(ct_ref, ds_ref, *rest, count, rows, feat):
    gq_ref, token_ref = rest[-2:]
    token_ref[...] = jnp.zeros_like(token_ref)
    store_turned(gq_ref, nn_dot(ct_ref[...], ds_ref[...]).astype(jnp.bfloat16), 0, count, rows, feat)


def passed_along(value, axis, steps):
    count = lax.axis_size(axis)
    first, last = (max(0, -steps), min(count, count - steps))
    return lax.ppermute(value, axis, [(source, source + steps) for source in range(first, last)])


def swapped(value, axis, bit):
    count = lax.axis_size(axis)
    return lax.ppermute(value, axis, [(source, source ^ bit) for source in range(count)])


def params(limit=vmem_bytes):
    return pltpu.CompilerParams(dimension_semantics=("arbitrary",), vmem_limit_bytes=limit)


def cost(flops, moved):
    return pl.CostEstimate(flops=int(flops), bytes_accessed=int(moved), transcendentals=0)


def bit_of(place, bit):
    return (place >> bit) & 1


def halving_kernel(place_ref, hold_ref, got_ref, send_ref, keep_ref, *, dim, bit):
    mine = bit_of(place_ref[0], bit)
    lead = (slice(None),) * dim
    for which, out_ref in ((1 - mine, send_ref), (mine, keep_ref)):
        where = lead + (which,)
        out_ref[...] = (hold_ref[where].astype(jnp.float32) + got_ref[where].astype(jnp.float32)).astype(
            out_ref.dtype
        )


def final_kernel(hold_ref, got_ref, *refs):
    out_ref, lat_ref = refs[-2:]
    lat_ref[...] = hold_ref[...] + got_ref[...].astype(jnp.float32)
    cols = refs[0].shape[-1]
    for i in range(len(refs) // 2 - 1):
        out_ref[:, i * cols : (i + 1) * cols] = refs[2 * i][...] + refs[2 * i + 1][...].astype(jnp.float32)


def latent_kernel(side_ref, near_ref, got1_ref, got2_ref, _, send_ref, hold_ref):
    low = near_ref[...] + got1_ref[...].astype(jnp.float32)
    part = send_ref.shape[1]
    spare = near_ref.shape[1] - got2_ref.shape[1]
    whole = jnp.concatenate([low[:, :spare], low[:, spare:] + got2_ref[...].astype(jnp.float32)], axis=1)
    first, second = whole[:, :part], whole[:, part:]
    lower = side_ref[0] == 0
    send_ref[...] = jnp.where(lower, second, first).astype(send_ref.dtype)
    hold_ref[...] = jnp.where(lower, first, second)


class Halving:
    def __init__(self, hold, got, bits, place, axis):
        self.hold, self.got, self.place, self.axis = hold, got, place, axis
        self.opened, self.order = sorted(bits, reverse=True), list(bits)

    def step(self):
        bit = self.order.pop(0)
        shape = (2,) * (len(self.opened) - 1) + self.hold.shape[-2:]
        vmem = pl.BlockSpec(memory_space=pltpu.VMEM)
        sent, self.hold = pl.pallas_call(
            functools.partial(halving_kernel, dim=self.opened.index(bit), bit=bit),
            in_specs=[pl.BlockSpec(memory_space=pltpu.SMEM), vmem, vmem],
            out_shape=[jax.ShapeDtypeStruct(shape, jnp.bfloat16), jax.ShapeDtypeStruct(shape, jnp.float32)],
            compiler_params=pltpu.CompilerParams(vmem_limit_bytes=small_bytes),
            cost_estimate=cost(1e6, 2e6),
            name="halving",
        )(self.place, self.hold, self.got)
        self.opened.remove(bit)
        self.got = swapped(sent.reshape((-1, shape[-1])), self.axis, 1 << bit).reshape(shape)
        return sent


def on_device(queries, latents, up_value, grad_out, out_saved, log_sums, doc_starts):
    rows = queries.shape[0]
    key_rows, feat = latents.shape
    lat = up_value.shape[0]
    heads = log_sums.shape[1]
    vdim = grad_out.shape[1] // heads
    ctx = lax.axis_size("ctx")
    own_rows = lat // ctx
    window = 2 * key_rows + rows
    far = window - key_rows
    width = -(-feat // 128) * 128
    unit = max(2, min(4, heads // pieces))

    place = lax.axis_index("ctx").astype(jnp.int32)
    turned = latents.T
    prev1 = passed_along(turned, "ctx", 1)
    prev2 = passed_along(turned[:, key_rows - (far - key_rows) :], "ctx", 2)
    sums_turned = log_sums.T

    def whole(*shape):
        return pl.BlockSpec(shape, lambda i: (0,) * len(shape))

    smem = pl.BlockSpec(memory_space=pltpu.SMEM)
    untouched = pl.BlockSpec(memory_space=pl.ANY)
    scalar = place.reshape(1)

    chunk_heads = heads // chunks
    units = max(1, min(2, heads // unit))
    group = units * unit
    lanes = lambda i: (0, i)
    rowed = lambda i: (i, 0)
    table, glat = pl.pallas_call(
        functools.partial(
            prepare_kernel, units=units, per_unit=unit, rows=rows, vdim=vdim, key_rows=key_rows
        ),
        grid=(heads // group,),
        in_specs=[
            smem,
            smem,
            whole(heads, rows),
            pl.BlockSpec((rows, group * vdim), lanes),
            pl.BlockSpec((rows, group * vdim), lanes),
            pl.BlockSpec((lat, group * vdim), lanes),
        ],
        out_specs=[
            whole(window + 2 * heads, rows),
            pl.BlockSpec((group * rows, lat), rowed),
        ],
        out_shape=[
            jax.ShapeDtypeStruct((window + 2 * heads, rows), jnp.float32),
            jax.ShapeDtypeStruct((heads * rows, lat), jnp.bfloat16),
        ],
        compiler_params=params(prepare_bytes),
        cost_estimate=cost(heads * rows * 4 * lat * vdim, 20e6),
        name="prepare",
    )(scalar, doc_starts, sums_turned, grad_out, out_saved, up_value)

    probs = None
    partials = []
    units = max(1, min(2, chunk_heads // unit))
    group = units * unit
    steps = chunk_heads // group
    for chunk in range(chunks):
        base = chunk * steps
        lanes = lambda i, base=base: (0, i + base)
        rowed = lambda i, base=base: (i + base, 0)
        first = chunk == 0
        in_specs = [smem]
        operands = [scalar]
        if first:
            in_specs += [whole(feat, key_rows), whole(feat, key_rows), whole(feat, far - key_rows)]
            operands += [turned, prev1, prev2]
        else:
            in_specs += [whole(feat, window), whole(window, width)]
            operands += [keys_turned, keys]
        in_specs += [
            pl.BlockSpec((rows, group * feat), lanes),
            pl.BlockSpec((rows, group * vdim), lanes),
            whole(window + 2 * heads, rows),
        ]
        operands += [queries, grad_out, table]
        halves = [pl.BlockSpec((lat // 2, group * vdim), lambda i: (0, i))] * 2
        out_specs = [pl.BlockSpec((window, group * rows), lanes)] + halves
        out_shape = [jax.ShapeDtypeStruct((window, heads * rows), jnp.bfloat16)]
        out_shape += [jax.ShapeDtypeStruct((lat // 2, chunk_heads * vdim), jnp.bfloat16)] * 2
        aliases = {}
        if first:
            out_specs += [whole(feat, window), whole(window, width)]
            out_shape += [
                jax.ShapeDtypeStruct((feat, window), jnp.bfloat16),
                jax.ShapeDtypeStruct((window, width), jnp.bfloat16),
            ]
        else:
            aliases = {len(operands): 0}
            in_specs.append(untouched)
            operands.append(probs)
        out = pl.pallas_call(
            functools.partial(
                forward_kernel, units=units, per_unit=unit, rows=rows, feat=feat, lat=lat, vdim=vdim,
                base=base, own_rows=own_rows, first=first, key_rows=key_rows,
            ),
            grid=(steps,),
            in_specs=in_specs,
            out_specs=out_specs,
            out_shape=out_shape,
            input_output_aliases=aliases,
            compiler_params=params(),
            cost_estimate=cost(chunk_heads * rows * 2 * window * (width + lat) * 2, 1e6),
            name="forward",
        )(*operands)
        if first:
            keys_turned, keys = out[3:]
        probs, keep, send = out[:3]
        partials.append((keep, send))

    upper = list(range(1, ctx.bit_length() - 1))
    shape = (2,) * len(upper) + (own_rows, chunk_heads * vdim)
    halvings = []
    for (keep, send), order in zip(partials, (upper[1:] + upper[:1], upper)):
        got = swapped(send, "ctx", 1)
        halvings.append(Halving(keep.reshape(shape), got.reshape(shape), order, scalar, "ctx"))

    piece_heads = heads // pieces
    units = max(1, min(2, piece_heads // unit))
    group = units * unit
    steps = piece_heads // group
    acc = None
    for piece in range(pieces):
        ties = [halving.step() for halving in halvings if halving.order]
        first, last = piece == 0, piece == pieces - 1
        base = piece * steps
        lanes = lambda i, base=base: (0, i + base)
        rowed = lambda i, base=base: (i + base, 0)
        in_specs = [
            whole(feat, window),
            whole(window, width),
            pl.BlockSpec((rows, group * feat), lanes),
            pl.BlockSpec((group * rows, lat), rowed),
            whole(window + 2 * heads, rows),
            pl.BlockSpec((window, group * rows), lanes),
        ]
        operands = [keys_turned, keys, queries, glat, table, probs]
        if not first:
            in_specs.append(whole(window, width))
            operands.append(acc)
        in_specs += [untouched] * len(ties)
        operands += ties
        scratch = [pltpu.VMEM((window, width), jnp.float32)]
        if last:
            out_specs = [pl.BlockSpec((window, group * rows), lambda i: (0, i))]
            out_shape = [jax.ShapeDtypeStruct((window, piece_heads * rows), jnp.bfloat16)]
            out_specs += [whole(feat, key_rows), whole(feat, key_rows), whole(feat, far - key_rows)]
            out_shape += [
                jax.ShapeDtypeStruct((feat, key_rows), jnp.float32),
                jax.ShapeDtypeStruct((feat, key_rows), jnp.bfloat16),
                jax.ShapeDtypeStruct((feat, far - key_rows), jnp.bfloat16),
            ]
        else:
            out_specs = [pl.BlockSpec((rows, group * feat), lanes), whole(window, width)]
            out_shape = [
                jax.ShapeDtypeStruct(queries.shape, jnp.bfloat16),
                jax.ShapeDtypeStruct((window, width), jnp.float32),
            ]
            scratch.append(pltpu.VMEM((window, group * rows), jnp.bfloat16))
        out = pl.pallas_call(
            functools.partial(
                backward_kernel, units=units, per_unit=unit, rows=rows, feat=feat, lat=lat, base=base,
                steps=steps, first=first, last=last, ties=len(ties), key_rows=key_rows,
            ),
            grid=(steps,),
            in_specs=in_specs,
            out_specs=out_specs,
            out_shape=out_shape,
            scratch_shapes=scratch,
            compiler_params=params(),
            cost_estimate=cost(piece_heads * rows * 2 * window * (width + 2 * lat) * 2, 1e6),
            name="backward",
        )(*operands)
        if last:
            dscores, near, far1, far2 = out
        else:
            grad_queries, acc = out

    late_heads = piece_heads // 2
    late_group = min(4, late_heads)
    late_steps = late_heads // late_group

    def query_gradient(call, so_far, ties):
        out_base = (heads - piece_heads + call * late_heads) // late_group
        return pl.pallas_call(
            functools.partial(query_kernel, count=late_group, rows=rows, feat=feat),
            grid=(late_steps,),
            in_specs=[
                whole(feat, window),
                pl.BlockSpec((window, late_group * rows), lambda i: (0, call * late_steps + i)),
            ]
            + [untouched] * (1 + len(ties)),
            out_specs=[
                pl.BlockSpec((rows, late_group * feat), lambda i: (0, out_base + i)),
                whole(8, 128),
            ],
            out_shape=[
                jax.ShapeDtypeStruct(queries.shape, jnp.bfloat16),
                jax.ShapeDtypeStruct((8, 128), jnp.float32),
            ],
            input_output_aliases={2: 0},
            compiler_params=params(),
            cost_estimate=cost(late_heads * rows * 2 * window * width * 3, 1e6),
            name="query_gradient",
        )(keys_turned, dscores, so_far, *ties)

    got1 = passed_along(far1, "ctx", -1)
    got2 = passed_along(far2, "ctx", -2)
    ties = [halving.step() for halving in halvings if halving.order]
    grad_queries, token = query_gradient(0, grad_queries, ties)
    position = lax.axis_index("head").astype(jnp.int32)
    bit = lax.axis_size("head") // 2
    part = key_rows // 2
    send, hold = pl.pallas_call(
        latent_kernel,
        in_specs=[smem] + [pl.BlockSpec(memory_space=pltpu.VMEM)] * 3 + [untouched],
        out_shape=[
            jax.ShapeDtypeStruct((feat, part), jnp.bfloat16),
            jax.ShapeDtypeStruct((feat, part), jnp.float32),
        ],
        compiler_params=pltpu.CompilerParams(vmem_limit_bytes=small_bytes),
        cost_estimate=cost(1e6, 2e6),
        name="latent",
    )((position // bit % 2).reshape(1), near, got1, got2, token)
    got = swapped(send, "head", bit)
    ties = [send] + [halving.got for halving in halvings]
    grad_queries, _ = query_gradient(1, grad_queries, ties)
    for halving in halvings:
        while halving.order:
            halving.step()
    while bit > 1:
        total = hold + got.astype(jnp.float32)
        bit //= 2
        part //= 2
        mine = (position // bit) % 2
        send = lax.dynamic_slice_in_dim(total, (1 - mine) * part, part, 1).astype(jnp.bfloat16)
        hold = lax.dynamic_slice_in_dim(total, mine * part, part, 1)
        got = swapped(send, "head", bit)
    vmem = pl.BlockSpec(memory_space=pltpu.VMEM)
    terms = sum(([halving.hold, halving.got] for halving in halvings), [])
    grad_up_value, turned_latents = pl.pallas_call(
        final_kernel,
        in_specs=[vmem] * (2 + len(terms)),
        out_shape=[
            jax.ShapeDtypeStruct((own_rows, heads * vdim), jnp.float32),
            jax.ShapeDtypeStruct((feat, part), jnp.float32),
        ],
        compiler_params=pltpu.CompilerParams(vmem_limit_bytes=small_bytes),
        cost_estimate=cost(1e6, 2e6),
        name="final",
    )(hold, got, *terms)
    return (grad_queries, turned_latents.T, grad_up_value)


def solution(mesh):
    return jax.shard_map(
        on_device,
        mesh=mesh,
        in_specs=(
            P("ctx", "head"),
            P("ctx", None),
            P(None, "head"),
            P("ctx", "head"),
            P("ctx", "head"),
            P("ctx", "head"),
            P(),
        ),
        out_specs=(P("ctx", "head"), P(("ctx", "head"), None), P("ctx", "head")),
        check_vma=False,
    )
```

```python
import functools

import jax
import jax.numpy as jnp
from jax import lax
from jax.experimental import pallas as pl
from jax.experimental.pallas import tpu as pltpu
from jax.sharding import PartitionSpec as P

softmax_scale = 192.0 ** (-0.5)
vmem_bytes = 20 * 1024 * 1024
prepare_bytes = 54 * 1024 * 1024
small_bytes = 8 * 1024 * 1024
chunks = 2
pieces = 2


def nt_dot(a, b):
    return lax.dot_general(a, b, (((1,), (1,)), ((), ())), preferred_element_type=jnp.float32)


def nn_dot(a, b):
    return lax.dot_general(a, b, (((1,), (0,)), ((), ())), preferred_element_type=jnp.float32)


def beside_heads(ref, heads, width):
    return jnp.concatenate([ref[:, h * width : (h + 1) * width] for h in heads], axis=1)


def on_diagonal(ref, heads, width):
    blocks = [ref[:, h * width : (h + 1) * width] for h in heads]
    zero = jnp.zeros_like(blocks[0])
    return jnp.concatenate(
        [
            jnp.concatenate([block if i == j else zero for j in range(len(blocks))], axis=1)
            for i, block in enumerate(blocks)
        ],
        axis=0,
    )


def pairs_of(unit, per_unit):
    heads = list(range(unit * per_unit, (unit + 1) * per_unit))
    return [heads[i : i + 2] for i in range(0, per_unit, 2)]


def wide_rows(q_ref, heads, feat, width):
    parts = []
    for head in heads:
        if head * feat % 128 == 0:
            parts.append(q_ref[:, head * feat : head * feat + width])
        else:
            end = (head + 1) * feat
            wide = q_ref[:, end - width : end]
            parts.append(jnp.concatenate([wide[:, width - feat :], wide[:, : width - feat]], axis=1))
    return jnp.concatenate(parts, axis=0)


def prepare_kernel(
    place_ref, docs_ref, lse_ref, g_ref, o_ref, w_ref, table_ref, glat_ref,
    *, units, per_unit, rows, vdim, key_rows,
):
    heads = lse_ref.shape[0]
    window = table_ref.shape[0] - 2 * heads
    span = per_unit * rows

    @pl.when(pl.program_id(0) == 0)
    def _():
        table_ref[window : window + heads, :] = lse_ref[...]
        place = place_ref[0]
        query_pos = place * key_rows + (key_rows - rows) + lax.broadcasted_iota(jnp.int32, (8, rows), 1)
        start = jnp.zeros((8, rows), jnp.int32)
        for i in range(docs_ref.shape[0]):
            entry = docs_ref[i]
            start = jnp.where(entry <= query_pos, jnp.maximum(start, entry), start)
        key_pos = (place + 1) * key_rows - window + lax.broadcasted_iota(jnp.int32, (window, rows), 0)
        allowed = (key_pos >= start[:1]) & (key_pos <= query_pos[:1])
        table_ref[:window, :] = jnp.where(allowed, 0.0, -1e30)

    deltas = []
    for unit in range(units):
        pairs = pairs_of(unit, per_unit)
        for i, pair in enumerate(pairs):
            row = unit * span + 2 * i * rows
            glat_ref[row : row + 2 * rows, :] = nt_dot(
                on_diagonal(g_ref, pair, vdim), beside_heads(w_ref, pair, vdim)
            ).astype(glat_ref.dtype)
            for head in pair:
                lanes = slice(head * vdim, (head + 1) * vdim)
                product = g_ref[:, lanes].astype(jnp.float32) * o_ref[:, lanes].astype(jnp.float32)
                deltas.append(jnp.sum(product.T, axis=0, keepdims=True))
    count = len(deltas)
    row = window + heads + pl.program_id(0) * count
    table_ref[pl.ds(pl.multiple_of(row, count), count), :] = jnp.concatenate(deltas, axis=0)


def forward_kernel(
    place_ref, *rest, units, per_unit, rows, feat, lat, vdim, base, own_rows, first, key_rows,
):
    if first:
        (lat0_ref, lat1_ref, lat2_ref, q_ref, g_ref, table_ref, p_ref, keep_ref, send_ref, ct_ref, c_ref) = rest
    else:
        (ct_ref, c_ref, q_ref, g_ref, table_ref, _, p_ref, keep_ref, send_ref) = rest
    window, width = c_ref.shape
    far = window - key_rows
    core = place_ref[0] % 2

    if first:

        @pl.when(pl.program_id(0) == 0)
        def _():
            ct_ref[:, : far - key_rows] = lat2_ref[...]
            ct_ref[:, far - key_rows : far] = lat1_ref[...]
            ct_ref[:, far:] = lat0_ref[...]
            gap = jnp.zeros((width - feat, window), ct_ref.dtype)
            c_ref[...] = jnp.concatenate([ct_ref[...], gap], axis=0).T

    bias = table_ref[:window, :]
    span = per_unit * rows
    scores = [
        nt_dot(c_ref[...], wide_rows(q_ref, sum(pairs_of(unit, per_unit), []), feat, width)) for unit in range(units)
    ]
    for unit in range(units):
        for k in range(per_unit):
            index = ((pl.program_id(0) + base) * units + unit) * per_unit + k
            shift = table_ref[pl.ds(window + index, 1), :]
            column = unit * span + k * rows
            p_ref[:, column : column + rows] = jnp.exp(
                scores[unit][:, k * rows : (k + 1) * rows] * softmax_scale + (bias - shift)
            ).astype(jnp.bfloat16)
    olats = [
        nn_dot(ct_ref[:lat, :], p_ref[:, unit * span : (unit + 1) * span]).astype(jnp.bfloat16)
        for unit in range(units)
    ]
    for unit in range(units):
        for i, pair in enumerate(pairs_of(unit, per_unit)):
            part = nn_dot(
                olats[unit][:, 2 * i * rows : 2 * (i + 1) * rows], on_diagonal(g_ref, pair, vdim)
            )
            lanes = slice(pair[0] * vdim, (pair[0] + 2) * vdim)
            part = part.reshape(lat // (2 * own_rows), 2, own_rows, 2 * vdim)
            low, high = part[:, 0], part[:, 1]
            keep_ref[:, lanes] = (
                jnp.where(core == 0, low, high).reshape(lat // 2, 2 * vdim).astype(keep_ref.dtype)
            )
            send_ref[:, lanes] = (
                jnp.where(core == 0, high, low).reshape(lat // 2, 2 * vdim).astype(send_ref.dtype)
            )


def store_turned(gq_ref, turned, first_head, count, rows, feat):
    for k in range(0, count, 2):
        both = jnp.concatenate(
            [turned[:, (k + j) * rows : (k + j + 1) * rows] for j in range(2)], axis=0
        )
        gq_ref[:, (first_head + k) * feat : (first_head + k + 2) * feat] = both.T


def backward_kernel(
    ct_ref, c_ref, q_ref, glat_ref, table_ref, p_ref, *rest,
    units, per_unit, rows, feat, lat, steps, base, first, last, ties, key_rows,
):
    rest = list(rest)
    acc_in = None if first else rest.pop(0)
    rest = rest[ties:]
    if last:
        ds_ref, near_ref, far1_ref, far2_ref, acc = rest
    else:
        gq_ref, acc_out, acc, ds_ref = rest
    span = per_unit * rows
    width = c_ref.shape[1]

    @pl.when(pl.program_id(0) == 0)
    def _():
        acc[...] = jnp.zeros_like(acc) if first else acc_in[...]

    first_delta = (table_ref.shape[0] + c_ref.shape[0]) // 2
    gprobs = [
        nt_dot(c_ref[:, :lat], glat_ref[unit * span : (unit + 1) * span, :]) for unit in range(units)
    ]
    for unit in range(units):
        for k in range(per_unit):
            index = ((pl.program_id(0) + base) * units + unit) * per_unit + k
            delta = table_ref[pl.ds(first_delta + index, 1), :]
            own = slice(unit * span + k * rows, unit * span + (k + 1) * rows)
            ds_ref[:, own] = (
                p_ref[:, own].astype(jnp.float32)
                * ((gprobs[unit][:, k * rows : (k + 1) * rows] - delta) * softmax_scale)
            ).astype(jnp.bfloat16)
    query = wide_rows(q_ref, list(range(units * per_unit)), feat, width)
    acc[:, :lat] += nn_dot(
        jnp.concatenate([ds_ref[...], p_ref[...]], axis=1),
        jnp.concatenate([query[:, :lat], glat_ref[...]], axis=0),
    )
    acc[:, lat:] += nn_dot(ds_ref[...], query[:, lat:])
    if not last:
        for unit in range(units):
            turned = nn_dot(ct_ref[...], ds_ref[:, unit * span : (unit + 1) * span]).astype(jnp.bfloat16)
            store_turned(gq_ref, turned, unit * per_unit, per_unit, rows, feat)

    @pl.when(pl.program_id(0) == steps - 1)
    def _():
        if last:
            far2 = far2_ref.shape[1]
            total = acc[...].T[:feat]
            far2_ref[...] = total[:, :far2].astype(far2_ref.dtype)
            far1_ref[...] = total[:, far2 : far2 + key_rows].astype(far1_ref.dtype)
            near_ref[...] = total[:, far2 + key_rows :]
        else:
            acc_out[...] = acc[...]


def query_kernel(ct_ref, ds_ref, *rest, count, rows, feat):
    gq_ref, token_ref = rest[-2:]
    token_ref[...] = jnp.zeros_like(token_ref)
    store_turned(gq_ref, nn_dot(ct_ref[...], ds_ref[...]).astype(jnp.bfloat16), 0, count, rows, feat)


def passed_along(value, axis, steps):
    count = lax.axis_size(axis)
    first, last = (max(0, -steps), min(count, count - steps))
    return lax.ppermute(value, axis, [(source, source + steps) for source in range(first, last)])


def swapped(value, axis, bit):
    count = lax.axis_size(axis)
    return lax.ppermute(value, axis, [(source, source ^ bit) for source in range(count)])


def params(limit=vmem_bytes):
    return pltpu.CompilerParams(dimension_semantics=("arbitrary",), vmem_limit_bytes=limit)


def cost(flops, moved):
    return pl.CostEstimate(flops=int(flops), bytes_accessed=int(moved), transcendentals=0)


def bit_of(place, bit):
    return (place >> bit) & 1


def halving_kernel(place_ref, hold_ref, got_ref, send_ref, keep_ref, *, dim, bit):
    mine = bit_of(place_ref[0], bit)
    lead = (slice(None),) * dim
    for which, out_ref in ((1 - mine, send_ref), (mine, keep_ref)):
        where = lead + (which,)
        out_ref[...] = (hold_ref[where].astype(jnp.float32) + got_ref[where].astype(jnp.float32)).astype(
            out_ref.dtype
        )


def final_kernel(hold_ref, got_ref, *refs):
    out_ref, lat_ref = refs[-2:]
    lat_ref[...] = hold_ref[...] + got_ref[...].astype(jnp.float32)
    cols = refs[0].shape[-1]
    for i in range(len(refs) // 2 - 1):
        out_ref[:, i * cols : (i + 1) * cols] = refs[2 * i][...] + refs[2 * i + 1][...].astype(jnp.float32)


def latent_kernel(side_ref, near_ref, got1_ref, got2_ref, _, send_ref, hold_ref):
    low = near_ref[...] + got1_ref[...].astype(jnp.float32)
    part = send_ref.shape[1]
    spare = near_ref.shape[1] - got2_ref.shape[1]
    whole = jnp.concatenate([low[:, :spare], low[:, spare:] + got2_ref[...].astype(jnp.float32)], axis=1)
    first, second = whole[:, :part], whole[:, part:]
    lower = side_ref[0] == 0
    send_ref[...] = jnp.where(lower, second, first).astype(send_ref.dtype)
    hold_ref[...] = jnp.where(lower, first, second)


class Halving:
    def __init__(self, hold, got, bits, place, axis):
        self.hold, self.got, self.place, self.axis = hold, got, place, axis
        self.opened, self.order = sorted(bits, reverse=True), list(bits)

    def step(self):
        bit = self.order.pop(0)
        shape = (2,) * (len(self.opened) - 1) + self.hold.shape[-2:]
        vmem = pl.BlockSpec(memory_space=pltpu.VMEM)
        sent, self.hold = pl.pallas_call(
            functools.partial(halving_kernel, dim=self.opened.index(bit), bit=bit),
            in_specs=[pl.BlockSpec(memory_space=pltpu.SMEM), vmem, vmem],
            out_shape=[jax.ShapeDtypeStruct(shape, jnp.bfloat16), jax.ShapeDtypeStruct(shape, jnp.float32)],
            compiler_params=pltpu.CompilerParams(vmem_limit_bytes=small_bytes),
            cost_estimate=cost(1e6, 2e6),
            name="halving",
        )(self.place, self.hold, self.got)
        self.opened.remove(bit)
        self.got = swapped(sent.reshape((-1, shape[-1])), self.axis, 1 << bit).reshape(shape)
        return sent


def on_device(queries, latents, up_value, grad_out, out_saved, log_sums, doc_starts):
    rows = queries.shape[0]
    key_rows, feat = latents.shape
    lat = up_value.shape[0]
    heads = log_sums.shape[1]
    vdim = grad_out.shape[1] // heads
    ctx = lax.axis_size("ctx")
    own_rows = lat // ctx
    window = 2 * key_rows + rows
    far = window - key_rows
    width = -(-feat // 128) * 128
    unit = max(2, min(4, heads // pieces))

    place = lax.axis_index("ctx").astype(jnp.int32)
    turned = latents.T
    prev1 = passed_along(turned, "ctx", 1)
    prev2 = passed_along(turned, "ctx", 2)
    sums_turned = log_sums.T

    def whole(*shape):
        return pl.BlockSpec(shape, lambda i: (0,) * len(shape))

    smem = pl.BlockSpec(memory_space=pltpu.SMEM)
    untouched = pl.BlockSpec(memory_space=pl.ANY)
    scalar = place.reshape(1)

    chunk_heads = heads // chunks
    units = max(1, min(2, heads // unit))
    group = units * unit
    lanes = lambda i: (0, i)
    rowed = lambda i: (i, 0)
    table, glat = pl.pallas_call(
        functools.partial(
            prepare_kernel, units=units, per_unit=unit, rows=rows, vdim=vdim, key_rows=key_rows
        ),
        grid=(heads // group,),
        in_specs=[
            smem,
            smem,
            whole(heads, rows),
            pl.BlockSpec((rows, group * vdim), lanes),
            pl.BlockSpec((rows, group * vdim), lanes),
            pl.BlockSpec((lat, group * vdim), lanes),
        ],
        out_specs=[
            whole(window + 2 * heads, rows),
            pl.BlockSpec((group * rows, lat), rowed),
        ],
        out_shape=[
            jax.ShapeDtypeStruct((window + 2 * heads, rows), jnp.float32),
            jax.ShapeDtypeStruct((heads * rows, lat), jnp.bfloat16),
        ],
        compiler_params=params(prepare_bytes),
        cost_estimate=cost(heads * rows * 4 * lat * vdim, 20e6),
        name="prepare",
    )(scalar, doc_starts, sums_turned, grad_out, out_saved, up_value)

    probs = None
    partials = []
    units = max(1, min(2, chunk_heads // unit))
    group = units * unit
    steps = chunk_heads // group
    for chunk in range(chunks):
        base = chunk * steps
        lanes = lambda i, base=base: (0, i + base)
        rowed = lambda i, base=base: (i + base, 0)
        first = chunk == 0
        in_specs = [smem]
        operands = [scalar]
        if first:
            last_part = key_rows // (far - key_rows) - 1
            in_specs += [whole(feat, key_rows)] * 2
            in_specs.append(pl.BlockSpec((feat, far - key_rows), lambda i: (0, last_part)))
            operands += [turned, prev1, prev2]
        else:
            in_specs += [whole(feat, window), whole(window, width)]
            operands += [keys_turned, keys]
        in_specs += [
            pl.BlockSpec((rows, group * feat), lanes),
            pl.BlockSpec((rows, group * vdim), lanes),
            whole(window + 2 * heads, rows),
        ]
        operands += [queries, grad_out, table]
        halves = [pl.BlockSpec((lat // 2, group * vdim), lambda i: (0, i))] * 2
        out_specs = [pl.BlockSpec((window, group * rows), lanes)] + halves
        out_shape = [jax.ShapeDtypeStruct((window, heads * rows), jnp.bfloat16)]
        out_shape += [jax.ShapeDtypeStruct((lat // 2, chunk_heads * vdim), jnp.bfloat16)] * 2
        aliases = {}
        if first:
            out_specs += [whole(feat, window), whole(window, width)]
            out_shape += [
                jax.ShapeDtypeStruct((feat, window), jnp.bfloat16),
                jax.ShapeDtypeStruct((window, width), jnp.bfloat16),
            ]
        else:
            aliases = {len(operands): 0}
            in_specs.append(untouched)
            operands.append(probs)
        out = pl.pallas_call(
            functools.partial(
                forward_kernel, units=units, per_unit=unit, rows=rows, feat=feat, lat=lat, vdim=vdim,
                base=base, own_rows=own_rows, first=first, key_rows=key_rows,
            ),
            grid=(steps,),
            in_specs=in_specs,
            out_specs=out_specs,
            out_shape=out_shape,
            input_output_aliases=aliases,
            compiler_params=params(),
            cost_estimate=cost(chunk_heads * rows * 2 * window * (width + lat) * 2, 1e6),
            name="forward",
        )(*operands)
        if first:
            keys_turned, keys = out[3:]
        probs, keep, send = out[:3]
        partials.append((keep, send))

    upper = list(range(1, ctx.bit_length() - 1))
    shape = (2,) * len(upper) + (own_rows, chunk_heads * vdim)
    halvings = []
    for (keep, send), order in zip(partials, (upper[1:] + upper[:1], upper)):
        got = swapped(send, "ctx", 1)
        halvings.append(Halving(keep.reshape(shape), got.reshape(shape), order, scalar, "ctx"))

    piece_heads = heads // pieces
    units = max(1, min(2, piece_heads // unit))
    group = units * unit
    steps = piece_heads // group
    acc = None
    for piece in range(pieces):
        ties = [halving.step() for halving in halvings if halving.order]
        first, last = piece == 0, piece == pieces - 1
        base = piece * steps
        lanes = lambda i, base=base: (0, i + base)
        rowed = lambda i, base=base: (i + base, 0)
        in_specs = [
            whole(feat, window),
            whole(window, width),
            pl.BlockSpec((rows, group * feat), lanes),
            pl.BlockSpec((group * rows, lat), rowed),
            whole(window + 2 * heads, rows),
            pl.BlockSpec((window, group * rows), lanes),
        ]
        operands = [keys_turned, keys, queries, glat, table, probs]
        if not first:
            in_specs.append(whole(window, width))
            operands.append(acc)
        in_specs += [untouched] * len(ties)
        operands += ties
        scratch = [pltpu.VMEM((window, width), jnp.float32)]
        if last:
            out_specs = [pl.BlockSpec((window, group * rows), lambda i: (0, i))]
            out_shape = [jax.ShapeDtypeStruct((window, piece_heads * rows), jnp.bfloat16)]
            out_specs += [whole(feat, key_rows), whole(feat, key_rows), whole(feat, far - key_rows)]
            out_shape += [
                jax.ShapeDtypeStruct((feat, key_rows), jnp.float32),
                jax.ShapeDtypeStruct((feat, key_rows), jnp.bfloat16),
                jax.ShapeDtypeStruct((feat, far - key_rows), jnp.bfloat16),
            ]
        else:
            out_specs = [pl.BlockSpec((rows, group * feat), lanes), whole(window, width)]
            out_shape = [
                jax.ShapeDtypeStruct(queries.shape, jnp.bfloat16),
                jax.ShapeDtypeStruct((window, width), jnp.float32),
            ]
            scratch.append(pltpu.VMEM((window, group * rows), jnp.bfloat16))
        out = pl.pallas_call(
            functools.partial(
                backward_kernel, units=units, per_unit=unit, rows=rows, feat=feat, lat=lat, base=base,
                steps=steps, first=first, last=last, ties=len(ties), key_rows=key_rows,
            ),
            grid=(steps,),
            in_specs=in_specs,
            out_specs=out_specs,
            out_shape=out_shape,
            scratch_shapes=scratch,
            compiler_params=params(),
            cost_estimate=cost(piece_heads * rows * 2 * window * (width + 2 * lat) * 2, 1e6),
            name="backward",
        )(*operands)
        if last:
            dscores, near, far1, far2 = out
        else:
            grad_queries, acc = out

    late_heads = piece_heads // 2
    late_group = min(4, late_heads)
    late_steps = late_heads // late_group

    def query_gradient(call, so_far, ties):
        out_base = (heads - piece_heads + call * late_heads) // late_group
        return pl.pallas_call(
            functools.partial(query_kernel, count=late_group, rows=rows, feat=feat),
            grid=(late_steps,),
            in_specs=[
                whole(feat, window),
                pl.BlockSpec((window, late_group * rows), lambda i: (0, call * late_steps + i)),
            ]
            + [untouched] * (1 + len(ties)),
            out_specs=[
                pl.BlockSpec((rows, late_group * feat), lambda i: (0, out_base + i)),
                whole(8, 128),
            ],
            out_shape=[
                jax.ShapeDtypeStruct(queries.shape, jnp.bfloat16),
                jax.ShapeDtypeStruct((8, 128), jnp.float32),
            ],
            input_output_aliases={2: 0},
            compiler_params=params(),
            cost_estimate=cost(late_heads * rows * 2 * window * width * 3, 1e6),
            name="query_gradient",
        )(keys_turned, dscores, so_far, *ties)

    got1 = passed_along(far1, "ctx", -1)
    got2 = passed_along(far2, "ctx", -2)
    ties = [halving.step() for halving in halvings if halving.order]
    grad_queries, token = query_gradient(0, grad_queries, ties)
    position = lax.axis_index("head").astype(jnp.int32)
    bit = lax.axis_size("head") // 2
    part = key_rows // 2
    send, hold = pl.pallas_call(
        latent_kernel,
        in_specs=[smem] + [pl.BlockSpec(memory_space=pltpu.VMEM)] * 3 + [untouched],
        out_shape=[
            jax.ShapeDtypeStruct((feat, part), jnp.bfloat16),
            jax.ShapeDtypeStruct((feat, part), jnp.float32),
        ],
        compiler_params=pltpu.CompilerParams(vmem_limit_bytes=small_bytes),
        cost_estimate=cost(1e6, 2e6),
        name="latent",
    )((position // bit % 2).reshape(1), near, got1, got2, token)
    got = swapped(send, "head", bit)
    ties = [send] + [halving.got for halving in halvings]
    grad_queries, _ = query_gradient(1, grad_queries, ties)
    for halving in halvings:
        while halving.order:
            halving.step()
    while bit > 1:
        total = hold + got.astype(jnp.float32)
        bit //= 2
        part //= 2
        mine = (position // bit) % 2
        send = lax.dynamic_slice_in_dim(total, (1 - mine) * part, part, 1).astype(jnp.bfloat16)
        hold = lax.dynamic_slice_in_dim(total, mine * part, part, 1)
        got = swapped(send, "head", bit)
    vmem = pl.BlockSpec(memory_space=pltpu.VMEM)
    terms = sum(([halving.hold, halving.got] for halving in halvings), [])
    grad_up_value, turned_latents = pl.pallas_call(
        final_kernel,
        in_specs=[vmem] * (2 + len(terms)),
        out_shape=[
            jax.ShapeDtypeStruct((own_rows, heads * vdim), jnp.float32),
            jax.ShapeDtypeStruct((feat, part), jnp.float32),
        ],
        compiler_params=pltpu.CompilerParams(vmem_limit_bytes=small_bytes),
        cost_estimate=cost(1e6, 2e6),
        name="final",
    )(hold, got, *terms)
    return (grad_queries, turned_latents.T, grad_up_value)


def solution(mesh):
    return jax.shard_map(
        on_device,
        mesh=mesh,
        in_specs=(
            P("ctx", "head"),
            P("ctx", None),
            P(None, "head"),
            P("ctx", "head"),
            P("ctx", "head"),
            P("ctx", "head"),
            P(),
        ),
        out_specs=(P("ctx", "head"), P(("ctx", "head"), None), P("ctx", "head")),
        check_vma=False,
    )
```
